32 devices in a mesh: dp: 8 (over z, x), seq: 4 (over y, core).
Axes of the slice: x: 2, y: 2, z: 4, core: 2. Of those that a mesh axis runs over, the one named last changes fastest.
Arguments:
- molecules: bfloat16 [64, 512, 768], P('dp', 'seq'), may hold values from -6 to 6
- lengths: int32 [64], P('dp'), may hold values from 200 to 2048, as said below
- norm1_gain: float32 [768], replicated, may hold values from 0.5 to 1.5
- norm1_bias: float32 [768], replicated, may hold values from -1.2 to 1.2
- qkv_weight: bfloat16 [768, 2304], replicated, may hold values from -0.21875 to 0.21875
- query_bias: float32 [768], replicated, may hold values from -1.2 to 1.2
- value_bias: float32 [768], replicated, may hold values from -1.2 to 1.2
- out_weight: bfloat16 [768, 768], replicated, may hold values from -1.75 to 1.75
- out_bias: float32 [768], replicated, may hold values from -1.2 to 1.2
- norm2_gain: float32 [768], replicated, may hold values from 0.5 to 1.5
- norm2_bias: float32 [768], replicated, may hold values from -1.2 to 1.2
- up_weight: bfloat16 [768, 3072], replicated, may hold values from -0.21875 to 0.21875
- up_bias: float32 [3072], replicated, may hold values from -1.2 to 1.2
- down_weight: bfloat16 [3072, 768], replicated, may hold values from -0.109375 to 0.109375
- down_bias: float32 [768], replicated, may hold values from -1.2 to 1.2
- cotangent: bfloat16 [64, 512, 768], P('dp', 'seq'), may hold values from -6 to 6
Outputs:
- output: bfloat16 [64, 512, 768], P('dp', 'seq')
- molecules_grad: float32 [64, 512, 768], P('dp', 'seq')
- norm1_gain_grad: float32 [768], replicated
- norm1_bias_grad: float32 [768], replicated
- qkv_weight_grad: float32 [768, 2304], replicated
- query_bias_grad: float32 [768], replicated
- value_bias_grad: float32 [768], replicated
- out_weight_grad: float32 [768, 768], replicated
- out_bias_grad: float32 [768], replicated
- norm2_gain_grad: float32 [768], replicated
- norm2_bias_grad: float32 [768], replicated
- up_weight_grad: float32 [768, 3072], replicated
- up_bias_grad: float32 [3072], replicated
- down_weight_grad: float32 [3072, 768], replicated
- down_bias_grad: float32 [768], replicated
The draws below stay inside these ranges and needn't reach their ends.
Inputs may be any that keep to these rules, and one draw needn't show every extreme that they name: `lengths`: among the rows of each index of dp, one row drawn from the seed has all 2048 characters.
All inputs are finite; a program needn't handle non-finite values.
Results may differ from the reference program's by a relative error of at most 0.011.
Values may be sent and summed in bfloat16 or wider, within the bound.
No kernel may reach another device: no remote copies, remote signals or barrier semaphores. Data moves between devices by JAX's collectives and lax.ppermute only.
A program may use at most 256 MiB of HBM per device.

```python
import math
import jax
import jax.numpy as jnp
from jax import lax

D = 768
HEAD = 64
FF = 3072
MOLS = 512
MIN_CHARS = 200
ROWS_DEV = 8
CHARS = 2048
ROWS = 64


def draw_lengths(key, part):
    key = jax.random.fold_in(key, 7)
    first_key, second_key = jax.random.split(key)
    blocks = ROWS // ROWS_DEV
    base = jax.random.randint(first_key, (blocks, ROWS_DEV), MIN_CHARS, CHARS + 1)
    chosen = jax.random.randint(second_key, (blocks, 1), 0, ROWS_DEV)
    slots = jnp.arange(ROWS_DEV, dtype=jnp.int32)[None, :]
    return jnp.where(slots == chosen, CHARS, base).reshape(ROWS).astype(jnp.int32)


def block_scale(rng, dims, cuts, smallest, high):
    loudness, own = 1.0, jax.random.fold_in(rng, 6)
    for dim, blocks in cuts:
        draws = jnp.exp(jax.random.uniform(jax.random.fold_in(own, dim), (blocks,), jnp.float32, smallest / len(cuts), high / len(cuts)))
        loudness = loudness * jnp.repeat(draws, dims[dim] // blocks).reshape([-1 if axis == dim else 1 for axis in range(len(dims))])
    return loudness


def gaussian(key, extent, scale, bound, cuts=(), kind=jnp.bfloat16):
    entries = scale * jax.random.normal(key, extent, jnp.float32)
    if cuts:
        entries = entries * block_scale(key, extent, cuts, -0.22, 0.18)
    return jnp.clip(entries, -bound, bound).astype(kind)


def setup_inputs(seed: int = 0) -> dict:
    seeds = jax.random.split(jax.random.key(seed), 17)
    molecules = gaussian(seeds[0], (ROWS, MOLS, D), 1.0, 6.0, ((0, 8), (1, 4)))
    lengths = draw_lengths(jax.random.fold_in(seeds[16], 71), 0)
    norm1_gain = jnp.clip(1.0 + 0.1 * jax.random.normal(seeds[2], (D,), jnp.float32), 0.5, 1.5)
    norm1_bias = gaussian(seeds[3], (D,), 0.2, 1.2, (), jnp.float32)
    qkv_weight = gaussian(seeds[4], (D, 3 * D), D ** -0.5, 0.21875)
    query_bias = gaussian(seeds[5], (D,), 0.2, 1.2, (), jnp.float32)
    value_bias = gaussian(seeds[6], (D,), 0.2, 1.2, (), jnp.float32)
    out_weight = gaussian(seeds[7], (D, D), (D // 64) ** -0.5, 1.75)
    out_bias = gaussian(seeds[8], (D,), 0.2, 1.2, (), jnp.float32)
    norm2_gain = jnp.clip(1.0 + 0.1 * jax.random.normal(seeds[9], (D,), jnp.float32), 0.5, 1.5)
    norm2_bias = gaussian(seeds[10], (D,), 0.2, 1.2, (), jnp.float32)
    up_weight = gaussian(seeds[11], (D, FF), D ** -0.5, 0.21875)
    up_bias = gaussian(seeds[12], (FF,), 0.2, 1.2, (), jnp.float32)
    down_weight = gaussian(seeds[13], (FF, D), FF ** -0.5, 0.109375)
    down_bias = gaussian(seeds[14], (D,), 0.2, 1.2, (), jnp.float32)
    cotangent = gaussian(seeds[15], (ROWS, MOLS, D), 1.0, 6.0, ((0, 8), (1, 4)))
    return dict(molecules=molecules, lengths=lengths, norm1_gain=norm1_gain, norm1_bias=norm1_bias, qkv_weight=qkv_weight, query_bias=query_bias, value_bias=value_bias, out_weight=out_weight, out_bias=out_bias, norm2_gain=norm2_gain, norm2_bias=norm2_bias, up_weight=up_weight, up_bias=up_bias, down_weight=down_weight, down_bias=down_bias, cotangent=cotangent)


epsilon = 1e-12

@jax.custom_vjp
def low(v):
    return lax.optimization_barrier(v.astype(jnp.bfloat16)).astype(jnp.float32)

@jax.custom_vjp
def low_back(v):
    return v

def low_keep(v):
    return (low(v), None)

def low_pass(kept, grad):
    return (grad,)

def back_keep(v):
    return (v, None)

def back_low(kept, grad):
    return (low(grad),)
low.defvjp(low_keep, low_pass)
low_back.defvjp(back_keep, back_low)

def layer_norm(values, gain, shift):
    center = values - lax.optimization_barrier(jnp.mean(values, axis=-1, keepdims=True))
    spread = lax.optimization_barrier(jnp.mean(center * center, axis=-1, keepdims=True))
    return center * lax.rsqrt(spread + epsilon) * gain + shift

def matmul(left, right):
    return jnp.dot(left, right, precision=lax.Precision.HIGHEST)

def block_forward(inputs, keys_ok, rows_ok, weights):
    norm1_gain, norm1_bias, qkv_weight, query_bias, value_bias, out_weight, out_bias, norm2_gain, norm2_bias, up_weight, up_bias, down_weight, down_bias = weights
    batch_rows, length, width = inputs.shape
    heads = width // HEAD
    score_scale = 1.0 / math.sqrt(HEAD)
    normed = low(layer_norm(inputs, norm1_gain, norm1_bias))
    shift_qkv = jnp.concatenate([query_bias, jnp.zeros_like(query_bias), value_bias])
    projected = low_back(low(matmul(normed, qkv_weight) + shift_qkv))
    projected = projected.reshape(batch_rows, length, 3, heads, HEAD)
    queries = projected[:, :, 0]
    keys_here = projected[:, :, 1]
    values_here = projected[:, :, 2]
    scores = jnp.einsum('blhd,bmhd->bhlm', queries, keys_here, precision=lax.Precision.HIGHEST)
    scores = low_back(scores * score_scale)
    scores = jnp.where(keys_ok[:, None, None, :], scores, -1e+30)
    top = lax.optimization_barrier(jnp.max(scores, axis=-1, keepdims=True))
    expo = jnp.exp(scores - top)
    attn_probs = low(expo / lax.optimization_barrier(jnp.sum(expo, axis=-1, keepdims=True)))
    context = jnp.einsum('bhlm,bmhd->blhd', attn_probs, values_here, precision=lax.Precision.HIGHEST)
    context = low_back(low(context)).reshape(batch_rows, length, width)
    middle = inputs + low_back(matmul(context, out_weight) + out_bias)
    normed_two = low(layer_norm(middle, norm2_gain, norm2_bias))
    hidden = low_back(matmul(normed_two, up_weight) + up_bias)
    active = low(jax.nn.gelu(hidden, approximate=False))
    result = middle + low_back(matmul(active, down_weight) + down_bias)
    return result * rows_ok[:, :, None]

def reference(molecules, lengths, norm1_gain, norm1_bias, qkv_weight, query_bias, value_bias, out_weight, out_bias, norm2_gain, norm2_bias, up_weight, up_bias, down_weight, down_bias, cotangent):
    weights = (norm1_gain, norm1_bias, qkv_weight.astype(jnp.float32), query_bias, value_bias, out_weight.astype(jnp.float32), out_bias, norm2_gain, norm2_bias, up_weight.astype(jnp.float32), up_bias, down_weight.astype(jnp.float32), down_bias)
    mol_len = (lengths + 3) // 4
    positions = jnp.arange(MOLS, dtype=jnp.int32)
    key_valid = positions[None, :] < mol_len[:, None]
    row_valid = key_valid.astype(jnp.float32)
    groups = ROWS // ROWS_DEV
    stacked = (molecules.astype(jnp.float32).reshape(groups, ROWS_DEV, MOLS, D), key_valid.reshape(groups, ROWS_DEV, MOLS), row_valid.reshape(groups, ROWS_DEV, MOLS), cotangent.astype(jnp.float32).reshape(groups, ROWS_DEV, MOLS, D))

    def one_group(totals, group):
        inputs, keys_ok, rows_ok, grad_out = group

        def forward(values, *params):
            return block_forward(values, keys_ok, rows_ok, params)
        result, pullback = jax.vjp(forward, inputs, *weights)
        grads = pullback(grad_out)
        totals = tuple((total + piece for total, piece in zip(totals, grads[1:])))
        return (totals, (result.astype(jnp.bfloat16), grads[0]))
    start_totals = tuple((jnp.zeros_like(weight) for weight in weights))
    totals, (results, input_grads) = lax.scan(one_group, start_totals, stacked)
    output = results.reshape(ROWS, MOLS, D)
    molecules_grad = input_grads.reshape(ROWS, MOLS, D)
    grad_norm1_gain, grad_norm1_bias, grad_qkv_weight, grad_query_bias, grad_value_bias, grad_out_weight, grad_out_bias, grad_norm2_gain, grad_norm2_bias, grad_up_weight, grad_up_bias, grad_down_weight, grad_down_bias = totals
    return (output, molecules_grad, grad_norm1_gain, grad_norm1_bias, grad_qkv_weight, grad_query_bias, grad_value_bias, grad_out_weight, grad_out_bias, grad_norm2_gain, grad_norm2_bias, grad_up_weight, grad_up_bias, grad_down_weight, grad_down_bias)
```

```python
import math

import jax
import jax.numpy as jnp
from jax import lax
from jax.experimental import pallas as pl
from jax.experimental.pallas import tpu as pltpu
from jax.sharding import PartitionSpec as P

HEAD = 64
PAIR = 2 * HEAD
BLK = 128
TILE = 256
FCHUNK = 512
PARTS = 2
LOG2E = 1.4426950408889634
SCALE = 1.0 / math.sqrt(HEAD)
NEG = -1e30
EPS = 1e-12
F32 = jnp.float32
BF16 = jnp.bfloat16
VMEM_LIMIT = 60 * 1024 * 1024

SMEM_SPEC = pl.BlockSpec(memory_space=pltpu.SMEM)
VMEM_SPEC = pl.BlockSpec(memory_space=pltpu.VMEM)
ANY_SPEC = pl.BlockSpec(memory_space=pl.ANY)


def cost(flops, exps, moved):
    return pl.CostEstimate(flops=int(flops), transcendentals=int(exps), bytes_accessed=int(moved))


def params():
    return pltpu.CompilerParams(vmem_limit_bytes=VMEM_LIMIT)


def nn(a, b):
    return lax.dot_general(a, b, (((1,), (0,)), ((), ())), preferred_element_type=F32)


def nt(a, b):
    return lax.dot_general(a, b, (((1,), (1,)), ((), ())), preferred_element_type=F32)


def tn(a, b):
    return lax.dot_general(a, b, (((0,), (0,)), ((), ())), preferred_element_type=F32)


def ranks_of(len_ref, rows):
    lens = [len_ref[r] for r in range(rows)]
    ranks = []
    for r in range(rows):
        rank = jnp.int32(0)
        for other in range(rows):
            if other < r:
                rank += (lens[other] >= lens[r]).astype(jnp.int32)
            elif other > r:
                rank += (lens[other] > lens[r]).astype(jnp.int32)
        ranks.append(rank)
    return lens, ranks


def rank_at(slot, group, groups):
    return slot * groups + (group if slot % 2 == 0 else groups - 1 - group)


def pick(values, ranks, wanted):
    found = jnp.int32(0)
    for value, rank in zip(values, ranks):
        found += jnp.where(rank == wanted, value, 0)
    return found


def my_counts(len_ref, rows, groups):
    me = lax.axis_index("seq")
    lens, ranks = ranks_of(len_ref, rows)
    return [
        (pick(lens, ranks, rank_at(slot, me, groups)) + 3) // 4
        for slot in range(rows // groups)
    ]


def blocks_of(count):
    return (count + BLK - 1) // BLK


def piece_rows(len_ref, rows, groups):
    me = lax.axis_index("seq")
    _, ranks = ranks_of(len_ref, rows)
    indices = [jnp.int32(r) for r in range(rows)]
    return {
        (slot, k): pick(indices, ranks, rank_at(slot, me ^ k, groups))
        for slot in range(rows // groups)
        for k in range(groups)
    }


def deal_kernel(rows, groups, len_ref, src, *dsts):
    for (slot, k), row in piece_rows(len_ref, rows, groups).items():
        dsts[k][slot] = src[row]


def deal(lengths, values, groups):
    rows, span, width = values.shape
    return pl.pallas_call(
        lambda *refs: deal_kernel(rows, groups, *refs),
        out_shape=[jax.ShapeDtypeStruct((rows // groups, span, width), values.dtype)] * groups,
        in_specs=[SMEM_SPEC, VMEM_SPEC],
        out_specs=[VMEM_SPEC] * groups,
        compiler_params=params(),
        cost_estimate=cost(0, 0, 3e6),
        name="deal_rows",
    )(lengths, values)


def undeal_kernel(rows, groups, len_ref, *rest):
    srcs, dst = rest[:groups], rest[groups]
    for (slot, k), row in piece_rows(len_ref, rows, groups).items():
        dst[row] = srcs[k][slot].astype(dst.dtype)


def undeal(lengths, pieces, kind):
    slots, span, width = pieces[0].shape
    groups = len(pieces)
    rows = groups * slots
    return pl.pallas_call(
        lambda *refs: undeal_kernel(rows, groups, *refs),
        out_shape=jax.ShapeDtypeStruct((rows, span, width), kind),
        in_specs=[SMEM_SPEC] + [VMEM_SPEC] * groups,
        out_specs=VMEM_SPEC,
        compiler_params=params(),
        cost_estimate=cost(0, 0, 4e6),
        name="undeal_rows",
    )(lengths, *pieces)


def swap(pieces):
    groups = len(pieces)
    return [pieces[0]] + [
        lax.ppermute(pieces[k], "seq", [(i, i ^ k) for i in range(groups)])
        for k in range(1, groups)
    ]


class Route:
    def __init__(self, x_first):
        seq, dp = lax.axis_index("seq"), lax.axis_index("dp")
        pair, y, x = seq & 1, (seq >> 1) & 1, dp & 1
        self.first = ("dp", 1) if x_first else ("seq", 2)
        self.second = ("seq", 2) if x_first else ("dp", 1)
        self.mine = pair * 4 + (x * 2 + y if x_first else y * 2 + x)


def cross(values, way):
    axis, mask = way
    size = lax.axis_size(axis)
    return lax.ppermute(values, axis, [(i, i ^ mask) for i in range(size)])


PAIR_WAY = ("seq", 1)


def fold(keep, recv):
    return (keep.astype(F32) + recv.astype(F32)).astype(keep.dtype)


def fold_halves(keep, recv):
    rows = keep.shape[0] // 2
    high = fold(keep[rows:], recv[rows:])
    return fold(keep[:rows], recv[:rows]), high


def far_ways():
    size, mask, ways = lax.axis_size("dp"), 2, []
    while mask < size:
        ways.append(("dp", mask))
        mask *= 2
    return ways


class Order:
    def __init__(self):
        self.last = None

    def __call__(self, step, *values):
        if self.last is not None:
            values, _ = lax.optimization_barrier((values, self.last))
        out = step(*values)
        self.last = out
        return out


class Sum:
    def __init__(self, order, keep, send, route):
        self.order, self.route, self.low = order, route, keep
        self.arriving = cross(send, PAIR_WAY)
        self.ways = [route.first, route.second]
        self.far = far_ways()

    def halve(self):
        self.low, high = self.order(fold_halves, self.low, self.arriving)
        self.arriving = cross(high, self.ways.pop(0))

    def settle(self):
        self.low = self.order(fold, self.low, self.arriving)

    def send_far(self):
        self.arriving = cross(self.low, self.far.pop(0))

    def fold_far(self):
        self.low = self.order(fold, self.low, self.arriving)

    def gather_second(self):
        self.one = cross(self.low, self.route.second)

    def gather_first(self):
        self.pair = self.order(lambda a, b: jnp.concatenate([a, b], axis=0), self.low, self.one)
        self.two = cross(self.pair, self.route.first)

    def gather_pair(self):
        near = [self.low, self.one, self.two]
        self.parts = near + [cross(part, PAIR_WAY) for part in near]


def reduce_far_together(values):
    size = lax.axis_size("dp")
    lines = [[i for i in range(size) if i % 2 == parity] for parity in range(2)]
    return lax.psum(values, "dp", axis_index_groups=lines)


def eighth(parts, rel):
    which = (rel % 4).bit_length()
    return parts[which + 3 * (rel // 4)], rel % 4 - (1 << which >> 1)


def spread_kernel(x_first, place, parts, out, stage, sems):
    mine = Route(x_first).mine
    rows = parts[0].shape[0]
    copies = []
    for rel in range(8):
        part, index = eighth(parts, rel)
        got = part[index * rows : (index + 1) * rows]
        moves = place(out, rel ^ mine, got, stage.at[rel])
        for i, (src, dst) in enumerate(moves):
            copy = pltpu.make_async_copy(src, dst, sems.at[rel, i])
            copy.start()
            copies.append(copy)
    for copy in copies:
        copy.wait()


def spread(parts, x_first, shapes, stage, place, before=()):
    before = [array for array in before]
    count = len(shapes)

    def kernel(*refs):
        outs = refs[6 + len(before) : 6 + len(before) + count]
        spread_kernel(x_first, place, refs[:6], outs, *refs[6 + len(before) + count :])

    return pl.pallas_call(
        kernel,
        out_shape=[jax.ShapeDtypeStruct(shape, F32) for shape in shapes],
        in_specs=[VMEM_SPEC] * 6 + [ANY_SPEC] * len(before),
        out_specs=[ANY_SPEC] * count,
        scratch_shapes=[pltpu.VMEM((8,) + stage, F32), pltpu.SemaphoreType.DMA((8, 6))],
        input_output_aliases={6 + i: i for i in range(len(before))},
        compiler_params=params(),
        cost_estimate=cost(0, 0, 3e6),
        name="spread",
    )(*parts, *before)


def norm_stats(values):
    center = values - jnp.mean(values, axis=-1, keepdims=True)
    rstd = lax.rsqrt(jnp.mean(center * center, axis=-1, keepdims=True) + EPS)
    return center * rstd, rstd


def norm_back(grad, hat, rstd, gain):
    scaled = grad * gain
    mean_scaled = jnp.mean(scaled, axis=-1, keepdims=True)
    mean_dot = jnp.mean(scaled * hat, axis=-1, keepdims=True)
    return rstd * (scaled - mean_scaled - hat * mean_dot)


def first_head(rows):
    return lax.broadcasted_iota(jnp.int32, (rows, PAIR), 1) < HEAD


def keep_head(values, low, head):
    zero = jnp.zeros_like(values)
    return jnp.where(low, values, zero) if head == 0 else jnp.where(low, zero, values)


def masked_scores(keys, queries, count, extent):
    scores = nt(keys, queries) * (SCALE * LOG2E)
    tail = scores[extent - BLK :]
    position = lax.broadcasted_iota(jnp.int32, tail.shape, 0) + (extent - BLK)
    tail = jnp.where(position < count, tail, NEG)
    if extent == BLK:
        return tail
    return jnp.concatenate([scores[: extent - BLK], tail], axis=0)


def attend_kernel(rows, groups, slot, len_ref, *refs):
    refs = list(refs)
    take = lambda n: [refs.pop(0) for _ in range(n)]
    pieces = take(groups)
    gain_ref, bias_ref, w_ref, shift_ref, wo_ref, bo_ref, g2_ref, b2_ref = take(8)
    if slot:
        take(7)
    x_ref, normed_ref, qkv_ref, ctx_ref, lse_ref, mid_ref, n2_ref = [ref.at[0] for ref in refs]
    count = my_counts(len_ref, rows, groups)[slot]
    whole, width = x_ref.shape
    span = whole // groups
    me = lax.axis_index("seq")
    for k in range(groups):
        x_ref[pl.ds(pl.multiple_of((me ^ k) * span, span), span)] = pieces[k][0]

    def body(extent):
        hat, _ = norm_stats(x_ref[:extent].astype(F32))
        normed = (hat * gain_ref[...] + bias_ref[...]).astype(BF16)
        normed_ref[:extent] = normed
        for part in range(3):
            cols = slice(part * width, (part + 1) * width)
            qkv_ref[:extent, cols] = (nn(normed, w_ref[:, cols]) + shift_ref[:, cols]).astype(BF16)
        low = first_head(extent)

        def pair(index, carry):
            start = pl.multiple_of(index * PAIR, PAIR)
            queries = qkv_ref[:extent, pl.ds(start, PAIR)]
            keys = qkv_ref[:extent, pl.ds(width + start, PAIR)]
            values = qkv_ref[:extent, pl.ds(2 * width + start, PAIR)]
            values_t = values.T
            outs = []
            for head in range(2):
                scores = masked_scores(keep_head(keys, low, head), queries, count, extent)
                top = jnp.max(scores, axis=0, keepdims=True)
                expo = jnp.exp2(scores - top)
                total = jnp.sum(expo, axis=0, keepdims=True)
                out = nn(values_t[head * HEAD : (head + 1) * HEAD], expo.astype(BF16))
                outs.append(out * (1.0 / total))
                lse_ref[index, head : head + 1, :extent] = top + jnp.log2(total)
            ctx_ref[:extent, pl.ds(start, PAIR)] = jnp.concatenate(outs, axis=0).T.astype(BF16)
            return carry

        lax.fori_loop(0, width // PAIR, pair, 0)
        middle = x_ref[:extent].astype(F32) + nn(ctx_ref[:extent], wo_ref[...]) + bo_ref[...]
        mid_ref[:extent] = middle
        hat, _ = norm_stats(middle)
        n2_ref[:extent] = (hat * g2_ref[...] + b2_ref[...]).astype(BF16)
        upto = (extent + TILE - 1) // TILE * TILE
        for ref in (normed_ref, ctx_ref, mid_ref, n2_ref):
            if upto > extent:
                ref[extent:upto] = jnp.zeros((upto - extent, width), ref.dtype)

    blocks = blocks_of(count)
    for n in range(1, whole // BLK + 1):
        pl.when(blocks == n)(lambda n=n: body(n * BLK))


def attend(slot, lengths, pieces, gain, bias, weight, shift, wo, bo, g2, b2, before):
    groups = len(pieces)
    slots, span, width = pieces[0].shape
    rows, whole = slots * groups, span * groups
    shapes = [
        ((slots, whole, width), BF16),
        ((slots, whole, width), BF16),
        ((slots, whole, 3 * width), BF16),
        ((slots, whole, width), BF16),
        ((slots, width // PAIR, 8, whole), F32),
        ((slots, whole, width), F32),
        ((slots, whole, width), BF16),
    ]
    one = lambda shape: pl.BlockSpec((1,) + shape[1:], lambda i: (slot,) + (0,) * (len(shape) - 1))
    return pl.pallas_call(
        lambda *refs: attend_kernel(rows, groups, slot, *refs),
        grid=(1,),
        out_shape=[jax.ShapeDtypeStruct(shape, kind) for shape, kind in shapes],
        in_specs=[SMEM_SPEC] + [one((slots, span, width))] * groups + [VMEM_SPEC] * 8
        + [ANY_SPEC] * len(before),
        out_specs=[one(shape) for shape, _ in shapes],
        input_output_aliases={1 + groups + 8 + i: i for i in range(len(before))},
        compiler_params=params(),
        cost_estimate=cost(5e9, 3e6, 12e6),
        name="attend",
    )(lengths, *pieces, gain, bias, weight, shift, wo, bo, g2, b2, *before)


def tile_state(len_ref, rows, groups, whole):
    counts = my_counts(len_ref, rows, groups)
    per_slot = whole // TILE

    def left(index):
        count = counts[0]
        for slot in range(1, len(counts)):
            count = jnp.where(index // per_slot == slot, counts[slot], count)
        return count - (index % per_slot) * TILE

    def valid(index):
        return lax.broadcasted_iota(jnp.int32, (TILE, 1), 0) < left(index)

    return left, valid


def write_eighths(scratch, keep, send, mine, write):
    rows_each = scratch.shape[0] // 8
    for rel in range(8):
        at = pl.ds(pl.multiple_of((rel ^ mine) * rows_each, rows_each), rows_each)
        write((keep, send)[rel // 4], rel % 4, rows_each, scratch[at].astype(BF16))


def feed_kernel(rows, groups, part, len_ref, *refs):
    refs = list(refs)
    take = lambda n: [refs.pop(0) for _ in range(n)]
    n2_ref = take(1)[0]
    sources = take(groups if part == 0 else 1)
    up_ref, ub_ref, down_ref = take(3)
    act_ref, hg_ref, dup_keep, dup_send, ddown_keep, ddown_send, dub_ref = take(7)
    if part == 0:
        grad_ref, vec_ref = take(2)
    else:
        grad_ref = sources[0]
    dup_s, ddown_s = refs
    chunk = pl.program_id(0)
    tokens, width = n2_ref.shape
    whole = tokens // (rows // groups)
    span = whole // groups
    left, valid = tile_state(len_ref, rows, groups, whole)
    tiles = tokens // TILE
    me = lax.axis_index("seq")

    if part == 0:
        @pl.when(chunk == 0)
        def _():
            for k in range(groups):
                for slot in range(rows // groups):
                    at = pl.ds(pl.multiple_of(slot * whole + (me ^ k) * span, span), span)
                    grad_ref[at] = sources[k][slot]
            vec_ref[...] = jnp.zeros_like(vec_ref)

            def mask(index, carry):
                @pl.when(left(index) > 0)
                def _():
                    at = pl.ds(pl.multiple_of(index * TILE, TILE), TILE)
                    grad = jnp.where(valid(index), grad_ref[at], jnp.zeros((), BF16))
                    grad_ref[at] = grad
                    vec_ref[0:1] += jnp.sum(grad.astype(F32), axis=0, keepdims=True)
                return carry

            lax.fori_loop(0, tiles, mask, 0)

    def feed(index, first):
        at = pl.ds(pl.multiple_of(index * TILE, TILE), TILE)
        normed = n2_ref[at]
        grad = grad_ref[at]
        hidden = nn(normed, up_ref[...]) + ub_ref[...]
        phi = 0.5 + 0.5 * lax.erf(hidden * (1.0 / math.sqrt(2.0)))
        slope = phi + hidden * (jnp.exp(-0.5 * hidden * hidden) * (1.0 / math.sqrt(2.0 * math.pi)))
        active = (hidden * phi).astype(BF16)
        hidden_grad = (nt(grad, down_ref[...]) * slope).astype(BF16)
        act_ref[at] = active
        hg_ref[at] = hidden_grad
        ddown = tn(active, grad)
        dup = tn(normed, hidden_grad)
        dub = jnp.sum(hidden_grad.astype(F32), axis=0, keepdims=True)
        if first:
            ddown_s[...] = ddown
            dup_s[...] = dup
            dub_ref[...] = dub
        else:
            ddown_s[...] += ddown
            dup_s[...] += dup
            dub_ref[...] += dub

    feed(0, True)

    def more(index, carry):
        pl.when(left(index) > 0)(lambda: feed(index, False))
        return carry

    lax.fori_loop(1, tiles, more, 0)

    def put_rows(dst, index, rows_each, value):
        dst[index * rows_each : (index + 1) * rows_each] = value

    def put_block(dst, index, rows_each, value):
        dst[index, 0] = value

    write_eighths(dup_s, dup_keep, dup_send, Route(True).mine, put_rows)
    write_eighths(ddown_s, ddown_keep, ddown_send, Route(False).mine, put_block)


def feed_forward(part, parts, lengths, groups, n2, sources, up, ub, down):
    tokens, width = n2.shape
    rows = sources[0].shape[0] * groups if part == 0 else lengths.shape[0]
    hidden = up.shape[1] // parts
    count = hidden // FCHUNK
    ahead = part * count
    f32 = lambda *shape: jax.ShapeDtypeStruct(shape, F32)
    bf16 = lambda *shape: jax.ShapeDtypeStruct(shape, BF16)
    const = lambda *shape: pl.BlockSpec(shape, lambda f: (0,) * len(shape))
    out_shape = [bf16(tokens, hidden)] * 2 + [bf16(width // 2, hidden)] * 2
    out_shape += [bf16(4, count, FCHUNK // 8, width)] * 2 + [f32(1, hidden)]
    out_specs = [pl.BlockSpec((tokens, FCHUNK), lambda f: (0, f))] * 2
    out_specs += [pl.BlockSpec((width // 2, FCHUNK), lambda f: (0, f))] * 2
    out_specs += [pl.BlockSpec((4, 1, FCHUNK // 8, width), lambda f: (0, f, 0, 0))] * 2
    out_specs += [pl.BlockSpec((1, FCHUNK), lambda f: (0, f))]
    if part == 0:
        out_shape += [bf16(tokens, width), f32(8, width)]
        out_specs += [const(tokens, width), const(8, width)]
    return pl.pallas_call(
        lambda *refs: feed_kernel(rows, groups, part, *refs),
        grid=(count,),
        out_shape=out_shape,
        in_specs=[SMEM_SPEC] + [VMEM_SPEC] * (1 + len(sources)) + [
            pl.BlockSpec((width, FCHUNK), lambda f: (0, ahead + f)),
            pl.BlockSpec((1, FCHUNK), lambda f: (0, ahead + f)),
            pl.BlockSpec((FCHUNK, width), lambda f: (ahead + f, 0)),
        ],
        out_specs=out_specs,
        scratch_shapes=[pltpu.VMEM((width, FCHUNK), F32), pltpu.VMEM((FCHUNK, width), F32)],
        compiler_params=params(),
        cost_estimate=cost(8 * tokens * width * hidden, 2 * tokens * hidden, 20e6),
        name="feed_forward",
    )(lengths, n2, *sources, up, ub, down)


def store_piece(refs, slot, block, value):
    me = lax.axis_index("seq")
    for k, ref in enumerate(refs):
        @pl.when((block ^ me) == k)
        def _(ref=ref):
            ref[slot] = value


def store_tile(refs, index, whole, value):
    per_slot = whole // TILE
    slot = index // per_slot
    for half in range(TILE // BLK):
        block = (index % per_slot) * (TILE // BLK) + half
        store_piece(refs, slot, block, value[half * BLK : (half + 1) * BLK])


def tile_call(kernel, name, tokens, in_parts, outs, estimate, scratch=()):
    specs = [SMEM_SPEC]
    for array, cut in in_parts[1:]:
        if cut:
            specs.append(pl.BlockSpec((TILE, array.shape[1]), lambda i: (i, 0)))
        else:
            specs.append(VMEM_SPEC)
    out_specs = []
    for shape, _, cut in outs:
        if cut:
            out_specs.append(pl.BlockSpec((TILE, shape[1]), lambda i: (i, 0)))
        else:
            out_specs.append(pl.BlockSpec(shape, lambda i, n=len(shape): (0,) * n))
    return pl.pallas_call(
        kernel,
        grid=(tokens // TILE,),
        out_shape=[jax.ShapeDtypeStruct(shape, kind) for shape, kind, _ in outs],
        in_specs=specs,
        out_specs=out_specs,
        scratch_shapes=list(scratch),
        compiler_params=params(),
        cost_estimate=estimate,
        name=name,
    )(*[array for array, _ in in_parts])


def feed_back_kernel(rows, groups, whole, parts, len_ref, *refs):
    hgs, refs = refs[:parts], refs[parts:]
    (up_ref, grad_ref, mid_ref, ctx_ref, wo_ref, g2_ref,
     mid_grad_ref, ctx_grad_ref, dwo_ref, vec_ref) = refs
    index = pl.program_id(0)
    left, _ = tile_state(len_ref, rows, groups, whole)

    @pl.when(index == 0)
    def _():
        dwo_ref[...] = jnp.zeros_like(dwo_ref)
        vec_ref[...] = jnp.zeros_like(vec_ref)

    @pl.when(left(index) > 0)
    def _():
        size = hgs[0].shape[1]
        back = nt(hgs[0][...], up_ref[:, :size])
        for part in range(1, parts):
            back += nt(hgs[part][...], up_ref[:, part * size : (part + 1) * size])
        hat, rstd = norm_stats(mid_ref[...])
        vec_ref[0:1] += jnp.sum(back * hat, axis=0, keepdims=True)
        vec_ref[1:2] += jnp.sum(back, axis=0, keepdims=True)
        mid_grad = norm_back(back, hat, rstd, g2_ref[...]) + grad_ref[...].astype(F32)
        branch = mid_grad.astype(BF16)
        mid_grad_ref[...] = mid_grad
        vec_ref[2:3] += jnp.sum(branch.astype(F32), axis=0, keepdims=True)
        dwo_ref[...] += tn(ctx_ref[...], branch)
        ctx_grad_ref[...] = nt(branch, wo_ref[...]).astype(BF16)


def feed_out_kernel(rows, groups, whole, parts, len_ref, *refs):
    acts, refs = refs[:parts], refs[parts:]
    (down_ref, mid_ref, bd_ref), outs = refs[:3], refs[3:]
    index = pl.program_id(0)
    left, valid = tile_state(len_ref, rows, groups, whole)

    @pl.when(left(index) > 0)
    def _():
        size = acts[0].shape[1]
        result = mid_ref[...] + bd_ref[...]
        for part in range(parts):
            result += nn(acts[part][...], down_ref[part * size : (part + 1) * size])
        store_tile(outs, index, whole, jnp.where(valid(index), result, 0.0).astype(BF16))

    @pl.when(left(index) <= 0)
    def _():
        store_tile(outs, index, whole, jnp.zeros((TILE, mid_ref.shape[1]), BF16))


def attend_back_kernel(rows, groups, part, len_ref, *refs):
    (normed_ref, q_ref, k_ref, v_ref, ctx_ref, ctx_grad_ref, lse_ref), refs = refs[:7], refs[7:]
    if part == 0:
        dwo_ref, refs = refs[0], refs[1:]
    dqkv_ref, keep_ref, send_ref, vec_ref, dw_s = refs
    slots, whole, width = normed_ref.shape
    size = q_ref.shape[2]
    counts = my_counts(len_ref, rows, groups)
    dw_s[...] = jnp.zeros_like(dw_s)
    vec_ref[...] = jnp.zeros_like(vec_ref)

    def body(slot, count, extent):
        low = first_head(extent)

        def pair(index, carry):
            lanes = pl.ds(pl.multiple_of(index * PAIR, PAIR), PAIR)
            queries = q_ref[slot, :extent, lanes]
            keys = k_ref[slot, :extent, lanes]
            values = v_ref[slot, :extent, lanes]
            grad = ctx_grad_ref[slot, :extent, lanes]
            context = ctx_ref[slot, :extent, lanes]
            keys_t = keys.T
            products = (grad.astype(F32) * context.astype(F32)).T
            dqs, dks, dvs = [], [], []
            for head in range(2):
                mine = slice(head * HEAD, (head + 1) * HEAD)
                delta = jnp.sum(products[mine], axis=0, keepdims=True)
                lse = lse_ref[slot, index, head : head + 1, :extent]
                scores = masked_scores(keep_head(keys, low, head), queries, count, extent)
                probs = jnp.exp2(scores - lse)
                probs_grad = nt(keep_head(values, low, head), grad)
                score_grad = (probs * (probs_grad - delta)).astype(BF16)
                dvs.append(nn(probs.astype(BF16), grad))
                dks.append(nn(score_grad, queries))
                dqs.append(nn(keys_t[mine], score_grad))
            put = lambda which, value: dqkv_ref.__setitem__(
                (slot, slice(0, extent),
                 pl.ds(pl.multiple_of(which * size + index * PAIR, PAIR), PAIR)),
                value.astype(BF16))
            put(0, jnp.concatenate(dqs, axis=0).T * SCALE)
            put(1, jnp.where(low, dks[0], dks[1]) * SCALE)
            put(2, jnp.where(low, dvs[0], dvs[1]))
            return carry

        lax.fori_loop(0, size // PAIR, pair, 0)
        grads = dqkv_ref[slot, :extent]
        dw_s[...] += tn(normed_ref[slot, :extent], grads)
        vec_ref[0:1] += jnp.sum(grads.astype(F32), axis=0, keepdims=True)
        upto = (extent + TILE - 1) // TILE * TILE
        if upto > extent:
            dqkv_ref[slot, extent:upto] = jnp.zeros((upto - extent, 3 * size), BF16)

    def per_slot(slot, carry):
        count = counts[0]
        for other in range(1, slots):
            count = jnp.where(slot == other, counts[other], count)
        for n in range(1, whole // BLK + 1):
            pl.when(blocks_of(count) == n)(lambda n=n: body(slot, count, n * BLK))
        return carry

    lax.fori_loop(0, slots, per_slot, 0)
    mine = Route(part == 0).mine
    stride = keep_ref.shape[0] // 4

    def put(dst, index, rows_each, value):
        dst[index * stride : index * stride + rows_each] = value

    write_eighths(dw_s, keep_ref, send_ref, mine, put)
    if part == 0:
        def put_out(dst, index, rows_each, value):
            at, cut = index * stride + width // 8, 2 * rows_each // 3
            dst[at : at + cut, :width] = value[:cut]
            dst[at : at + cut // 2, width:] = value[cut:, : width // 2]
            dst[at + cut // 2 : at + cut, width:] = value[cut:, width // 2 :]

        write_eighths(dwo_ref, keep_ref, send_ref, mine, put_out)


def attend_back(part, groups, lengths, normed, qkv, ctx, ctx_grad, lse, dwo):
    slots, whole, width = normed.shape
    half = width // 2
    stride = width // 8 + (width // 12 if part == 0 else 0)
    column = lambda block: pl.BlockSpec((slots, whole, half), lambda i: (0, 0, block))
    const = lambda *shape: pl.BlockSpec(shape, lambda i: (0,) * len(shape))
    pairs = width // PAIR // 2
    bf16 = lambda *shape: jax.ShapeDtypeStruct(shape, BF16)
    return pl.pallas_call(
        lambda *refs: attend_back_kernel(slots * groups, groups, part, *refs),
        grid=(1,),
        out_shape=[
            bf16(slots, whole, 3 * half), bf16(4 * stride, 3 * half), bf16(4 * stride, 3 * half),
            jax.ShapeDtypeStruct((8, 3 * half), F32),
        ],
        in_specs=[SMEM_SPEC, VMEM_SPEC, column(part), column(2 + part), column(4 + part),
                  column(part), column(part),
                  pl.BlockSpec((slots, pairs, 8, whole), lambda i: (0, part, 0, 0))]
        + [VMEM_SPEC] * (part == 0),
        out_specs=[const(slots, whole, 3 * half), const(4 * stride, 3 * half),
                   const(4 * stride, 3 * half), const(8, 3 * half)],
        scratch_shapes=[pltpu.VMEM((width, 3 * half), F32)],
        compiler_params=params(),
        cost_estimate=cost(9e9, 3e6, 12e6),
        name="attend_back",
    )(lengths, normed, qkv, qkv, qkv, ctx, ctx_grad, lse, *([dwo] if part == 0 else []))


def input_back_kernel(rows, groups, whole, len_ref, *refs):
    (grad_a, grad_b, w_ref, x_ref, mid_grad_ref, gain_ref), refs = refs[:6], refs[6:]
    outs, vec_ref = refs[:groups], refs[groups]
    index = pl.program_id(0)
    left, _ = tile_state(len_ref, rows, groups, whole)
    width = x_ref.shape[1]
    half = width // 2

    @pl.when(index == 0)
    def _():
        vec_ref[...] = jnp.zeros_like(vec_ref)

    @pl.when(left(index) > 0)
    def _():
        back = jnp.zeros((TILE, width), F32)
        for part, grads in enumerate((grad_a, grad_b)):
            for which in range(3):
                start = which * width + part * half
                back += nt(grads[:, which * half : (which + 1) * half],
                           w_ref[:, start : start + half])
        hat, rstd = norm_stats(x_ref[...].astype(F32))
        vec_ref[0:1] += jnp.sum(back * hat, axis=0, keepdims=True)
        vec_ref[1:2] += jnp.sum(back, axis=0, keepdims=True)
        grad = norm_back(back, hat, rstd, gain_ref[...]) + mid_grad_ref[...]
        store_tile(outs, index, whole, grad.astype(BF16))

    @pl.when(left(index) <= 0)
    def _():
        store_tile(outs, index, whole, jnp.zeros((TILE, width), BF16))


def shards(
    molecules, lengths, norm1_gain, norm1_bias, qkv_weight, query_bias, value_bias, out_weight,
    out_bias, norm2_gain, norm2_bias, up_weight, up_bias, down_weight, down_bias, cotangent,
):
    rows, span, width = molecules.shape
    hidden = up_weight.shape[1]
    groups = lax.axis_size("seq")
    slots, whole = rows // groups, span * groups
    tokens = slots * whole
    line = lambda v: v.reshape(1, -1)
    shift = line(jnp.concatenate([query_bias, jnp.zeros_like(query_bias), value_bias]))
    g1, b1, g2, b2 = line(norm1_gain), line(norm1_bias), line(norm2_gain), line(norm2_bias)
    route_x, route_y = Route(True), Route(False)
    eighth_rows = width // 8

    pieces = swap(deal(lengths, molecules, groups))
    cots = swap(deal(lengths, cotangent, groups))
    saved = ()
    for slot in range(slots):
        saved = attend(slot, lengths, pieces, g1, b1, qkv_weight, shift, out_weight,
                       line(out_bias), g2, b2, saved)
    x, normed, qkv, ctx, lse, mid, n2 = saved
    flat = lambda v: v.reshape(tokens, v.shape[-1])

    part_hidden = hidden // PARTS
    part_chunks = part_hidden // FCHUNK
    acts, hgs, dubs, pairs, order = [], [], [], [], Order()
    rows_of = lambda v: v.reshape(-1, width)

    def feed(part, n2, sources):
        act, hg, dup_keep, dup_send, ddown_keep, ddown_send, dub, *rest = feed_forward(
            part, PARTS, lengths, groups, n2, sources, up_weight, line(up_bias), down_weight)
        acts.append(act)
        hgs.append(hg)
        dubs.append(dub)
        pairs.append((
            Sum(order, dup_keep, dup_send, route_x),
            Sum(order, rows_of(ddown_keep), rows_of(ddown_send), route_y),
        ))
        return rest

    grad_out, down_bias_sum = feed(0, flat(n2), cots)
    feed(1, flat(n2), [grad_out])
    (u0, d0), (u1, d1) = pairs
    u0.halve()
    d0.halve()
    mid_grad, ctx_grad, dwo, vec_mid = order(
        lambda hg0, hg1: tile_call(
            lambda *refs: feed_back_kernel(rows, groups, whole, PARTS, *refs), "feed_back", tokens,
            [(lengths, False), (hg0, True), (hg1, True), (up_weight, False), (grad_out, True),
             (flat(mid), True), (flat(ctx), True), (out_weight, False), (g2, False)],
            [((tokens, width), F32, True), ((tokens, width), BF16, True),
             ((width, width), F32, False), ((8, width), F32, False)],
            cost(2 * tokens * width * (hidden + 2 * width), 0, 25e6)),
        *hgs)
    u0.halve()
    d0.halve()
    u1.halve()
    d1.halve()

    ctx_grad = ctx_grad.reshape(slots, whole, width)
    half = 3 * width // 2

    def back(part):
        dqkv, keep, send, vec = order(
            lambda grad: attend_back(part, groups, lengths, normed, qkv, ctx, grad, lse, dwo),
            ctx_grad)
        return dqkv, vec, Sum(order, keep, send, (route_x, route_y)[part])

    dqkv_a, vec_qkv_a, q0 = back(0)
    u0.settle()
    u0.send_far()
    d0.settle()
    d0.send_far()
    u1.halve()
    d1.halve()
    dqkv_b, vec_qkv_b, q1 = back(1)

    u1.settle()
    d1.settle()
    far_pair = reduce_far_together((u1.low, d1.low))
    q0.halve()
    u0.fold_far()
    u0.send_far()
    d0.fold_far()
    d0.send_far()
    *grad_pieces, vec_in = order(
        lambda grads: tile_call(
            lambda *refs: input_back_kernel(rows, groups, whole, *refs), "input_back", tokens,
            [(lengths, False), (flat(dqkv_a), True), (flat(grads), True), (qkv_weight, False),
             (flat(x), True), (mid_grad, True), (g1, False)],
            [((slots, span, width), BF16, False)] * groups + [((8, width), F32, False)],
            cost(6 * tokens * width * width, 0, 15e6)),
        dqkv_b)
    q1.halve()
    out_pieces = order(
        lambda act0, act1: tile_call(
            lambda *refs: feed_out_kernel(rows, groups, whole, PARTS, *refs), "feed_out", tokens,
            [(lengths, False), (act0, True), (act1, True), (down_weight, False),
             (flat(mid), True), (line(down_bias), False)],
            [((slots, span, width), BF16, False)] * groups,
            cost(2 * tokens * width * hidden, 0, 16e6)),
        *acts)
    third = lambda which: jnp.concatenate(
        [vec[:1, which * width // 2 : (which + 1) * width // 2]
         for vec in (vec_qkv_a, vec_qkv_b)], axis=1)
    small_ways = [PAIR_WAY, ("seq", 2), ("dp", 1)] + far_ways()
    small = order(
        lambda *parts: jnp.concatenate(parts, axis=0),
        vec_in[:2], third(0), third(2), vec_mid[:3], down_bias_sum[:1],
        jnp.concatenate(dubs, axis=1).reshape(-1, width))
    small_arriving = cross(small, small_ways.pop(0))

    def small_step():
        nonlocal small, small_arriving
        small = order(lambda a, b: a + b, small, small_arriving)
        if small_ways:
            small_arriving = cross(small, small_ways.pop(0))

    q0.halve()
    q1.halve()
    small_step()
    u0.fold_far()
    u0.gather_second()
    d0.fold_far()
    d0.gather_second()
    q1.settle()
    q1.send_far()
    q0.settle()
    q0.send_far()
    small_step()
    u0.gather_first()
    d0.gather_first()
    q1.fold_far()
    q1.send_far()
    small_step()
    q0.fold_far()
    q0.send_far()
    grad_pieces = swap(order(lambda *v: v, *grad_pieces))
    u0.gather_pair()
    d0.gather_pair()

    def columns(start, size):
        def place(outs, e, got, stage):
            stage[...] = got.astype(F32)
            rows_at = pl.ds(pl.multiple_of(e * eighth_rows, eighth_rows), eighth_rows)
            return [(stage, outs[0].at[rows_at, pl.ds(start, size)])]
        return place

    def blocks(part):
        def place(outs, e, got, stage):
            stage[...] = got.astype(F32).reshape(stage.shape)
            return [(stage, outs[0].at[pl.ds(part * part_chunks, part_chunks), e])]
        return place

    def qkv_and_out(outs, e, got, stage):
        stage[...] = got.astype(F32)
        cut = width // 12
        rows_at = pl.ds(pl.multiple_of(e * eighth_rows, eighth_rows), eighth_rows)
        begin = pl.multiple_of(e * eighth_rows, eighth_rows)
        left_rows = pl.ds(begin, cut)
        moves = [(stage.at[pl.ds(eighth_rows, cut), pl.ds(0, width)], outs[1].at[left_rows])]
        for side in range(2):
            moves.append((
                stage.at[pl.ds(eighth_rows + side * cut // 2, cut // 2), pl.ds(width, width // 2)],
                outs[1].at[pl.ds(pl.multiple_of(begin + cut, 8), cut // 2),
                           pl.ds(side * width // 2, width // 2)]))
        return qkv_moves(outs, rows_at, stage, 0) + moves

    def qkv_moves(outs, rows_at, stage, part):
        third = width // 2
        return [
            (stage.at[pl.ds(0, eighth_rows), pl.ds(which * third, third)],
             outs[0].at[rows_at, pl.ds(which * width + part * third, third)])
            for which in range(3)
        ]

    def qkv_only(outs, e, got, stage):
        stage[...] = got.astype(F32)
        return qkv_moves(
            outs, pl.ds(pl.multiple_of(e * eighth_rows, eighth_rows), eighth_rows), stage, 1)

    def spread_up(part, before):
        return order(
            lambda *parts: spread(parts, True, [(width, hidden)], (eighth_rows, part_hidden),
                                  columns(part * part_hidden, part_hidden), before),
            *(u0, u1)[part].parts)

    def spread_down(part, before):
        return order(
            lambda *parts: spread(parts, False, [(hidden // FCHUNK, 8, FCHUNK // 8, width)],
                                  (part_chunks, FCHUNK // 8, width), blocks(part), before),
            *(d0, d1)[part].parts)

    dup = spread_up(0, ())
    q1.fold_far()
    q1.gather_second()
    u1.low, d1.low = order(lambda *v: v, *far_pair)
    u1.gather_second()
    d1.gather_second()
    small_step()
    ddown = spread_down(0, ())
    q1.gather_first()
    q0.fold_far()
    q0.gather_second()
    u1.gather_first()
    d1.gather_first()
    small_step()
    molecules_grad = order(lambda *v: undeal(lengths, v, F32), *grad_pieces)
    q1.gather_pair()
    q0.gather_first()
    out_pieces = swap(order(lambda *v: v, *out_pieces))
    u1.gather_pair()
    d1.gather_pair()
    (dqkv,) = order(
        lambda *parts: spread(parts, False, [(width, 3 * width)], (eighth_rows, half), qkv_only),
        *q1.parts)
    dup = spread_up(1, dup)
    ddown = spread_down(1, ddown)
    q0.gather_pair()
    dqkv, dwo = order(
        lambda *parts: spread(parts, True, [(width, 3 * width), (width, width)],
                              (eighth_rows + width // 12, half), qkv_and_out, (dqkv,)),
        *q0.parts)
    output = order(lambda *v: undeal(lengths, v, BF16), *out_pieces)
    dup, ddown = dup[0], ddown[0].reshape(hidden, width)
    return (
        output, molecules_grad, small[0], small[1], dqkv, small[2], small[3], dwo, small[6],
        small[4], small[5], dup, small[8 : 8 + hidden // width].reshape(-1), ddown, small[7],
    )


def solution(mesh):
    tokens, whole = P("dp", "seq", None), P()
    in_specs = (tokens, P("dp")) + (whole,) * 13 + (tokens,)
    out_specs = (tokens, tokens) + (whole,) * 13
    return jax.shard_map(shards, mesh=mesh, in_specs=in_specs, out_specs=out_specs, check_vma=False)
```

```python
import math

import jax
import jax.numpy as jnp
from jax import lax
from jax.experimental import pallas as pl
from jax.experimental.pallas import tpu as pltpu
from jax.sharding import PartitionSpec as P

HEAD = 64
PAIR = 2 * HEAD
BLK = 128
TILE = 256
FCHUNK = 512
PARTS = 2
WEIGHT = 0.5
LOG2E = 1.4426950408889634
SCALE = 1.0 / math.sqrt(HEAD)
NEG = -1e30
EPS = 1e-12
F32 = jnp.float32
BF16 = jnp.bfloat16
VMEM_LIMIT = 24 * 1024 * 1024

SMEM_SPEC = pl.BlockSpec(memory_space=pltpu.SMEM)
VMEM_SPEC = pl.BlockSpec(memory_space=pltpu.VMEM)
ANY_SPEC = pl.BlockSpec(memory_space=pl.ANY)


def cost(flops, exps, moved):
    return pl.CostEstimate(
        flops=int(flops * WEIGHT), transcendentals=int(exps * WEIGHT), bytes_accessed=int(moved * WEIGHT))


def params():
    return pltpu.CompilerParams(vmem_limit_bytes=VMEM_LIMIT)


def in_hbm(array):
    return pltpu.with_memory_space_constraint(array, pltpu.HBM)


def nn(a, b):
    return lax.dot_general(a, b, (((1,), (0,)), ((), ())), preferred_element_type=F32)


def nt(a, b):
    return lax.dot_general(a, b, (((1,), (1,)), ((), ())), preferred_element_type=F32)


def tn(a, b):
    return lax.dot_general(a, b, (((0,), (0,)), ((), ())), preferred_element_type=F32)


def ranks_of(len_ref, rows):
    lens = [len_ref[r] for r in range(rows)]
    ranks = []
    for r in range(rows):
        rank = jnp.int32(0)
        for other in range(rows):
            if other < r:
                rank += (lens[other] >= lens[r]).astype(jnp.int32)
            elif other > r:
                rank += (lens[other] > lens[r]).astype(jnp.int32)
        ranks.append(rank)
    return lens, ranks


def rank_at(slot, group, groups):
    return slot * groups + (group if slot % 2 == 0 else groups - 1 - group)


def pick(values, ranks, wanted):
    found = jnp.int32(0)
    for value, rank in zip(values, ranks):
        found += jnp.where(rank == wanted, value, 0)
    return found


def my_counts(len_ref, rows, groups):
    me = lax.axis_index("seq")
    lens, ranks = ranks_of(len_ref, rows)
    return [
        (pick(lens, ranks, rank_at(slot, me, groups)) + 3) // 4
        for slot in range(rows // groups)
    ]


def blocks_of(count):
    return (count + BLK - 1) // BLK


def piece_rows(len_ref, rows, groups):
    me = lax.axis_index("seq")
    _, ranks = ranks_of(len_ref, rows)
    indices = [jnp.int32(r) for r in range(rows)]
    return {
        (slot, k): pick(indices, ranks, rank_at(slot, me ^ k, groups))
        for slot in range(rows // groups)
        for k in range(groups)
    }


def deal_kernel(rows, groups, len_ref, src, *dsts):
    for (slot, k), row in piece_rows(len_ref, rows, groups).items():
        dsts[k][slot] = src[row]


def deal(lengths, values, groups):
    rows, span, width = values.shape
    return pl.pallas_call(
        lambda *refs: deal_kernel(rows, groups, *refs),
        out_shape=[jax.ShapeDtypeStruct((rows // groups, span, width), values.dtype)] * groups,
        in_specs=[SMEM_SPEC, VMEM_SPEC],
        out_specs=[VMEM_SPEC] * groups,
        compiler_params=params(),
        cost_estimate=cost(0, 0, 3e6),
        name="deal_rows",
    )(lengths, values)


def undeal_kernel(rows, groups, len_ref, *rest):
    srcs, dst = rest[:groups], rest[groups]
    for (slot, k), row in piece_rows(len_ref, rows, groups).items():
        dst[row] = srcs[k][slot].astype(dst.dtype)


def undeal(lengths, pieces, kind):
    slots, span, width = pieces[0].shape
    groups = len(pieces)
    rows = groups * slots
    return pl.pallas_call(
        lambda *refs: undeal_kernel(rows, groups, *refs),
        out_shape=jax.ShapeDtypeStruct((rows, span, width), kind),
        in_specs=[SMEM_SPEC] + [VMEM_SPEC] * groups,
        out_specs=VMEM_SPEC,
        compiler_params=params(),
        cost_estimate=cost(0, 0, 4e6),
        name="undeal_rows",
    )(lengths, *pieces)


def swap(pieces):
    groups = len(pieces)
    return [pieces[0]] + [
        lax.ppermute(pieces[k], "seq", [(i, i ^ k) for i in range(groups)])
        for k in range(1, groups)
    ]


class Route:
    def __init__(self):
        seq, dp = lax.axis_index("seq"), lax.axis_index("dp")
        pair, y, x = seq & 1, (seq >> 1) & 1, dp & 1
        low, high = x * 2 + y, y * 2 + x
        self.mine = pair * 4 + jnp.where(pair == 0, low, high)
        self.pairs = (1 - pair) * 4 + jnp.where(pair == 0, high, low)

    def eighth(self, rel):
        return rel ^ self.mine if rel < 4 else (rel - 4) ^ self.pairs


def turn(x_first):
    groups, size = lax.axis_size("seq"), lax.axis_size("dp")
    partners = []
    for dp in range(size):
        for seq in range(groups):
            if (seq % 2 == 0) == x_first:
                partners.append((dp ^ 1) * groups + seq)
            else:
                partners.append(dp * groups + (seq ^ 2))
    return list(enumerate(partners))


FIRST, SECOND = "first", "second"


def cross(values, way):
    if way in (FIRST, SECOND):
        return lax.ppermute(values, ("dp", "seq"), turn(way == FIRST))
    axis, mask = way
    size = lax.axis_size(axis)
    return lax.ppermute(values, axis, [(i, i ^ mask) for i in range(size)])


PAIR_WAY = ("seq", 1)


def fold(keep, recv):
    return (keep.astype(F32) + recv.astype(F32)).astype(keep.dtype)


def fold_halves(keep, recv):
    rows = keep.shape[0] // 2
    high = fold(keep[rows:], recv[rows:])
    return fold(keep[:rows], recv[:rows]), high


def far_ways():
    size, mask, ways = lax.axis_size("dp"), 2, []
    while mask < size:
        ways.append(("dp", mask))
        mask *= 2
    return ways


class Order:
    def __init__(self):
        self.last = None

    def __call__(self, step, *values):
        if self.last is not None:
            values, _ = lax.optimization_barrier((values, self.last))
        out = step(*values)
        self.last = jax.tree.leaves(out)
        return out


class Sum:
    def __init__(self, order, keep, send):
        self.order, self.low = order, keep
        self.arriving = cross(send, PAIR_WAY)
        self.ways = [FIRST, SECOND]
        self.far = far_ways()

    def halve(self):
        self.low, high = self.order(fold_halves, self.low, self.arriving)
        self.arriving = cross(high, self.ways.pop(0))

    def settle(self):
        self.low = self.order(fold, self.low, self.arriving)

    def send_far(self):
        self.arriving = cross(self.low, self.far.pop(0))

    def fold_far(self):
        self.low = self.order(fold, self.low, self.arriving)

    def gather_second(self):
        self.one = cross(self.low, SECOND)

    def gather_first(self):
        self.pair = self.order(stack, self.low, self.one)
        self.two = cross(self.pair, FIRST)

    def gather_pair(self):
        near = [self.low, self.one, self.two]
        self.parts = near + [cross(part, PAIR_WAY) for part in near]


def line_size():
    return lax.axis_size("dp") // 2


def line_index():
    return lax.axis_index("dp") // 2 if line_size() == QUARTERS else 0


def fold_quarters_kernel(keep, recv, *outs):
    rows = outs[0].shape[0]
    for q in (*range(1, len(outs)), 0):
        at = slice(q * rows, (q + 1) * rows)
        outs[q][...] = (keep[at].astype(F32) + recv[at].astype(F32)).astype(keep.dtype)


def sum_kernel(*refs):
    total = refs[0][...].astype(F32)
    for ref in refs[1:-1]:
        total += ref[...].astype(F32)
    refs[-1][...] = total.astype(refs[-1].dtype)


class Pieces:
    def __init__(self, order, keep, send):
        self.order, self.low = order, keep
        self.arriving = cross(send, PAIR_WAY)
        self.ways = [FIRST, SECOND]

    halve = Sum.halve

    def settle(self):
        rows, width = self.low.shape
        quarter = ((rows // QUARTERS, width), self.low.dtype)
        self.quarters = self.order(
            lambda *v: small_call(fold_quarters_kernel, "fold_quarters", [quarter] * QUARTERS, *v),
            self.low, self.arriving)

    def send_line(self):
        if line_size() == QUARTERS:
            self.arriving = [cross(self.quarters[q], ("dp", 2 * q)) for q in range(1, QUARTERS)]
        else:
            size = lax.axis_size("dp")
            lines = [[i for i in range(size) if i % 2 == parity] for parity in range(2)]
            self.arriving = lax.psum(stack(*self.quarters), "dp", axis_index_groups=lines)

    def fold_line(self):
        if line_size() != QUARTERS:
            return
        mine = self.quarters[0]
        (self.low,) = self.order(
            lambda *v: small_call(sum_kernel, "sum_quarters", [(mine.shape, mine.dtype)], *v),
            mine, *self.arriving)
        self.arriving = [cross(self.low, ("dp", 2 * q)) for q in range(1, QUARTERS)]

    def join(self):
        if line_size() == QUARTERS:
            self.low = self.order(stack, self.low, *self.arriving)
        else:
            self.low = self.order(lambda v: v, self.arriving)
        self.one = cross(self.low, SECOND)

    def gather_first(self):
        self.pair = self.order(stack, self.low, self.one)
        self.two = cross(self.pair, FIRST)

    def gather_pair(self):
        near = [self.pair, self.two]
        self.parts = near + [cross(part, PAIR_WAY) for part in near]


def stack(*parts):
    return jnp.concatenate(parts, axis=0)


def lay_kernel(part, *refs):
    gathered, (up, down, up_s, down_s, sems) = refs[:4], refs[-5:]
    route, line = Route(), line_index()
    slots = up_s.shape[0]
    size, down_rows = FCHUNK, FCHUNK // 32
    chunks = down_s.shape[1]
    columns = size // QUARTERS
    up_rows = up_s.shape[1] // 2
    copies = {}
    for rel in range(8):
        slot = rel % slots
        for copy in copies.pop(slot, ()):
            copy.wait()
        for q in range(QUARTERS):
            quarter = q ^ line
            piece = ((rel % 2) * QUARTERS + q) * (2 * up_rows)
            got = gathered[rel // 2].at[piece : piece + 2 * up_rows]
            for chunk in range(chunks):
                to = pl.ds(pl.multiple_of(chunk * size + quarter * columns, columns), columns)
                for half in range(2):
                    lanes = slice((2 * chunk + half) * columns, (2 * chunk + half + 1) * columns)
                    up_s[slot, half * up_rows : (half + 1) * up_rows, to] = (
                        got[:up_rows, lanes].astype(F32))
                at = up_rows + chunk * down_rows
                to = pl.ds(pl.multiple_of(quarter * down_rows, down_rows), down_rows)
                down_s[slot, chunk, to] = got[at : at + down_rows].astype(F32)
        eighth = route.eighth(rel)
        rows = pl.ds(pl.multiple_of(eighth * (2 * up_rows), 2 * up_rows), 2 * up_rows)
        copies[slot] = [
            pltpu.make_async_copy(
                up_s.at[slot], up.at[rows, pl.ds(part * chunks * size, chunks * size)],
                sems.at[slot, 0]),
            pltpu.make_async_copy(
                down_s.at[slot], down.at[pl.ds(part * chunks, chunks), eighth], sems.at[slot, 1]),
        ]
        for copy in copies[slot]:
            copy.start()
    for pair in copies.values():
        for copy in pair:
            copy.wait()


def lay_pieces(part, parts, gathered, width, hidden, before=()):
    chunks = hidden // FCHUNK // parts
    return pl.pallas_call(
        lambda *refs: lay_kernel(part, *refs),
        out_shape=[
            jax.ShapeDtypeStruct((width, hidden), F32),
            jax.ShapeDtypeStruct((hidden // FCHUNK, 8, FCHUNK // 8, width), F32),
        ],
        in_specs=[VMEM_SPEC] * 4 + [ANY_SPEC] * len(before),
        out_specs=[ANY_SPEC] * 2,
        scratch_shapes=[
            pltpu.VMEM((4, width // 8, chunks * FCHUNK), F32),
            pltpu.VMEM((4, chunks, FCHUNK // 8, width), F32),
            pltpu.SemaphoreType.DMA((4, 2)),
        ],
        input_output_aliases={4 + i: i for i in range(len(before))},
        compiler_params=params(),
        cost_estimate=cost(0, 0, 14e6),
        name="lay_pieces",
    )(*gathered, *before)


def eighth(parts, rel):
    which = (rel % 4).bit_length()
    return parts[which + 3 * (rel // 4)], rel % 4 - (1 << which >> 1)


def small_call(kernel, name, outs, *values):
    return pl.pallas_call(
        kernel,
        out_shape=[jax.ShapeDtypeStruct(shape, kind) for shape, kind in outs],
        in_specs=[VMEM_SPEC] * len(values),
        out_specs=[VMEM_SPEC] * len(outs),
        compiler_params=params(),
        cost_estimate=cost(0, 0, 1e6),
        name=name,
    )(*values)


def pack_kernel(vec_in, vec_a, vec_b, vec_mid, down_bias, *rest):
    dubs, out = rest[:-1], rest[-1]
    width = out.shape[1]
    half = width // 2
    out[...] = jnp.zeros_like(out)
    out[0:2] = vec_in[0:2]
    for which in (0, 2):
        row = 2 + which // 2
        for side, vec in enumerate((vec_a, vec_b)):
            out[row : row + 1, side * half : (side + 1) * half] = (
                vec[0:1, which * half : (which + 1) * half])
    out[4:7] = vec_mid[0:3]
    out[7:8] = down_bias[0:1]
    row = 8
    for dub in dubs:
        for start in range(0, dub.shape[1], width):
            out[row : row + 1] = dub[0:1, start : start + width]
            row += 1


def spread_kernel(place, parts, out, stage, sems):
    route = Route()
    rows = parts[0].shape[0]
    copies = []
    for rel in range(8):
        part, index = eighth(parts, rel)
        got = part[index * rows : (index + 1) * rows]
        moves = place(out, route.eighth(rel), got, stage.at[rel])
        for i, (src, dst) in enumerate(moves):
            copy = pltpu.make_async_copy(src, dst, sems.at[rel, i])
            copy.start()
            copies.append(copy)
    for copy in copies:
        copy.wait()


def spread(parts, shapes, stage, place, before=()):
    before = [array for array in before]
    count = len(shapes)

    def kernel(*refs):
        outs = refs[6 + len(before) : 6 + len(before) + count]
        spread_kernel(place, refs[:6], outs, *refs[6 + len(before) + count :])

    return pl.pallas_call(
        kernel,
        out_shape=[jax.ShapeDtypeStruct(shape, F32) for shape in shapes],
        in_specs=[VMEM_SPEC] * 6 + [ANY_SPEC] * len(before),
        out_specs=[ANY_SPEC] * count,
        scratch_shapes=[pltpu.VMEM((8,) + stage, F32), pltpu.SemaphoreType.DMA((8, 6))],
        input_output_aliases={6 + i: i for i in range(len(before))},
        compiler_params=params(),
        cost_estimate=cost(0, 0, 3e6),
        name="spread",
    )(*parts, *before)


def norm_stats(values):
    center = values - jnp.mean(values, axis=-1, keepdims=True)
    rstd = lax.rsqrt(jnp.mean(center * center, axis=-1, keepdims=True) + EPS)
    return center * rstd, rstd


def norm_back(grad, hat, rstd, gain):
    scaled = grad * gain
    mean_scaled = jnp.mean(scaled, axis=-1, keepdims=True)
    mean_dot = jnp.mean(scaled * hat, axis=-1, keepdims=True)
    return rstd * (scaled - mean_scaled - hat * mean_dot)


def first_head(rows):
    return lax.broadcasted_iota(jnp.int32, (rows, PAIR), 1) < HEAD


def keep_head(values, low, head):
    zero = jnp.zeros_like(values)
    return jnp.where(low, values, zero) if head == 0 else jnp.where(low, zero, values)


def masked_scores(keys, queries, count, extent):
    scores = nt(keys, queries) * (SCALE * LOG2E)
    tail = scores[extent - BLK :]
    position = lax.broadcasted_iota(jnp.int32, tail.shape, 0) + (extent - BLK)
    tail = jnp.where(position < count, tail, NEG)
    if extent == BLK:
        return tail
    return jnp.concatenate([scores[: extent - BLK], tail], axis=0)


def attend_kernel(rows, groups, slot, len_ref, *refs):
    refs = list(refs)
    take = lambda n: [refs.pop(0) for _ in range(n)]
    pieces = take(groups)
    gain_ref, bias_ref, w_ref, shift_ref, wo_ref, bo_ref, g2_ref, b2_ref = take(8)
    if slot:
        take(7)
    x_ref, normed_ref, qkv_ref, ctx_ref, lse_ref, mid_ref, n2_ref = [ref.at[0] for ref in refs]
    count = my_counts(len_ref, rows, groups)[slot]
    whole, width = x_ref.shape
    span = whole // groups
    me = lax.axis_index("seq")
    for k in range(groups):
        x_ref[pl.ds(pl.multiple_of((me ^ k) * span, span), span)] = pieces[k][0]

    def body(extent):
        hat, _ = norm_stats(x_ref[:extent].astype(F32))
        normed = (hat * gain_ref[...] + bias_ref[...]).astype(BF16)
        normed_ref[:extent] = normed
        for part in range(3):
            cols = slice(part * width, (part + 1) * width)
            qkv_ref[:extent, cols] = (nn(normed, w_ref[:, cols]) + shift_ref[:, cols]).astype(BF16)
        low = first_head(extent)

        def pair(index, carry):
            start = pl.multiple_of(index * PAIR, PAIR)
            queries = qkv_ref[:extent, pl.ds(start, PAIR)]
            keys = qkv_ref[:extent, pl.ds(width + start, PAIR)]
            values = qkv_ref[:extent, pl.ds(2 * width + start, PAIR)]
            values_t = values.T
            outs = []
            for head in range(2):
                scores = masked_scores(keep_head(keys, low, head), queries, count, extent)
                top = jnp.max(scores, axis=0, keepdims=True)
                expo = jnp.exp2(scores - top)
                total = jnp.sum(expo, axis=0, keepdims=True)
                out = nn(values_t[head * HEAD : (head + 1) * HEAD], expo.astype(BF16))
                outs.append(out * (1.0 / total))
                lse_ref[index, head : head + 1, :extent] = top + jnp.log2(total)
            ctx_ref[:extent, pl.ds(start, PAIR)] = jnp.concatenate(outs, axis=0).T.astype(BF16)
            return carry

        lax.fori_loop(0, width // PAIR, pair, 0)
        middle = x_ref[:extent].astype(F32) + nn(ctx_ref[:extent], wo_ref[...]) + bo_ref[...]
        mid_ref[:extent] = middle
        hat, _ = norm_stats(middle)
        n2_ref[:extent] = (hat * g2_ref[...] + b2_ref[...]).astype(BF16)
        upto = (extent + TILE - 1) // TILE * TILE
        for ref in (normed_ref, ctx_ref, mid_ref, n2_ref):
            if upto > extent:
                ref[extent:upto] = jnp.zeros((upto - extent, width), ref.dtype)

    blocks = blocks_of(count)
    for n in range(1, whole // BLK + 1):
        pl.when(blocks == n)(lambda n=n: body(n * BLK))


def attend(slot, lengths, pieces, gain, bias, weight, shift, wo, bo, g2, b2, before):
    groups = len(pieces)
    slots, span, width = pieces[0].shape
    rows, whole = slots * groups, span * groups
    shapes = [
        ((slots, whole, width), BF16),
        ((slots, whole, width), BF16),
        ((slots, whole, 3 * width), BF16),
        ((slots, whole, width), BF16),
        ((slots, width // PAIR, 8, whole), F32),
        ((slots, whole, width), F32),
        ((slots, whole, width), BF16),
    ]
    one = lambda shape: pl.BlockSpec((1,) + shape[1:], lambda i: (slot,) + (0,) * (len(shape) - 1))
    return pl.pallas_call(
        lambda *refs: attend_kernel(rows, groups, slot, *refs),
        grid=(1,),
        out_shape=[jax.ShapeDtypeStruct(shape, kind) for shape, kind in shapes],
        in_specs=[SMEM_SPEC] + [one((slots, span, width))] * groups + [VMEM_SPEC] * 8
        + [ANY_SPEC] * len(before),
        out_specs=[one(shape) for shape, _ in shapes],
        input_output_aliases={1 + groups + 8 + i: i for i in range(len(before))},
        compiler_params=params(),
        cost_estimate=cost(5e9, 3e6, 12e6),
        name="attend",
    )(lengths, *pieces, gain, bias, weight, shift, wo, bo, g2, b2, *before)


def tile_state(len_ref, rows, groups, whole):
    counts = my_counts(len_ref, rows, groups)
    per_slot = whole // TILE

    def left(index):
        count = counts[0]
        for slot in range(1, len(counts)):
            count = jnp.where(index // per_slot == slot, counts[slot], count)
        return count - (index % per_slot) * TILE

    def valid(index):
        return lax.broadcasted_iota(jnp.int32, (TILE, 1), 0) < left(index)

    return left, valid


def write_eighths(scratch, keep, send, write):
    rows_each, route = scratch.shape[0] // 8, Route()
    for rel in range(8):
        at = pl.ds(pl.multiple_of(route.eighth(rel) * rows_each, rows_each), rows_each)
        write((keep, send)[rel // 4], rel % 4, rows_each, scratch[at].astype(BF16))


QUARTERS = 4


def write_pieces(dup_s, ddown_s, keep, send, line, chunk):
    route = Route()
    width, size = dup_s.shape
    up_rows, down_rows = width // 16, size // 32
    columns = size // QUARTERS
    for rel in range(8):
        dst = (keep, send)[rel // 4]
        eighth = route.eighth(rel)
        for q in range(QUARTERS):
            quarter = q ^ line
            piece = ((rel % 4) * QUARTERS + q) * (2 * up_rows)
            lanes = pl.ds(pl.multiple_of(quarter * columns, columns), columns)
            for half in range(2):
                begin = eighth * (2 * up_rows) + half * up_rows
                value = dup_s[pl.ds(pl.multiple_of(begin, up_rows), up_rows), lanes]
                to = pl.ds(pl.multiple_of((2 * chunk + half) * columns, columns), columns)
                dst[piece : piece + up_rows, to] = value.astype(BF16)
            begin = (eighth * QUARTERS + quarter) * down_rows
            value = ddown_s[pl.ds(pl.multiple_of(begin, down_rows), down_rows)]
            to = piece + up_rows + chunk * down_rows
            dst[pl.ds(pl.multiple_of(to, down_rows), down_rows)] = value.astype(BF16)


def feed_kernel(rows, groups, part, len_ref, *refs):
    refs = list(refs)
    take = lambda n: [refs.pop(0) for _ in range(n)]
    n2_ref = take(1)[0]
    sources = take(groups if part == 0 else 1)
    up_ref, ub_ref, down_ref = take(3)
    act_ref, hg_ref, keep_ref, send_ref, dub_ref = take(5)
    if part == 0:
        grad_ref, vec_ref = take(2)
    else:
        grad_ref = sources[0]
    dup_s, ddown_s = refs
    chunk = pl.program_id(0)
    tokens, width = n2_ref.shape
    whole = tokens // (rows // groups)
    span = whole // groups
    left, valid = tile_state(len_ref, rows, groups, whole)
    tiles = tokens // TILE
    me = lax.axis_index("seq")

    if part == 0:
        @pl.when(chunk == 0)
        def _():
            for k in range(groups):
                for slot in range(rows // groups):
                    at = pl.ds(pl.multiple_of(slot * whole + (me ^ k) * span, span), span)
                    grad_ref[at] = sources[k][slot]
            vec_ref[...] = jnp.zeros_like(vec_ref)

            def mask(index, carry):
                @pl.when(left(index) > 0)
                def _():
                    at = pl.ds(pl.multiple_of(index * TILE, TILE), TILE)
                    grad = jnp.where(valid(index), grad_ref[at], jnp.zeros((), BF16))
                    grad_ref[at] = grad
                    vec_ref[0:1] += jnp.sum(grad.astype(F32), axis=0, keepdims=True)
                return carry

            lax.fori_loop(0, tiles, mask, 0)

    def feed(index, first):
        at = pl.ds(pl.multiple_of(index * TILE, TILE), TILE)
        normed = n2_ref[at]
        grad = grad_ref[at]
        hidden = nn(normed, up_ref[...]) + ub_ref[...]
        phi = 0.5 + 0.5 * lax.erf(hidden * (1.0 / math.sqrt(2.0)))
        slope = phi + hidden * (jnp.exp(-0.5 * hidden * hidden) * (1.0 / math.sqrt(2.0 * math.pi)))
        active = (hidden * phi).astype(BF16)
        hidden_grad = (nt(grad, down_ref[...]) * slope).astype(BF16)
        act_ref[at] = active
        hg_ref[at] = hidden_grad
        ddown = tn(active, grad)
        dup = tn(normed, hidden_grad)
        dub = jnp.sum(hidden_grad.astype(F32), axis=0, keepdims=True)
        if first:
            ddown_s[...] = ddown
            dup_s[...] = dup
            dub_ref[...] = dub
        else:
            ddown_s[...] += ddown
            dup_s[...] += dup
            dub_ref[...] += dub

    feed(0, True)

    def more(index, carry):
        pl.when(left(index) > 0)(lambda: feed(index, False))
        return carry

    lax.fori_loop(1, tiles, more, 0)

    write_pieces(dup_s, ddown_s, keep_ref, send_ref, line_index(), chunk)


def feed_forward(part, parts, lengths, groups, n2, sources, up, ub, down):
    tokens, width = n2.shape
    rows = sources[0].shape[0] * groups if part == 0 else lengths.shape[0]
    hidden = up.shape[1] // parts
    count = hidden // FCHUNK
    ahead = part * count
    f32 = lambda *shape: jax.ShapeDtypeStruct(shape, F32)
    bf16 = lambda *shape: jax.ShapeDtypeStruct(shape, BF16)
    const = lambda *shape: pl.BlockSpec(shape, lambda f: (0,) * len(shape))
    half = (hidden * width) // width
    out_shape = [pltpu.HBM((tokens, hidden), BF16)] * 2 + [bf16(half, width)] * 2 + [f32(1, hidden)]
    out_specs = [pl.BlockSpec((tokens, FCHUNK), lambda f: (0, f))] * 2
    out_specs += [const(half, width)] * 2 + [pl.BlockSpec((1, FCHUNK), lambda f: (0, f))]
    if part == 0:
        out_shape += [bf16(tokens, width), f32(8, width)]
        out_specs += [const(tokens, width), const(8, width)]
    return pl.pallas_call(
        lambda *refs: feed_kernel(rows, groups, part, *refs),
        grid=(count,),
        out_shape=out_shape,
        in_specs=[SMEM_SPEC] + [VMEM_SPEC] * (1 + len(sources)) + [
            pl.BlockSpec((width, FCHUNK), lambda f: (0, ahead + f)),
            pl.BlockSpec((1, FCHUNK), lambda f: (0, ahead + f)),
            pl.BlockSpec((FCHUNK, width), lambda f: (ahead + f, 0)),
        ],
        out_specs=out_specs,
        scratch_shapes=[pltpu.VMEM((width, FCHUNK), F32), pltpu.VMEM((FCHUNK, width), F32)],
        compiler_params=params(),
        cost_estimate=cost(8 * tokens * width * hidden, 2 * tokens * hidden, 20e6),
        name="feed_forward",
    )(lengths, n2, *sources, in_hbm(up), ub, in_hbm(down))


def store_piece(refs, slot, block, value):
    me = lax.axis_index("seq")
    for k, ref in enumerate(refs):
        @pl.when((block ^ me) == k)
        def _(ref=ref):
            ref[slot] = value


def store_tile(refs, index, whole, value):
    per_slot = whole // TILE
    slot = index // per_slot
    for half in range(TILE // BLK):
        block = (index % per_slot) * (TILE // BLK) + half
        store_piece(refs, slot, block, value[half * BLK : (half + 1) * BLK])


def tile_call(kernel, name, tokens, in_parts, outs, estimate, scratch=()):
    specs = [SMEM_SPEC]
    for array, cut in in_parts[1:]:
        if cut:
            specs.append(pl.BlockSpec((TILE, array.shape[1]), lambda i: (i, 0)))
        else:
            specs.append(VMEM_SPEC)
    out_specs = []
    for shape, _, cut in outs:
        if cut:
            out_specs.append(pl.BlockSpec((TILE, shape[1]), lambda i: (i, 0)))
        else:
            out_specs.append(pl.BlockSpec(shape, lambda i, n=len(shape): (0,) * n))
    return pl.pallas_call(
        kernel,
        grid=(tokens // TILE,),
        out_shape=[jax.ShapeDtypeStruct(shape, kind) for shape, kind, _ in outs],
        in_specs=specs,
        out_specs=out_specs,
        scratch_shapes=list(scratch),
        compiler_params=params(),
        cost_estimate=estimate,
        name=name,
    )(*[array for array, _ in in_parts])


def feed_back_kernel(rows, groups, whole, parts, len_ref, *refs):
    hgs, refs = refs[:parts], refs[parts:]
    (up_ref, grad_ref, mid_ref, ctx_ref, wo_ref, g2_ref,
     mid_grad_ref, ctx_grad_ref, dwo_ref, vec_ref) = refs
    index = pl.program_id(0)
    left, _ = tile_state(len_ref, rows, groups, whole)

    @pl.when(index == 0)
    def _():
        dwo_ref[...] = jnp.zeros_like(dwo_ref)
        vec_ref[...] = jnp.zeros_like(vec_ref)

    @pl.when(left(index) > 0)
    def _():
        size = hgs[0].shape[1]
        back = nt(hgs[0][...], up_ref[:, :size])
        for part in range(1, parts):
            back += nt(hgs[part][...], up_ref[:, part * size : (part + 1) * size])
        hat, rstd = norm_stats(mid_ref[...])
        vec_ref[0:1] += jnp.sum(back * hat, axis=0, keepdims=True)
        vec_ref[1:2] += jnp.sum(back, axis=0, keepdims=True)
        mid_grad = norm_back(back, hat, rstd, g2_ref[...]) + grad_ref[...].astype(F32)
        branch = mid_grad.astype(BF16)
        mid_grad_ref[...] = mid_grad
        vec_ref[2:3] += jnp.sum(branch.astype(F32), axis=0, keepdims=True)
        dwo_ref[...] += tn(ctx_ref[...], branch)
        ctx_grad_ref[...] = nt(branch, wo_ref[...]).astype(BF16)


def feed_out_kernel(rows, groups, whole, parts, len_ref, *refs):
    acts, refs = refs[:parts], refs[parts:]
    (down_ref, mid_ref, bd_ref), outs = refs[:3], refs[3:]
    index = pl.program_id(0)
    left, valid = tile_state(len_ref, rows, groups, whole)

    @pl.when(left(index) > 0)
    def _():
        size = acts[0].shape[1]
        result = mid_ref[...] + bd_ref[...]
        for part in range(parts):
            result += nn(acts[part][...], down_ref[part * size : (part + 1) * size])
        store_tile(outs, index, whole, jnp.where(valid(index), result, 0.0).astype(BF16))

    @pl.when(left(index) <= 0)
    def _():
        store_tile(outs, index, whole, jnp.zeros((TILE, mid_ref.shape[1]), BF16))


def attend_back_kernel(rows, groups, part, len_ref, *refs):
    (normed_ref, q_ref, k_ref, v_ref, ctx_ref, ctx_grad_ref, lse_ref), refs = refs[:7], refs[7:]
    if part == 0:
        dwo_ref, refs = refs[0], refs[1:]
    dqkv_ref, keep_ref, send_ref, vec_ref, dw_s = refs
    slots, whole, width = normed_ref.shape
    size = q_ref.shape[2]
    counts = my_counts(len_ref, rows, groups)
    dw_s[...] = jnp.zeros_like(dw_s)
    vec_ref[...] = jnp.zeros_like(vec_ref)

    def body(slot, count, extent):
        low = first_head(extent)

        def pair(index, carry):
            lanes = pl.ds(pl.multiple_of(index * PAIR, PAIR), PAIR)
            queries = q_ref[slot, :extent, lanes]
            keys = k_ref[slot, :extent, lanes]
            values = v_ref[slot, :extent, lanes]
            grad = ctx_grad_ref[slot, :extent, lanes]
            context = ctx_ref[slot, :extent, lanes]
            keys_t = keys.T
            products = (grad.astype(F32) * context.astype(F32)).T
            dqs, dks, dvs = [], [], []
            for head in range(2):
                mine = slice(head * HEAD, (head + 1) * HEAD)
                delta = jnp.sum(products[mine], axis=0, keepdims=True)
                lse = lse_ref[slot, index, head : head + 1, :extent]
                scores = masked_scores(keep_head(keys, low, head), queries, count, extent)
                probs = jnp.exp2(scores - lse)
                probs_grad = nt(keep_head(values, low, head), grad)
                score_grad = (probs * (probs_grad - delta)).astype(BF16)
                dvs.append(nn(probs.astype(BF16), grad))
                dks.append(nn(score_grad, queries))
                dqs.append(nn(keys_t[mine], score_grad))
            put = lambda which, value: dqkv_ref.__setitem__(
                (slot, slice(0, extent),
                 pl.ds(pl.multiple_of(which * size + index * PAIR, PAIR), PAIR)),
                value.astype(BF16))
            put(0, jnp.concatenate(dqs, axis=0).T * SCALE)
            put(1, jnp.where(low, dks[0], dks[1]) * SCALE)
            put(2, jnp.where(low, dvs[0], dvs[1]))
            return carry

        lax.fori_loop(0, size // PAIR, pair, 0)
        grads = dqkv_ref[slot, :extent]
        dw_s[...] += tn(normed_ref[slot, :extent], grads)
        vec_ref[0:1] += jnp.sum(grads.astype(F32), axis=0, keepdims=True)
        upto = (extent + TILE - 1) // TILE * TILE
        if upto > extent:
            dqkv_ref[slot, extent:upto] = jnp.zeros((upto - extent, 3 * size), BF16)

    def per_slot(slot, carry):
        count = counts[0]
        for other in range(1, slots):
            count = jnp.where(slot == other, counts[other], count)
        for n in range(1, whole // BLK + 1):
            pl.when(blocks_of(count) == n)(lambda n=n: body(slot, count, n * BLK))
        return carry

    lax.fori_loop(0, slots, per_slot, 0)
    stride = keep_ref.shape[0] // 4

    def put(dst, index, rows_each, value):
        dst[index * stride : index * stride + rows_each] = value

    write_eighths(dw_s, keep_ref, send_ref, put)
    if part == 0:
        def put_out(dst, index, rows_each, value):
            at, cut = index * stride + width // 8, 2 * rows_each // 3
            dst[at : at + cut, :width] = value[:cut]
            dst[at : at + cut // 2, width:] = value[cut:, : width // 2]
            dst[at + cut // 2 : at + cut, width:] = value[cut:, width // 2 :]

        write_eighths(dwo_ref, keep_ref, send_ref, put_out)


def attend_back(part, groups, lengths, normed, qkv, ctx, ctx_grad, lse, dwo):
    slots, whole, width = normed.shape
    half = width // 2
    stride = width // 8 + (width // 12 if part == 0 else 0)
    column = lambda block: pl.BlockSpec((slots, whole, half), lambda i: (0, 0, block))
    const = lambda *shape: pl.BlockSpec(shape, lambda i: (0,) * len(shape))
    pairs = width // PAIR // 2
    bf16 = lambda *shape: jax.ShapeDtypeStruct(shape, BF16)
    return pl.pallas_call(
        lambda *refs: attend_back_kernel(slots * groups, groups, part, *refs),
        grid=(1,),
        out_shape=[
            bf16(slots, whole, 3 * half), bf16(4 * stride, 3 * half), bf16(4 * stride, 3 * half),
            jax.ShapeDtypeStruct((8, 3 * half), F32),
        ],
        in_specs=[SMEM_SPEC, VMEM_SPEC, column(part), column(2 + part), column(4 + part),
                  column(part), column(part),
                  pl.BlockSpec((slots, pairs, 8, whole), lambda i: (0, part, 0, 0))]
        + [VMEM_SPEC] * (part == 0),
        out_specs=[const(slots, whole, 3 * half), const(4 * stride, 3 * half),
                   const(4 * stride, 3 * half), const(8, 3 * half)],
        scratch_shapes=[pltpu.VMEM((width, 3 * half), F32)],
        compiler_params=params(),
        cost_estimate=cost(9e9, 3e6, 12e6),
        name="attend_back",
    )(lengths, normed, qkv, qkv, qkv, ctx, ctx_grad, lse, *([dwo] if part == 0 else []))


def input_back_kernel(rows, groups, whole, len_ref, *refs):
    (grad_a, grad_b, w_ref, x_ref, mid_grad_ref, gain_ref), refs = refs[:6], refs[6:]
    outs, vec_ref = refs[:groups], refs[groups]
    index = pl.program_id(0)
    left, _ = tile_state(len_ref, rows, groups, whole)
    width = x_ref.shape[1]
    half = width // 2

    @pl.when(index == 0)
    def _():
        vec_ref[...] = jnp.zeros_like(vec_ref)

    @pl.when(left(index) > 0)
    def _():
        back = jnp.zeros((TILE, width), F32)
        for part, grads in enumerate((grad_a, grad_b)):
            for which in range(3):
                start = which * width + part * half
                back += nt(grads[:, which * half : (which + 1) * half],
                           w_ref[:, start : start + half])
        hat, rstd = norm_stats(x_ref[...].astype(F32))
        vec_ref[0:1] += jnp.sum(back * hat, axis=0, keepdims=True)
        vec_ref[1:2] += jnp.sum(back, axis=0, keepdims=True)
        grad = norm_back(back, hat, rstd, gain_ref[...]) + mid_grad_ref[...]
        store_tile(outs, index, whole, grad.astype(BF16))

    @pl.when(left(index) <= 0)
    def _():
        store_tile(outs, index, whole, jnp.zeros((TILE, width), BF16))


def shards(
    molecules, lengths, norm1_gain, norm1_bias, qkv_weight, query_bias, value_bias, out_weight,
    out_bias, norm2_gain, norm2_bias, up_weight, up_bias, down_weight, down_bias, cotangent,
):
    rows, span, width = molecules.shape
    hidden = up_weight.shape[1]
    groups = lax.axis_size("seq")
    slots, whole = rows // groups, span * groups
    tokens = slots * whole
    line = lambda v: v.reshape(1, -1)
    shift = line(jnp.concatenate([query_bias, jnp.zeros_like(query_bias), value_bias]))
    g1, b1, g2, b2 = line(norm1_gain), line(norm1_bias), line(norm2_gain), line(norm2_bias)
    eighth_rows = width // 8

    pieces = swap(deal(lengths, molecules, groups))
    cots = swap(deal(lengths, cotangent, groups))
    saved = ()
    for slot in range(slots):
        saved = attend(slot, lengths, pieces, g1, b1, qkv_weight, shift, out_weight,
                       line(out_bias), g2, b2, saved)
    x, normed, qkv, ctx, lse, mid, n2 = saved
    flat = lambda v: v.reshape(tokens, v.shape[-1])

    acts, hgs, dubs, order = [], [], [], Order()

    def feed(part, n2, sources):
        act, hg, keep, send, dub, *rest = feed_forward(
            part, PARTS, lengths, groups, n2, sources, up_weight, line(up_bias), down_weight)
        acts.append(act)
        hgs.append(hg)
        dubs.append(dub)
        pieces.append(Pieces(order, keep, send))
        return rest, keep

    pieces = []
    (grad_out, down_bias_sum), _ = feed(0, flat(n2), cots)
    p0 = pieces[0]
    p0.halve()
    order(lambda values: feed(1, values, [grad_out]), flat(n2))
    p1 = pieces[1]
    out_pieces = order(
        lambda act0, act1: tile_call(
            lambda *refs: feed_out_kernel(rows, groups, whole, PARTS, *refs), "feed_out", tokens,
            [(lengths, False), (act0, True), (act1, True), (down_weight, False),
             (flat(mid), True), (line(down_bias), False)],
            [((slots, span, width), BF16, False)] * groups,
            cost(2 * tokens * width * hidden, 0, 16e6)),
        *acts)
    p1.halve()
    p0.halve()
    mid_grad, ctx_grad, dwo, vec_mid = order(
        lambda hg0, hg1: tile_call(
            lambda *refs: feed_back_kernel(rows, groups, whole, PARTS, *refs), "feed_back", tokens,
            [(lengths, False), (hg0, True), (hg1, True), (up_weight, False), (grad_out, True),
             (flat(mid), True), (flat(ctx), True), (out_weight, False), (g2, False)],
            [((tokens, width), F32, True), ((tokens, width), BF16, True),
             ((width, width), F32, False), ((8, width), F32, False)],
            cost(2 * tokens * width * (hidden + 2 * width), 0, 25e6)),
        *hgs)
    p0.settle()
    p0.send_line()
    p1.halve()
    out_pieces = swap(order(lambda *v: v, *out_pieces))

    ctx_grad = ctx_grad.reshape(slots, whole, width)
    half = 3 * width // 2

    def back(part):
        dqkv, keep, send, vec = order(
            lambda grad: attend_back(part, groups, lengths, normed, qkv, ctx, grad, lse, dwo),
            ctx_grad)
        return dqkv, vec, Sum(order, keep, send)

    dqkv_a, vec_qkv_a, q0 = back(0)
    p0.fold_line()
    p1.settle()
    p1.send_line()
    dqkv_b, vec_qkv_b, q1 = back(1)
    q0.halve()
    output = order(lambda *v: undeal(lengths, v, BF16), *out_pieces)
    p0.join()
    p1.fold_line()
    *grad_pieces, vec_in = order(
        lambda grads: tile_call(
            lambda *refs: input_back_kernel(rows, groups, whole, *refs), "input_back", tokens,
            [(lengths, False), (flat(dqkv_a), True), (flat(grads), True), (qkv_weight, False),
             (flat(x), True), (mid_grad, True), (g1, False)],
            [((slots, span, width), BF16, False)] * groups + [((8, width), F32, False)],
            cost(6 * tokens * width * width, 0, 15e6)),
        dqkv_b)
    q1.halve()
    p0.gather_first()
    q0.halve()
    p1.join()
    small_ways = [PAIR_WAY, ("seq", 2), ("dp", 1)] + far_ways()
    small = order(
        lambda *parts: small_call(pack_kernel, "pack_small", [((16, width), F32)], *parts)[0],
        vec_in, vec_qkv_a, vec_qkv_b, vec_mid, down_bias_sum, *dubs)
    small_arriving = cross(small, small_ways.pop(0))

    def small_step():
        nonlocal small, small_arriving
        small = order(lambda a, b: a + b, small, small_arriving)
        if small_ways:
            small_arriving = cross(small, small_ways.pop(0))

    q1.halve()
    q0.settle()
    q0.send_far()
    p0.gather_pair()
    p1.gather_first()
    small_step()
    q1.settle()
    q1.send_far()
    dup, ddown = order(lambda *v: lay_pieces(0, PARTS, v, width, hidden), *p0.parts)
    q0.fold_far()
    q0.send_far()
    q1.fold_far()
    q1.send_far()
    small_step()
    p1.gather_pair()
    grad_pieces = swap(order(lambda *v: v, *grad_pieces))
    dup, ddown = order(
        lambda *v: lay_pieces(1, PARTS, v, width, hidden, (dup, ddown)), *p1.parts)
    small_step()
    q0.fold_far()
    q0.gather_second()
    q1.fold_far()
    q1.gather_second()
    small_step()
    molecules_grad = order(lambda *v: undeal(lengths, v, F32), *grad_pieces)
    q0.gather_first()
    q1.gather_first()
    small_step()
    q0.gather_pair()
    q1.gather_pair()
    while small_ways:
        small_step()
    ddown = ddown.reshape(hidden, width)

    def qkv_and_out(outs, e, got, stage):
        stage[...] = got.astype(F32)
        cut = width // 12
        rows_at = pl.ds(pl.multiple_of(e * eighth_rows, eighth_rows), eighth_rows)
        begin = pl.multiple_of(e * eighth_rows, eighth_rows)
        left_rows = pl.ds(begin, cut)
        moves = [(stage.at[pl.ds(eighth_rows, cut), pl.ds(0, width)], outs[1].at[left_rows])]
        for side in range(2):
            moves.append((
                stage.at[pl.ds(eighth_rows + side * cut // 2, cut // 2), pl.ds(width, width // 2)],
                outs[1].at[pl.ds(pl.multiple_of(begin + cut, 8), cut // 2),
                           pl.ds(side * width // 2, width // 2)]))
        return qkv_moves(outs, rows_at, stage, 0) + moves

    def qkv_moves(outs, rows_at, stage, part):
        third = width // 2
        return [
            (stage.at[pl.ds(0, eighth_rows), pl.ds(which * third, third)],
             outs[0].at[rows_at, pl.ds(which * width + part * third, third)])
            for which in range(3)
        ]

    def qkv_only(outs, e, got, stage):
        stage[...] = got.astype(F32)
        return qkv_moves(
            outs, pl.ds(pl.multiple_of(e * eighth_rows, eighth_rows), eighth_rows), stage, 1)

    (dqkv,) = order(
        lambda *parts: spread(parts, [(width, 3 * width)], (eighth_rows, half), qkv_only),
        *q1.parts)
    dqkv, dwo = order(
        lambda *parts: spread(parts, [(width, 3 * width), (width, width)],
                              (eighth_rows + width // 12, half), qkv_and_out, (dqkv,)),
        *q0.parts)
    return (
        output, molecules_grad, small[0], small[1], dqkv, small[2], small[3], dwo, small[6],
        small[4], small[5], dup, small[8 : 8 + hidden // width].reshape(-1), ddown, small[7],
    )


def solution(mesh):
    tokens, whole = P("dp", "seq", None), P()
    in_specs = (tokens, P("dp")) + (whole,) * 13 + (tokens,)
    out_specs = (tokens, tokens) + (whole,) * 13
    return jax.shard_map(shards, mesh=mesh, in_specs=in_specs, out_specs=out_specs, check_vma=False)
```

```python
import math

import jax
import jax.numpy as jnp
from jax import lax
from jax.experimental import pallas as pl
from jax.experimental.pallas import tpu as pltpu
from jax.sharding import PartitionSpec as P

HEAD = 64
PAIR = 2 * HEAD
BLK = 128
TILE = 256
FCHUNK = 512
PARTS = 2
WEIGHT = 0.5
LOG2E = 1.4426950408889634
SCALE = 1.0 / math.sqrt(HEAD)
NEG = -1e30
EPS = 1e-12
F32 = jnp.float32
BF16 = jnp.bfloat16
VMEM_LIMIT = 24 * 1024 * 1024

SMEM_SPEC = pl.BlockSpec(memory_space=pltpu.SMEM)
VMEM_SPEC = pl.BlockSpec(memory_space=pltpu.VMEM)
ANY_SPEC = pl.BlockSpec(memory_space=pl.ANY)


def cost(flops, exps, moved):
    return pl.CostEstimate(
        flops=int(flops * WEIGHT), transcendentals=int(exps * WEIGHT), bytes_accessed=int(moved * WEIGHT))


def params(limit=VMEM_LIMIT):
    return pltpu.CompilerParams(vmem_limit_bytes=limit)


def in_hbm(array):
    return pltpu.with_memory_space_constraint(array, pltpu.HBM)


def nn(a, b):
    return lax.dot_general(a, b, (((1,), (0,)), ((), ())), preferred_element_type=F32)


def nt(a, b):
    return lax.dot_general(a, b, (((1,), (1,)), ((), ())), preferred_element_type=F32)


def tn(a, b):
    return lax.dot_general(a, b, (((0,), (0,)), ((), ())), preferred_element_type=F32)


def ranks_of(len_ref, rows):
    lens = [len_ref[r] for r in range(rows)]
    ranks = []
    for r in range(rows):
        rank = jnp.int32(0)
        for other in range(rows):
            if other < r:
                rank += (lens[other] >= lens[r]).astype(jnp.int32)
            elif other > r:
                rank += (lens[other] > lens[r]).astype(jnp.int32)
        ranks.append(rank)
    return lens, ranks


def rank_at(slot, group, groups):
    return slot * groups + (group if slot % 2 == 0 else groups - 1 - group)


def pick(values, ranks, wanted):
    found = jnp.int32(0)
    for value, rank in zip(values, ranks):
        found += jnp.where(rank == wanted, value, 0)
    return found


def my_counts(len_ref, rows, groups):
    me = lax.axis_index("seq")
    lens, ranks = ranks_of(len_ref, rows)
    return [
        (pick(lens, ranks, rank_at(slot, me, groups)) + 3) // 4
        for slot in range(rows // groups)
    ]


def blocks_of(count):
    return (count + BLK - 1) // BLK


def piece_rows(len_ref, rows, groups):
    me = lax.axis_index("seq")
    _, ranks = ranks_of(len_ref, rows)
    indices = [jnp.int32(r) for r in range(rows)]
    return {
        (slot, k): pick(indices, ranks, rank_at(slot, me ^ k, groups))
        for slot in range(rows // groups)
        for k in range(groups)
    }


def deal_kernel(rows, groups, apart, len_ref, src, *dsts):
    for (slot, k), row in piece_rows(len_ref, rows, groups).items():
        if apart:
            dsts[slot * groups + k][0] = src[row]
        else:
            dsts[k][slot] = src[row]


def deal(lengths, values, groups, apart=False):
    rows, span, width = values.shape
    slots = rows // groups
    count, deep = (slots * groups, 1) if apart else (groups, slots)
    return pl.pallas_call(
        lambda *refs: deal_kernel(rows, groups, apart, *refs),
        out_shape=[jax.ShapeDtypeStruct((deep, span, width), values.dtype)] * count,
        in_specs=[SMEM_SPEC, VMEM_SPEC],
        out_specs=[VMEM_SPEC] * count,
        compiler_params=params(),
        cost_estimate=cost(0, 0, 3e6),
        name="deal_rows",
    )(lengths, values)


def undeal_kernel(rows, groups, len_ref, *rest):
    srcs, dst = rest[:groups], rest[groups]
    for (slot, k), row in piece_rows(len_ref, rows, groups).items():
        dst[row] = srcs[k][slot].astype(dst.dtype)


def undeal(lengths, pieces, kind):
    slots, span, width = pieces[0].shape
    groups = len(pieces)
    rows = groups * slots
    return pl.pallas_call(
        lambda *refs: undeal_kernel(rows, groups, *refs),
        out_shape=jax.ShapeDtypeStruct((rows, span, width), kind),
        in_specs=[SMEM_SPEC] + [VMEM_SPEC] * groups,
        out_specs=VMEM_SPEC,
        compiler_params=params(),
        cost_estimate=cost(0, 0, 4e6),
        name="undeal_rows",
    )(lengths, *pieces)


def swap(pieces):
    groups = len(pieces)
    return [pieces[0]] + [
        lax.ppermute(pieces[k], "seq", [(i, i ^ k) for i in range(groups)])
        for k in range(1, groups)
    ]


class Route:
    def __init__(self):
        seq, dp = lax.axis_index("seq"), lax.axis_index("dp")
        pair, y, x = seq & 1, (seq >> 1) & 1, dp & 1
        low, high = x * 2 + y, y * 2 + x
        self.mine = pair * 4 + jnp.where(pair == 0, low, high)
        self.pairs = (1 - pair) * 4 + jnp.where(pair == 0, high, low)

    def eighth(self, rel):
        return rel ^ self.mine if rel < 4 else (rel - 4) ^ self.pairs


def turn(x_first):
    groups, size = lax.axis_size("seq"), lax.axis_size("dp")
    partners = []
    for dp in range(size):
        for seq in range(groups):
            if (seq % 2 == 0) == x_first:
                partners.append((dp ^ 1) * groups + seq)
            else:
                partners.append(dp * groups + (seq ^ 2))
    return list(enumerate(partners))


FIRST, SECOND = "first", "second"


def cross(values, way):
    if way in (FIRST, SECOND):
        return lax.ppermute(values, ("dp", "seq"), turn(way == FIRST))
    axis, mask = way
    size = lax.axis_size(axis)
    return lax.ppermute(values, axis, [(i, i ^ mask) for i in range(size)])


PAIR_WAY = ("seq", 1)


def far_ways():
    size, mask, ways = lax.axis_size("dp"), 2, []
    while mask < size:
        ways.append(("dp", mask))
        mask *= 2
    return ways


class Order:
    def __init__(self):
        self.last = None

    def __call__(self, step, *values):
        if self.last is not None:
            values, _ = lax.optimization_barrier((values, self.last))
        out = step(*values)
        self.last = jax.tree.leaves(out)
        return out


def line_size():
    return lax.axis_size("dp") // 2


def line_index():
    return (lax.axis_index("dp") // 2) % QUARTERS


def halve_kernel(keep, recv, low, high):
    rows = low.shape[0]
    for out, at in ((high, slice(rows, 2 * rows)), (low, slice(0, rows))):
        out[...] = (keep[at].astype(F32) + recv[at].astype(F32)).astype(out.dtype)


def sum_kernel(*refs):
    total = refs[0][...].astype(F32)
    for ref in refs[1:-1]:
        total += ref[...].astype(F32)
    refs[-1][...] = total.astype(refs[-1].dtype)


def stack_kernel(*refs):
    begin = 0
    for ref in refs[:-1]:
        refs[-1][begin : begin + ref.shape[0]] = ref[...]
        begin += ref.shape[0]


def merge_kernel(parts, *refs):
    ins, outs = refs[: 2 * parts], refs[2 * parts :]
    rows = ins[0].shape[0] // QUARTERS
    each = QUARTERS // len(outs)
    for q in (2, 3, 1, 0):
        for part in range(parts):
            keep, recv = ins[2 * part : 2 * part + 2]
            at = slice(q * rows, (q + 1) * rows)
            begin = ((q % each) * parts + part) * rows
            outs[q // each][begin : begin + rows] = (
                keep[at].astype(F32) + recv[at].astype(F32)).astype(keep.dtype)


LINE_WAYS = (("dp", 2), ("dp", 4))


def extra_ways():
    return [way for way in far_ways() if way not in LINE_WAYS]


class Steps:
    def next(self):
        return self.steps.pop(0)()

    def shape(self, parts=1, of=1):
        rows, width = self.low.shape
        return ((rows * parts // of, width), self.low.dtype)

    def begin(self):
        def done(send):
            self.arriving = [cross(send, PAIR_WAY)]
        return None, [self.send], None, done

    def halve(self, way):
        def done(low, high):
            self.low, self.arriving = low, [cross(high, way)]
        return halve_kernel, [self.low, *self.arriving], [self.shape(1, 2)] * 2, done

    def double(self, way):
        def done(low):
            self.low, self.arriving = low, [cross(low, way)]
        return sum_kernel, [self.low, *self.arriving], [self.shape()], done

    def gather(self, way):
        def done(low):
            self.low, self.arriving = low, [cross(low, way)]
        return stack_kernel, [self.low, *self.arriving], [self.shape(1 + len(self.arriving))], done

    def gather_pair(self):
        def done(*near):
            self.parts = list(near) + [cross(part, PAIR_WAY) for part in near]
        return None, [self.low, *self.arriving], None, done

    def along_line(self):
        near, far = LINE_WAYS
        ways = extra_ways() + [far]
        return [lambda: self.halve(far)] + [lambda way=way: self.double(way) for way in ways] + [
            lambda way=way: self.gather(way) for way in (near, SECOND, FIRST)]


class Pieces(Steps):
    def __init__(self, keep, send):
        self.low, self.send = keep, send
        self.steps = [self.begin, lambda: self.halve(FIRST), lambda: self.halve(SECOND)]


class Merged(Steps):
    def __init__(self, pieces, straight=False):
        self.pieces = pieces
        if straight and lax.axis_size("dp") == 2 * QUARTERS:
            self.steps = [self.quarter, self.sum]
            self.steps += [lambda way=way: self.gather(way) for way in (SECOND, FIRST)]
        else:
            self.steps = [self.merge] + self.along_line()
        self.steps.append(self.gather_pair)

    def merging(self, outs, done):
        parts = len(self.pieces)
        inputs = [v for one in self.pieces for v in (one.low, *one.arriving)]
        self.low = self.pieces[0].low
        shapes = [self.shape(parts, outs)] * outs
        return (lambda *refs: merge_kernel(parts, *refs)), inputs, shapes, done

    def merge(self):
        def done(low, high):
            self.low, self.arriving = low, [cross(high, LINE_WAYS[0])]
        return self.merging(2, done)

    def send_quarters(self, values):
        return [cross(value, ("dp", 2 * rel)) for value, rel in zip(values, ORDER[1:])]

    def quarter(self):
        def done(*quarters):
            self.low = quarters[0]
            self.arriving = self.send_quarters(quarters[1:])
        return self.merging(QUARTERS, done)

    def sum(self):
        def done(low):
            self.low, self.arriving = low, self.send_quarters([low] * (QUARTERS - 1))
        return sum_kernel, [self.low, *self.arriving], [self.shape()], done


class Small:
    def __init__(self, value):
        self.value = value
        self.ways = [PAIR_WAY, ("seq", 2), ("dp", 1)] + far_ways()
        self.arriving = cross(value, self.ways.pop(0))

    def next(self):
        def done(value):
            self.value = value
            if self.ways:
                self.arriving = cross(value, self.ways.pop(0))
        shape = (self.value.shape, self.value.dtype)
        return sum_kernel, [self.value, self.arriving], [shape], done


def advance(order, *sums):
    steps = [one.next() for one in sums]

    def kernel(*refs):
        refs = list(refs)
        ins, outs = refs[:count], refs[count:]
        for body, inputs, shapes, _ in steps:
            if body is not None:
                body(*ins[: len(inputs)], *outs[: len(shapes)])
                ins, outs = ins[len(inputs) :], outs[len(shapes) :]

    count = sum(len(inputs) for body, inputs, _, _ in steps if body is not None)
    shapes = [shape for body, _, outs, _ in steps if body is not None for shape in outs]

    def step(*values):
        values = list(values)
        worked = [value for value, own in zip(values, owned) if own]
        results = list(small_call(kernel, "advance", shapes, *worked)) if worked else []
        out, at = [], 0
        for body, inputs, own, _ in steps:
            if body is None:
                out.append(values[at : at + len(inputs)])
            else:
                out.append([results.pop(0) for _ in own])
            at += len(inputs)
        return out

    owned = [body is not None for body, inputs, _, _ in steps for _ in inputs]
    outs = order(step, *[value for _, inputs, _, _ in steps for value in inputs])
    for (_, _, _, done), out in zip(steps, outs):
        done(*out)


def lay_kernel(part, parts, *refs):
    gathered, (up, down, up_s, down_s, sems) = refs[:4], refs[-5:]
    route, line = Route(), line_index()
    slots = up_s.shape[0]
    size, down_rows = FCHUNK, FCHUNK // 32
    chunks = down_s.shape[1]
    columns = size // QUARTERS
    up_rows = up_s.shape[1] // 2
    copies = {}
    for rel in range(8):
        slot = rel % slots
        for copy in copies.pop(slot, ()):
            copy.wait()
        for q in range(QUARTERS):
            quarter = ORDER[q] ^ line
            piece = (((rel % 2) * QUARTERS + q) * parts + part) * (2 * up_rows)
            got = gathered[rel // 2].at[piece : piece + 2 * up_rows]
            for chunk in range(chunks):
                to = pl.ds(pl.multiple_of(chunk * size + quarter * columns, columns), columns)
                for half in range(2):
                    lanes = slice((2 * chunk + half) * columns, (2 * chunk + half + 1) * columns)
                    up_s[slot, half * up_rows : (half + 1) * up_rows, to] = (
                        got[:up_rows, lanes].astype(F32))
                at = up_rows + chunk * down_rows
                to = pl.ds(pl.multiple_of(quarter * down_rows, down_rows), down_rows)
                down_s[slot, chunk, to] = got[at : at + down_rows].astype(F32)
        eighth = route.eighth(rel)
        rows = pl.ds(pl.multiple_of(eighth * (2 * up_rows), 2 * up_rows), 2 * up_rows)
        copies[slot] = [
            pltpu.make_async_copy(
                up_s.at[slot], up.at[rows, pl.ds(part * chunks * size, chunks * size)],
                sems.at[slot, 0]),
            pltpu.make_async_copy(
                down_s.at[slot], down.at[pl.ds(part * chunks, chunks), eighth], sems.at[slot, 1]),
        ]
        for copy in copies[slot]:
            copy.start()
    for slot in copies:
        for copy in copies[slot]:
            copy.wait()


def lay_pieces(part, parts, gathered, width, hidden, before=()):
    chunks = hidden // FCHUNK // parts
    return pl.pallas_call(
        lambda *refs: lay_kernel(part, parts, *refs),
        out_shape=[
            jax.ShapeDtypeStruct((width, hidden), F32),
            jax.ShapeDtypeStruct((hidden // FCHUNK, 8, FCHUNK // 8, width), F32),
        ],
        in_specs=[VMEM_SPEC] * 4 + [ANY_SPEC] * len(before),
        out_specs=[ANY_SPEC] * 2,
        scratch_shapes=[
            pltpu.VMEM((4, width // 8, chunks * FCHUNK), F32),
            pltpu.VMEM((4, chunks, FCHUNK // 8, width), F32),
            pltpu.SemaphoreType.DMA((4, 2)),
        ],
        input_output_aliases={4 + i: i for i in range(len(before))},
        compiler_params=params(),
        cost_estimate=cost(0, 0, 14e6),
        name="lay_pieces",
    )(*gathered, *before)


def small_call(kernel, name, outs, *values):
    return pl.pallas_call(
        kernel,
        out_shape=[jax.ShapeDtypeStruct(shape, kind) for shape, kind in outs],
        in_specs=[VMEM_SPEC] * len(values),
        out_specs=[VMEM_SPEC] * len(outs),
        compiler_params=params(VMEM_LIMIT // 2),
        cost_estimate=cost(0, 0, 1e6),
        name=name,
    )(*values)


def pack_kernel(vec_in, vec_a, vec_b, vec_mid, down_bias, *rest):
    dubs, out = rest[:-1], rest[-1]
    width = out.shape[1]
    out[...] = jnp.zeros_like(out)
    out[0:2] = vec_in[0:2]
    for which in (0, 2):
        row, begin = 2 + which // 2, 0
        for vec in (vec_a, vec_b):
            size = vec.shape[1] // 3
            out[row : row + 1, begin : begin + size] = vec[0:1, which * size : (which + 1) * size]
            begin += size
    out[4:7] = vec_mid[0:3]
    out[7:8] = down_bias[0:1]
    row = 8
    for dub in dubs:
        for start in range(0, dub.shape[1], width):
            out[row : row + 1] = dub[0:1, start : start + width]
            row += 1


def lay_qkv_kernel(part, parts, *refs):
    gathered, refs = refs[:4], refs[4 + 2 * part :]
    out, dwo, stage, sems = refs
    route, line = Route(), line_index()
    slots, rows, size = stage.shape
    columns = size // QUARTERS
    width = dwo.shape[1]
    block = width // 3
    begin, count = (0, 2 * block) if part == 0 else (2 * block, block)
    copies = {}
    for rel in range(8):
        slot = rel % slots
        for copy in copies.pop(slot, ()):
            copy.wait()
        for q in range(QUARTERS):
            piece = (((rel % 2) * QUARTERS + q) * parts + part) * rows
            to = pl.ds(pl.multiple_of((ORDER[q] ^ line) * columns, columns), columns)
            stage[slot, :, to] = gathered[rel // 2][piece : piece + rows].astype(F32)
        at = pl.ds(pl.multiple_of(route.eighth(rel) * rows, rows), rows)
        moves = [
            (stage.at[slot, :, pl.ds(which * count, count)],
             out.at[at, pl.ds(which * width + begin, count)])
            for which in range(3)
        ]
        if part == 1:
            moves.append((stage.at[slot, :, pl.ds(3 * count, width)], dwo.at[at]))
        copies[slot] = [
            pltpu.make_async_copy(src, dst, sems.at[slot, i]) for i, (src, dst) in enumerate(moves)
        ]
        for copy in copies[slot]:
            copy.start()
    for slot in copies:
        for copy in copies[slot]:
            copy.wait()


def lay_qkv(part, gathered, width, before=()):
    return pl.pallas_call(
        lambda *refs: lay_qkv_kernel(part, 2, *refs),
        out_shape=[
            jax.ShapeDtypeStruct((width, 3 * width), F32),
            jax.ShapeDtypeStruct((width, width), F32),
        ],
        in_specs=[VMEM_SPEC] * 4 + [ANY_SPEC] * len(before),
        out_specs=[ANY_SPEC] * 2,
        scratch_shapes=[
            pltpu.VMEM((4, width // 8, 2 * width), F32),
            pltpu.SemaphoreType.DMA((4, 4)),
        ],
        input_output_aliases={4 + i: i for i in range(len(before))},
        compiler_params=params(),
        cost_estimate=cost(0, 0, 8e6),
        name="lay_qkv",
    )(*gathered, *before)


def norm_stats(values):
    center = values - jnp.mean(values, axis=-1, keepdims=True)
    rstd = lax.rsqrt(jnp.mean(center * center, axis=-1, keepdims=True) + EPS)
    return center * rstd, rstd


def norm_back(grad, hat, rstd, gain):
    scaled = grad * gain
    mean_scaled = jnp.mean(scaled, axis=-1, keepdims=True)
    mean_dot = jnp.mean(scaled * hat, axis=-1, keepdims=True)
    return rstd * (scaled - mean_scaled - hat * mean_dot)


def first_head(rows):
    return lax.broadcasted_iota(jnp.int32, (rows, PAIR), 1) < HEAD


def keep_head(values, low, head):
    zero = jnp.zeros_like(values)
    return jnp.where(low, values, zero) if head == 0 else jnp.where(low, zero, values)


def masked_scores(keys, queries, count, extent):
    scores = nt(keys, queries) * (SCALE * LOG2E)
    tail = scores[extent - BLK :]
    position = lax.broadcasted_iota(jnp.int32, tail.shape, 0) + (extent - BLK)
    tail = jnp.where(position < count, tail, NEG)
    if extent == BLK:
        return tail
    return jnp.concatenate([scores[: extent - BLK], tail], axis=0)


def attend_kernel(rows, groups, slot, len_ref, *refs):
    refs = list(refs)
    take = lambda n: [refs.pop(0) for _ in range(n)]
    pieces = take(groups)
    gain_ref, bias_ref, w_ref, shift_ref, wo_ref, bo_ref, g2_ref, b2_ref = take(8)
    if slot:
        take(7)
    x_ref, normed_ref, qkv_ref, ctx_ref, lse_ref, mid_ref, n2_ref = [ref.at[0] for ref in refs]
    count = my_counts(len_ref, rows, groups)[slot]
    whole, width = x_ref.shape
    span = whole // groups
    me = lax.axis_index("seq")
    for k in range(groups):
        x_ref[pl.ds(pl.multiple_of((me ^ k) * span, span), span)] = pieces[k][0]

    def body(extent):
        hat, _ = norm_stats(x_ref[:extent].astype(F32))
        normed = (hat * gain_ref[...] + bias_ref[...]).astype(BF16)
        normed_ref[:extent] = normed
        for part in range(3):
            cols = slice(part * width, (part + 1) * width)
            qkv_ref[:extent, cols] = (nn(normed, w_ref[:, cols]) + shift_ref[:, cols]).astype(BF16)
        low = first_head(extent)

        def pair(index, carry):
            start = pl.multiple_of(index * PAIR, PAIR)
            queries = qkv_ref[:extent, pl.ds(start, PAIR)]
            keys = qkv_ref[:extent, pl.ds(width + start, PAIR)]
            values = qkv_ref[:extent, pl.ds(2 * width + start, PAIR)]
            values_t = values.T
            outs = []
            for head in range(2):
                scores = masked_scores(keep_head(keys, low, head), queries, count, extent)
                top = jnp.max(scores, axis=0, keepdims=True)
                expo = jnp.exp2(scores - top)
                total = jnp.sum(expo, axis=0, keepdims=True)
                out = nn(values_t[head * HEAD : (head + 1) * HEAD], expo.astype(BF16))
                outs.append(out * (1.0 / total))
                lse_ref[index, head : head + 1, :extent] = top + jnp.log2(total)
            ctx_ref[:extent, pl.ds(start, PAIR)] = jnp.concatenate(outs, axis=0).T.astype(BF16)
            return carry

        lax.fori_loop(0, width // PAIR, pair, 0)
        middle = x_ref[:extent].astype(F32) + nn(ctx_ref[:extent], wo_ref[...]) + bo_ref[...]
        mid_ref[:extent] = middle
        hat, _ = norm_stats(middle)
        n2_ref[:extent] = (hat * g2_ref[...] + b2_ref[...]).astype(BF16)
        upto = (extent + TILE - 1) // TILE * TILE
        for ref in (normed_ref, ctx_ref, mid_ref, n2_ref):
            if upto > extent:
                ref[extent:upto] = jnp.zeros((upto - extent, width), ref.dtype)

    blocks = blocks_of(count)
    for n in range(1, whole // BLK + 1):
        pl.when(blocks == n)(lambda n=n: body(n * BLK))


def attend(slot, slots, lengths, pieces, gain, bias, weight, shift, wo, bo, g2, b2, before):
    groups = len(pieces)
    _, span, width = pieces[0].shape
    rows, whole = slots * groups, span * groups
    shapes = [
        ((slots, whole, width), BF16),
        ((slots, whole, width), BF16),
        ((slots, whole, 3 * width), BF16),
        ((slots, whole, width), BF16),
        ((slots, width // PAIR, 8, whole), F32),
        ((slots, whole, width), F32),
        ((slots, whole, width), BF16),
    ]
    one = lambda shape: pl.BlockSpec((1,) + shape[1:], lambda i: (slot,) + (0,) * (len(shape) - 1))
    return pl.pallas_call(
        lambda *refs: attend_kernel(rows, groups, slot, *refs),
        grid=(1,),
        out_shape=[jax.ShapeDtypeStruct(shape, kind) for shape, kind in shapes],
        in_specs=[SMEM_SPEC] + [VMEM_SPEC] * (groups + 8)
        + [ANY_SPEC] * len(before),
        out_specs=[one(shape) for shape, _ in shapes],
        input_output_aliases={1 + groups + 8 + i: i for i in range(len(before))},
        compiler_params=params(),
        cost_estimate=cost(5e9, 3e6, 12e6),
        name="attend",
    )(lengths, *pieces, gain, bias, weight, shift, wo, bo, g2, b2, *before)


def tile_state(len_ref, rows, groups, whole):
    counts = my_counts(len_ref, rows, groups)
    per_slot = whole // TILE

    def left(index):
        count = counts[0]
        for slot in range(1, len(counts)):
            count = jnp.where(index // per_slot == slot, counts[slot], count)
        return count - (index % per_slot) * TILE

    def valid(index):
        return lax.broadcasted_iota(jnp.int32, (TILE, 1), 0) < left(index)

    return left, valid


QUARTERS = 4
ORDER = (0, 2, 1, 3)


def write_pieces(dup_s, ddown_s, keep, send, line, chunk):
    route = Route()
    width, size = dup_s.shape
    up_rows, down_rows = width // 16, size // 32
    columns = size // QUARTERS
    for rel in range(8):
        dst = (keep, send)[rel // 4]
        eighth = route.eighth(rel)
        for q in range(QUARTERS):
            quarter = ORDER[q] ^ line
            piece = ((rel % 4) * QUARTERS + q) * (2 * up_rows)
            lanes = pl.ds(pl.multiple_of(quarter * columns, columns), columns)
            for half in range(2):
                begin = eighth * (2 * up_rows) + half * up_rows
                value = dup_s[pl.ds(pl.multiple_of(begin, up_rows), up_rows), lanes]
                to = pl.ds(pl.multiple_of((2 * chunk + half) * columns, columns), columns)
                dst[piece : piece + up_rows, to] = value.astype(BF16)
            begin = (eighth * QUARTERS + quarter) * down_rows
            value = ddown_s[pl.ds(pl.multiple_of(begin, down_rows), down_rows)]
            to = piece + up_rows + chunk * down_rows
            dst[pl.ds(pl.multiple_of(to, down_rows), down_rows)] = value.astype(BF16)


def feed_kernel(rows, groups, part, len_ref, *refs):
    refs = list(refs)
    take = lambda n: [refs.pop(0) for _ in range(n)]
    n2_ref = take(1)[0]
    sources = take(groups if part == 0 else 1)
    up_ref, ub_ref, down_ref = take(3)
    act_ref, hg_ref, keep_ref, send_ref, dub_ref = take(5)
    if part == 0:
        grad_ref, vec_ref = take(2)
    else:
        grad_ref = sources[0]
    dup_s, ddown_s = refs
    chunk = pl.program_id(0)
    tokens, width = n2_ref.shape
    whole = tokens // (rows // groups)
    span = whole // groups
    left, valid = tile_state(len_ref, rows, groups, whole)
    tiles = tokens // TILE
    me = lax.axis_index("seq")

    if part == 0:
        @pl.when(chunk == 0)
        def _():
            for k in range(groups):
                for slot in range(rows // groups):
                    at = pl.ds(pl.multiple_of(slot * whole + (me ^ k) * span, span), span)
                    grad_ref[at] = sources[k][slot]
            vec_ref[...] = jnp.zeros_like(vec_ref)

            def mask(index, carry):
                @pl.when(left(index) > 0)
                def _():
                    at = pl.ds(pl.multiple_of(index * TILE, TILE), TILE)
                    grad = jnp.where(valid(index), grad_ref[at], jnp.zeros((), BF16))
                    grad_ref[at] = grad
                    vec_ref[0:1] += jnp.sum(grad.astype(F32), axis=0, keepdims=True)
                return carry

            lax.fori_loop(0, tiles, mask, 0)

    def feed(index, first):
        at = pl.ds(pl.multiple_of(index * TILE, TILE), TILE)
        normed = n2_ref[at]
        grad = grad_ref[at]
        hidden = nn(normed, up_ref[...]) + ub_ref[...]
        phi = 0.5 + 0.5 * lax.erf(hidden * (1.0 / math.sqrt(2.0)))
        slope = phi + hidden * (jnp.exp(-0.5 * hidden * hidden) * (1.0 / math.sqrt(2.0 * math.pi)))
        active = (hidden * phi).astype(BF16)
        hidden_grad = (nt(grad, down_ref[...]) * slope).astype(BF16)
        act_ref[at] = active
        hg_ref[at] = hidden_grad
        ddown = tn(active, grad)
        dup = tn(normed, hidden_grad)
        dub = jnp.sum(hidden_grad.astype(F32), axis=0, keepdims=True)
        if first:
            ddown_s[...] = ddown
            dup_s[...] = dup
            dub_ref[...] = dub
        else:
            ddown_s[...] += ddown
            dup_s[...] += dup
            dub_ref[...] += dub

    feed(0, True)

    def more(index, carry):
        pl.when(left(index) > 0)(lambda: feed(index, False))
        return carry

    lax.fori_loop(1, tiles, more, 0)

    write_pieces(dup_s, ddown_s, keep_ref, send_ref, line_index(), chunk)


def feed_forward(part, parts, lengths, groups, n2, sources, up, ub, down):
    tokens, width = n2.shape
    rows = sources[0].shape[0] * groups if part == 0 else lengths.shape[0]
    hidden = up.shape[1] // parts
    count = hidden // FCHUNK
    ahead = part * count
    f32 = lambda *shape: jax.ShapeDtypeStruct(shape, F32)
    bf16 = lambda *shape: jax.ShapeDtypeStruct(shape, BF16)
    const = lambda *shape: pl.BlockSpec(shape, lambda f: (0,) * len(shape))
    half = (hidden * width) // width
    out_shape = [pltpu.HBM((tokens, hidden), BF16)] * 2 + [bf16(half, width)] * 2 + [f32(1, hidden)]
    out_specs = [pl.BlockSpec((tokens, FCHUNK), lambda f: (0, f))] * 2
    out_specs += [const(half, width)] * 2 + [pl.BlockSpec((1, FCHUNK), lambda f: (0, f))]
    if part == 0:
        out_shape += [bf16(tokens, width), f32(8, width)]
        out_specs += [const(tokens, width), const(8, width)]
    return pl.pallas_call(
        lambda *refs: feed_kernel(rows, groups, part, *refs),
        grid=(count,),
        out_shape=out_shape,
        in_specs=[SMEM_SPEC] + [VMEM_SPEC] * (1 + len(sources)) + [
            pl.BlockSpec((width, FCHUNK), lambda f: (0, ahead + f)),
            pl.BlockSpec((1, FCHUNK), lambda f: (0, ahead + f)),
            pl.BlockSpec((FCHUNK, width), lambda f: (ahead + f, 0)),
        ],
        out_specs=out_specs,
        scratch_shapes=[pltpu.VMEM((width, FCHUNK), F32), pltpu.VMEM((FCHUNK, width), F32)],
        compiler_params=params(),
        cost_estimate=cost(8 * tokens * width * hidden, 2 * tokens * hidden, 20e6),
        name="feed_forward",
    )(lengths, n2, *sources, in_hbm(up), ub, in_hbm(down))


def store_piece(refs, slot, block, value):
    me = lax.axis_index("seq")
    for k, ref in enumerate(refs):
        @pl.when((block ^ me) == k)
        def _(ref=ref):
            ref[slot] = value


def store_tile(refs, index, whole, value):
    per_slot = whole // TILE
    slot = index // per_slot
    for half in range(TILE // BLK):
        block = (index % per_slot) * (TILE // BLK) + half
        store_piece(refs, slot, block, value[half * BLK : (half + 1) * BLK])


def tile_call(kernel, name, tokens, in_parts, outs, estimate, scratch=()):
    specs = [SMEM_SPEC]
    for array, cut in in_parts[1:]:
        if cut:
            specs.append(pl.BlockSpec((TILE, array.shape[1]), lambda i: (i, 0)))
        else:
            specs.append(VMEM_SPEC)
    out_specs = []
    for shape, _, cut in outs:
        if cut:
            out_specs.append(pl.BlockSpec((TILE, shape[1]), lambda i: (i, 0)))
        else:
            out_specs.append(pl.BlockSpec(shape, lambda i, n=len(shape): (0,) * n))
    return pl.pallas_call(
        kernel,
        grid=(tokens // TILE,),
        out_shape=[jax.ShapeDtypeStruct(shape, kind) for shape, kind, _ in outs],
        in_specs=specs,
        out_specs=out_specs,
        scratch_shapes=list(scratch),
        compiler_params=params(),
        cost_estimate=estimate,
        name=name,
    )(*[array for array, _ in in_parts])


def feed_back_kernel(rows, groups, whole, parts, len_ref, *refs):
    hgs, refs = refs[:parts], refs[parts:]
    (up_ref, grad_ref, mid_ref, ctx_ref, wo_ref, g2_ref,
     mid_grad_ref, ctx_grad_ref, dwo_ref, vec_ref) = refs
    index = pl.program_id(0)
    left, _ = tile_state(len_ref, rows, groups, whole)

    @pl.when(index == 0)
    def _():
        dwo_ref[...] = jnp.zeros_like(dwo_ref)
        vec_ref[...] = jnp.zeros_like(vec_ref)

    @pl.when(left(index) > 0)
    def _():
        size = hgs[0].shape[1]
        back = nt(hgs[0][...], up_ref[:, :size])
        for part in range(1, parts):
            back += nt(hgs[part][...], up_ref[:, part * size : (part + 1) * size])
        hat, rstd = norm_stats(mid_ref[...])
        vec_ref[0:1] += jnp.sum(back * hat, axis=0, keepdims=True)
        vec_ref[1:2] += jnp.sum(back, axis=0, keepdims=True)
        mid_grad = norm_back(back, hat, rstd, g2_ref[...]) + grad_ref[...].astype(F32)
        branch = mid_grad.astype(BF16)
        mid_grad_ref[...] = mid_grad
        vec_ref[2:3] += jnp.sum(branch.astype(F32), axis=0, keepdims=True)
        dwo_ref[...] += tn(ctx_ref[...], branch)
        ctx_grad_ref[...] = nt(branch, wo_ref[...]).astype(BF16)


def feed_out_kernel(rows, groups, whole, parts, len_ref, *refs):
    acts, refs = refs[:parts], refs[parts:]
    (down_ref, mid_ref, bd_ref), outs = refs[:3], refs[3:]
    index = pl.program_id(0)
    left, valid = tile_state(len_ref, rows, groups, whole)

    @pl.when(left(index) > 0)
    def _():
        size = acts[0].shape[1]
        result = mid_ref[...] + bd_ref[...]
        for part in range(parts):
            result += nn(acts[part][...], down_ref[part * size : (part + 1) * size])
        store_tile(outs, index, whole, jnp.where(valid(index), result, 0.0).astype(BF16))

    @pl.when(left(index) <= 0)
    def _():
        store_tile(outs, index, whole, jnp.zeros((TILE, mid_ref.shape[1]), BF16))


def attend_back_kernel(rows, groups, part, len_ref, *refs):
    refs = list(refs)
    take = lambda n: [refs.pop(0) for _ in range(n)]
    blocks = 2 - part
    normed_ref = take(1)[0]
    qs, ks, vs, ctxs, grads = (take(blocks) for _ in range(5))
    lse_ref = take(1)[0]
    if part == 1:
        dwo_ref = take(1)[0]
    dqkv_ref, keep_ref, send_ref, vec_ref, dw_s = refs
    slots, whole, width = normed_ref.shape
    block = qs[0].shape[2]
    size = blocks * block
    counts = my_counts(len_ref, rows, groups)
    dw_s[:, : 3 * size] = jnp.zeros((width, 3 * size), F32)
    vec_ref[...] = jnp.zeros_like(vec_ref)

    def body(slot, count, extent):
        low = first_head(extent)

        def pair(b, index, carry):
            lanes = pl.ds(pl.multiple_of(index * PAIR, PAIR), PAIR)
            queries, keys, values, context, grad = (
                ref[b][slot, :extent, lanes] for ref in (qs, ks, vs, ctxs, grads))
            keys_t = keys.T
            products = (grad.astype(F32) * context.astype(F32)).T
            dqs, dks, dvs = [], [], []
            for head in range(2):
                mine = slice(head * HEAD, (head + 1) * HEAD)
                delta = jnp.sum(products[mine], axis=0, keepdims=True)
                lse = lse_ref[slot, b * (block // PAIR) + index, head : head + 1, :extent]
                scores = masked_scores(keep_head(keys, low, head), queries, count, extent)
                probs = jnp.exp2(scores - lse)
                probs_grad = nt(keep_head(values, low, head), grad)
                score_grad = (probs * (probs_grad - delta)).astype(BF16)
                dvs.append(nn(probs.astype(BF16), grad))
                dks.append(nn(score_grad, queries))
                dqs.append(nn(keys_t[mine], score_grad))
            put = lambda which, value: dqkv_ref.__setitem__(
                (slot, slice(0, extent),
                 pl.ds(pl.multiple_of(which * size + b * block + index * PAIR, PAIR), PAIR)),
                value.astype(BF16))
            put(0, jnp.concatenate(dqs, axis=0).T * SCALE)
            put(1, jnp.where(low, dks[0], dks[1]) * SCALE)
            put(2, jnp.where(low, dvs[0], dvs[1]))
            return carry

        for b in range(blocks):
            lax.fori_loop(0, block // PAIR, lambda index, carry, b=b: pair(b, index, carry), 0)
        got = dqkv_ref[slot, :extent]
        dw_s[:, : 3 * size] += tn(normed_ref[slot, :extent], got)
        vec_ref[0:1] += jnp.sum(got.astype(F32), axis=0, keepdims=True)
        upto = (extent + TILE - 1) // TILE * TILE
        if upto > extent:
            dqkv_ref[slot, extent:upto] = jnp.zeros((upto - extent, 3 * size), BF16)

    def per_slot(slot, carry):
        count = counts[0]
        for other in range(1, slots):
            count = jnp.where(slot == other, counts[other], count)
        for n in range(1, whole // BLK + 1):
            pl.when(blocks_of(count) == n)(lambda n=n: body(slot, count, n * BLK))
        return carry

    lax.fori_loop(0, slots, per_slot, 0)
    if part == 1:
        dw_s[:, 3 * size :] = dwo_ref[...]
    route, line = Route(), line_index()
    rows_each, columns = width // 8, dw_s.shape[1] // QUARTERS
    for rel in range(8):
        at = pl.ds(pl.multiple_of(route.eighth(rel) * rows_each, rows_each), rows_each)
        for q in range(QUARTERS):
            lanes = pl.ds(pl.multiple_of((ORDER[q] ^ line) * columns, columns), columns)
            to = ((rel % 4) * QUARTERS + q) * rows_each
            (keep_ref, send_ref)[rel // 4][to : to + rows_each] = dw_s[at, lanes].astype(BF16)


def attend_back(part, groups, lengths, normed, qkv, ctx, ctx_grad, lse, dwo):
    slots, whole, width = normed.shape
    block = width // 3
    mine = (0, 1) if part == 0 else (2,)
    size = len(mine) * block
    column = lambda index: pl.BlockSpec((slots, whole, block), lambda i: (0, 0, index))
    const = lambda *shape: pl.BlockSpec(shape, lambda i: (0,) * len(shape))
    pairs = size // PAIR
    bf16 = lambda *shape: jax.ShapeDtypeStruct(shape, BF16)
    half = (width // 2 * QUARTERS, 2 * width // QUARTERS)
    return pl.pallas_call(
        lambda *refs: attend_back_kernel(slots * groups, groups, part, *refs),
        grid=(1,),
        out_shape=[
            bf16(slots, whole, 3 * size), bf16(*half), bf16(*half),
            jax.ShapeDtypeStruct((8, 3 * size), F32),
        ],
        in_specs=[SMEM_SPEC, VMEM_SPEC] + [column(3 * which + b) for which in range(3) for b in mine]
        + [column(b) for b in mine] * 2
        + [pl.BlockSpec((slots, pairs, 8, whole), lambda i: (0, part * 2, 0, 0))]
        + [VMEM_SPEC] * part,
        out_specs=[const(slots, whole, 3 * size), const(*half), const(*half), const(8, 3 * size)],
        scratch_shapes=[pltpu.VMEM((width, 2 * width), F32)],
        compiler_params=params(),
        cost_estimate=cost(len(mine) * 6e9, 3e6, 12e6),
        name="attend_back",
    )(lengths, normed, *[qkv] * (3 * len(mine)), *[ctx] * len(mine), *[ctx_grad] * len(mine), lse,
      *[dwo] * part)


def input_back_kernel(rows, groups, whole, len_ref, *refs):
    (grad_a, grad_b, w_ref, x_ref, mid_grad_ref, gain_ref), refs = refs[:6], refs[6:]
    outs, vec_ref = refs[:groups], refs[groups]
    index = pl.program_id(0)
    left, _ = tile_state(len_ref, rows, groups, whole)
    width = x_ref.shape[1]

    @pl.when(index == 0)
    def _():
        vec_ref[...] = jnp.zeros_like(vec_ref)

    @pl.when(left(index) > 0)
    def _():
        back = jnp.zeros((TILE, width), F32)
        begin = 0
        for grads in (grad_a, grad_b):
            size = grads.shape[1] // 3
            for which in range(3):
                start = which * width + begin
                back += nt(grads[:, which * size : (which + 1) * size],
                           w_ref[:, start : start + size])
            begin += size
        hat, rstd = norm_stats(x_ref[...].astype(F32))
        vec_ref[0:1] += jnp.sum(back * hat, axis=0, keepdims=True)
        vec_ref[1:2] += jnp.sum(back, axis=0, keepdims=True)
        grad = norm_back(back, hat, rstd, gain_ref[...]) + mid_grad_ref[...]
        store_tile(outs, index, whole, grad.astype(BF16))

    @pl.when(left(index) <= 0)
    def _():
        store_tile(outs, index, whole, jnp.zeros((TILE, width), BF16))


def shards(
    molecules, lengths, norm1_gain, norm1_bias, qkv_weight, query_bias, value_bias, out_weight,
    out_bias, norm2_gain, norm2_bias, up_weight, up_bias, down_weight, down_bias, cotangent,
):
    rows, span, width = molecules.shape
    hidden = up_weight.shape[1]
    groups = lax.axis_size("seq")
    slots, whole = rows // groups, span * groups
    tokens = slots * whole
    line = lambda v: v.reshape(1, -1)
    shift = line(jnp.concatenate([query_bias, jnp.zeros_like(query_bias), value_bias]))
    g1, b1, g2, b2 = line(norm1_gain), line(norm1_bias), line(norm2_gain), line(norm2_bias)

    dealt = deal(lengths, molecules, groups, apart=True)
    pieces = [swap(dealt[slot * groups : (slot + 1) * groups]) for slot in range(slots)]
    cots = swap(deal(lengths, cotangent, groups))
    saved = ()
    for slot in range(slots):
        saved = attend(slot, slots, lengths, pieces[slot], g1, b1, qkv_weight, shift, out_weight,
                       line(out_bias), g2, b2, saved)
    x, normed, qkv, ctx, lse, mid, n2 = saved
    flat = lambda v: v.reshape(tokens, v.shape[-1])

    acts, hgs, dubs, order = [], [], [], Order()

    def feed(part, n2, sources):
        act, hg, keep, send, dub, *rest = feed_forward(
            part, PARTS, lengths, groups, n2, sources, up_weight, line(up_bias), down_weight)
        return act, hg, dub, keep, send, *rest

    def back(part, ctx_grad):
        return attend_back(part, groups, lengths, normed, qkv, ctx, ctx_grad, lse, dwo)

    def fed(act, hg, dub, keep, send, *rest):
        acts.append(act)
        hgs.append(hg)
        dubs.append(dub)
        return Pieces(keep, send), rest

    p0, (grad_out, down_bias_sum) = fed(*order(lambda v: feed(0, v, cots), flat(n2)))
    advance(order, p0)
    advance(order, p0)
    p1, _ = fed(*order(lambda v: feed(1, v, [grad_out]), flat(n2)))
    advance(order, p0, p1)
    mid_grad, ctx_grad, dwo, vec_mid = order(
        lambda hg0, hg1: tile_call(
            lambda *refs: feed_back_kernel(rows, groups, whole, PARTS, *refs), "feed_back", tokens,
            [(lengths, False), (hg0, True), (hg1, True), (up_weight, False), (grad_out, True),
             (flat(mid), True), (flat(ctx), True), (out_weight, False), (g2, False)],
            [((tokens, width), F32, True), ((tokens, width), BF16, True),
             ((width, width), F32, False), ((8, width), F32, False)],
            cost(2 * tokens * width * (hidden + 2 * width), 0, 25e6)),
        *hgs)
    ctx_grad = ctx_grad.reshape(slots, whole, width)
    advance(order, p1)
    dqkv_a, keep, send, vec_qkv_a = order(lambda v: back(0, v), ctx_grad)
    q0 = Pieces(keep, send)
    advance(order, p1, q0)
    dqkv_b, keep, send, vec_qkv_b = order(lambda v: back(1, v), ctx_grad)
    q1 = Pieces(keep, send)
    p = Merged([p0, p1])
    advance(order, p, q0, q1)
    out_pieces = order(
        lambda act0, act1: tile_call(
            lambda *refs: feed_out_kernel(rows, groups, whole, PARTS, *refs), "feed_out", tokens,
            [(lengths, False), (act0, True), (act1, True), (down_weight, False),
             (flat(mid), True), (line(down_bias), False)],
            [((slots, span, width), BF16, False)] * groups,
            cost(2 * tokens * width * hidden, 0, 16e6)),
        *acts)
    out_pieces = swap(out_pieces)
    *grad_pieces, vec_in = order(
        lambda grads: tile_call(
            lambda *refs: input_back_kernel(rows, groups, whole, *refs), "input_back", tokens,
            [(lengths, False), (flat(dqkv_a), True), (flat(grads), True), (qkv_weight, False),
             (flat(x), True), (mid_grad, True), (g1, False)],
            [((slots, span, width), BF16, False)] * groups + [((8, width), F32, False)],
            cost(6 * tokens * width * width, 0, 15e6)),
        dqkv_b)
    grad_pieces = swap(grad_pieces)
    advance(order, p, q0, q1)
    small = Small(order(
        lambda *parts: small_call(pack_kernel, "pack_small", [((16, width), F32)], *parts)[0],
        vec_in, vec_qkv_a, vec_qkv_b, vec_mid, down_bias_sum, *dubs))
    advance(order, p, q1)
    output = order(lambda *v: undeal(lengths, v, BF16), *out_pieces)
    q = Merged([q0, q1], straight=True)
    advance(order, p, small)
    molecules_grad = order(lambda *v: undeal(lengths, v, F32), *grad_pieces)
    while q.steps or p.steps:
        going = [one for one in (p, q) if one.steps]
        if small.ways:
            going.append(small)
        advance(order, *going)
        if len(q.steps) == 1:
            dup, ddown = order(lambda *v: lay_pieces(0, PARTS, v, width, hidden), *p.parts)
            dup, ddown = order(
                lambda *v: lay_pieces(1, PARTS, v, width, hidden, (dup, ddown)), *p.parts)
    dqkv, dwo = order(lambda *v: lay_qkv(0, v, width), *q.parts)
    dqkv, dwo = order(lambda *v: lay_qkv(1, v, width, (dqkv, dwo)), *q.parts)
    while small.ways:
        advance(order, small)
    small = order(lambda a, b: a + b, small.value, small.arriving)
    return (
        output, molecules_grad, small[0], small[1], dqkv, small[2], small[3], dwo, small[6],
        small[4], small[5], dup, small[8 : 8 + hidden // width].reshape(-1),
        ddown.reshape(hidden, width), small[7],
    )


def solution(mesh):
    tokens, whole = P("dp", "seq", None), P()
    in_specs = (tokens, P("dp")) + (whole,) * 13 + (tokens,)
    out_specs = (tokens, tokens) + (whole,) * 13
    return jax.shard_map(shards, mesh=mesh, in_specs=in_specs, out_specs=out_specs, check_vma=False)
```

```python
import math

import jax
import jax.numpy as jnp
from jax import lax
from jax.experimental import pallas as pl
from jax.experimental.pallas import tpu as pltpu
from jax.sharding import PartitionSpec as P

HEAD = 64
PAIR = 2 * HEAD
BLK = 128
TILE = 256
FCHUNK = 512
PARTS = 2
WEIGHT = 0.5
LOG2E = 1.4426950408889634
SCALE = 1.0 / math.sqrt(HEAD)
NEG = -1e30
EPS = 1e-12
F32 = jnp.float32
BF16 = jnp.bfloat16
VMEM_LIMIT = 20 * 1024 * 1024

SMEM_SPEC = pl.BlockSpec(memory_space=pltpu.SMEM)
VMEM_SPEC = pl.BlockSpec(memory_space=pltpu.VMEM)
ANY_SPEC = pl.BlockSpec(memory_space=pl.ANY)


def cost(flops, exps, moved):
    return pl.CostEstimate(
        flops=int(flops * WEIGHT), transcendentals=int(exps * WEIGHT), bytes_accessed=int(moved * WEIGHT))


def params(limit=VMEM_LIMIT):
    return pltpu.CompilerParams(vmem_limit_bytes=limit)


def in_hbm(array):
    return pltpu.with_memory_space_constraint(array, pltpu.HBM)


def nn(a, b):
    return lax.dot_general(a, b, (((1,), (0,)), ((), ())), preferred_element_type=F32)


def nt(a, b):
    return lax.dot_general(a, b, (((1,), (1,)), ((), ())), preferred_element_type=F32)


def tn(a, b):
    return lax.dot_general(a, b, (((0,), (0,)), ((), ())), preferred_element_type=F32)


def ranks_of(len_ref, rows):
    lens = [len_ref[r] for r in range(rows)]
    ranks = []
    for r in range(rows):
        rank = jnp.int32(0)
        for other in range(rows):
            if other < r:
                rank += (lens[other] >= lens[r]).astype(jnp.int32)
            elif other > r:
                rank += (lens[other] > lens[r]).astype(jnp.int32)
        ranks.append(rank)
    return lens, ranks


def rank_at(slot, group, groups):
    return slot * groups + (group if slot % 2 == 0 else groups - 1 - group)


def pick(values, ranks, wanted):
    found = jnp.int32(0)
    for value, rank in zip(values, ranks):
        found += jnp.where(rank == wanted, value, 0)
    return found


def my_counts(len_ref, rows, groups):
    me = lax.axis_index("seq")
    lens, ranks = ranks_of(len_ref, rows)
    return [
        (pick(lens, ranks, rank_at(slot, me, groups)) + 3) // 4
        for slot in range(rows // groups)
    ]


def blocks_of(count):
    return (count + BLK - 1) // BLK


def piece_rows(len_ref, rows, groups):
    me = lax.axis_index("seq")
    _, ranks = ranks_of(len_ref, rows)
    indices = [jnp.int32(r) for r in range(rows)]
    return {
        (slot, k): pick(indices, ranks, rank_at(slot, me ^ k, groups))
        for slot in range(rows // groups)
        for k in range(groups)
    }


def deal_kernel(rows, groups, apart, len_ref, src, *dsts):
    for (slot, k), row in piece_rows(len_ref, rows, groups).items():
        if apart:
            dsts[slot * groups + k][0] = src[row]
        else:
            dsts[k][slot] = src[row]


def deal(lengths, values, groups, apart=False):
    rows, span, width = values.shape
    slots = rows // groups
    count, deep = (slots * groups, 1) if apart else (groups, slots)
    return pl.pallas_call(
        lambda *refs: deal_kernel(rows, groups, apart, *refs),
        out_shape=[jax.ShapeDtypeStruct((deep, span, width), values.dtype)] * count,
        in_specs=[SMEM_SPEC, VMEM_SPEC],
        out_specs=[VMEM_SPEC] * count,
        compiler_params=params(),
        cost_estimate=cost(0, 0, 3e6),
        name="deal_rows",
    )(lengths, values)


def undeal_kernel(rows, groups, len_ref, *rest):
    srcs, dst = rest[:groups], rest[groups]
    for (slot, k), row in piece_rows(len_ref, rows, groups).items():
        dst[row] = srcs[k][slot].astype(dst.dtype)


def undeal(lengths, pieces, kind):
    slots, span, width = pieces[0].shape
    groups = len(pieces)
    rows = groups * slots
    return pl.pallas_call(
        lambda *refs: undeal_kernel(rows, groups, *refs),
        out_shape=jax.ShapeDtypeStruct((rows, span, width), kind),
        in_specs=[SMEM_SPEC] + [VMEM_SPEC] * groups,
        out_specs=VMEM_SPEC,
        compiler_params=params(),
        cost_estimate=cost(0, 0, 4e6),
        name="undeal_rows",
    )(lengths, *pieces)


def swap(pieces):
    groups = len(pieces)
    return [pieces[0]] + [
        lax.ppermute(pieces[k], "seq", [(i, i ^ k) for i in range(groups)])
        for k in range(1, groups)
    ]


class Route:
    def __init__(self):
        seq, dp = lax.axis_index("seq"), lax.axis_index("dp")
        pair, y, x = seq & 1, (seq >> 1) & 1, dp & 1
        low, high = x * 2 + y, y * 2 + x
        self.mine = pair * 4 + jnp.where(pair == 0, low, high)
        self.pairs = (1 - pair) * 4 + jnp.where(pair == 0, high, low)

    def eighth(self, rel):
        return rel ^ self.mine if rel < 4 else (rel - 4) ^ self.pairs


def turn(x_first):
    groups, size = lax.axis_size("seq"), lax.axis_size("dp")
    partners = []
    for dp in range(size):
        for seq in range(groups):
            if (seq % 2 == 0) == x_first:
                partners.append((dp ^ 1) * groups + seq)
            else:
                partners.append(dp * groups + (seq ^ 2))
    return list(enumerate(partners))


FIRST, SECOND = "first", "second"


def cross(values, way):
    if way in (FIRST, SECOND):
        return lax.ppermute(values, ("dp", "seq"), turn(way == FIRST))
    axis, mask = way
    size = lax.axis_size(axis)
    return lax.ppermute(values, axis, [(i, i ^ mask) for i in range(size)])


PAIR_WAY = ("seq", 1)


def far_ways():
    size, mask, ways = lax.axis_size("dp"), 2, []
    while mask < size:
        ways.append(("dp", mask))
        mask *= 2
    return ways


class Order:
    def __init__(self):
        self.last = None

    def __call__(self, step, *values):
        if self.last is not None:
            values, _ = lax.optimization_barrier((values, self.last))
        out = step(*values)
        self.last = jax.tree.leaves(out)
        return out


def line_size():
    return lax.axis_size("dp") // 2


def line_index():
    return (lax.axis_index("dp") // 2) % QUARTERS


def halve_kernel(keep, recv, low, high):
    rows = low.shape[0]
    for out, at in ((high, slice(rows, 2 * rows)), (low, slice(0, rows))):
        out[...] = (keep[at].astype(F32) + recv[at].astype(F32)).astype(out.dtype)


def sum_kernel(*refs):
    total = refs[0][...].astype(F32)
    for ref in refs[1:-1]:
        total += ref[...].astype(F32)
    refs[-1][...] = total.astype(refs[-1].dtype)


def stack_kernel(*refs):
    begin = 0
    for ref in refs[:-1]:
        refs[-1][begin : begin + ref.shape[0]] = ref[...]
        begin += ref.shape[0]


def merge_kernel(parts, *refs):
    ins, outs = refs[: 2 * parts], refs[2 * parts :]
    rows = ins[0].shape[0] // QUARTERS
    each = QUARTERS // len(outs)
    for q in (2, 3, 1, 0):
        for part in range(parts):
            keep, recv = ins[2 * part : 2 * part + 2]
            at = slice(q * rows, (q + 1) * rows)
            begin = ((q % each) * parts + part) * rows
            outs[q // each][begin : begin + rows] = (
                keep[at].astype(F32) + recv[at].astype(F32)).astype(keep.dtype)


LINE_WAYS = (("dp", 2), ("dp", 4))


def extra_ways():
    return [way for way in far_ways() if way not in LINE_WAYS]


class Steps:
    def next(self):
        return self.steps.pop(0)()

    def shape(self, parts=1, of=1):
        rows, width = self.low.shape
        return ((rows * parts // of, width), self.low.dtype)

    def begin(self):
        def done(send):
            self.arriving = [cross(send, PAIR_WAY)]
        return None, [self.send], None, done

    def halve(self, way):
        def done(low, high):
            self.low, self.arriving = low, [cross(high, way)]
        return halve_kernel, [self.low, *self.arriving], [self.shape(1, 2)] * 2, done

    def double(self, way):
        def done(low):
            self.low, self.arriving = low, [cross(low, way)]
        return sum_kernel, [self.low, *self.arriving], [self.shape()], done

    def gather(self, way):
        def done(low):
            self.low, self.arriving = low, [cross(low, way)]
        return stack_kernel, [self.low, *self.arriving], [self.shape(1 + len(self.arriving))], done

    def gather_pair(self):
        def done(*near):
            self.parts = list(near) + [cross(part, PAIR_WAY) for part in near]
        return None, [self.low, *self.arriving], None, done

    def along_line(self):
        near, far = LINE_WAYS
        ways = extra_ways() + [far]
        return [lambda: self.halve(far)] + [lambda way=way: self.double(way) for way in ways] + [
            lambda way=way: self.gather(way) for way in (near, SECOND, FIRST)]


class Pieces(Steps):
    def __init__(self, keep, send):
        self.low, self.send = keep, send
        self.steps = [self.begin, lambda: self.halve(FIRST), lambda: self.halve(SECOND)]


class Merged(Steps):
    def __init__(self, pieces, straight=False):
        self.pieces = pieces
        if straight and lax.axis_size("dp") == 2 * QUARTERS:
            self.steps = [self.quarter, self.sum]
            self.steps += [lambda way=way: self.gather(way) for way in (SECOND, FIRST)]
        else:
            self.steps = [self.merge] + self.along_line()
        self.steps.append(self.gather_pair)

    def merging(self, outs, done):
        parts = len(self.pieces)
        inputs = [v for one in self.pieces for v in (one.low, *one.arriving)]
        self.low = self.pieces[0].low
        shapes = [self.shape(parts, outs)] * outs
        return (lambda *refs: merge_kernel(parts, *refs)), inputs, shapes, done

    def merge(self):
        def done(low, high):
            self.low, self.arriving = low, [cross(high, LINE_WAYS[0])]
        return self.merging(2, done)

    def send_quarters(self, values):
        return [cross(value, ("dp", 2 * rel)) for value, rel in zip(values, ORDER[1:])]

    def quarter(self):
        def done(*quarters):
            self.low = quarters[0]
            self.arriving = self.send_quarters(quarters[1:])
        return self.merging(QUARTERS, done)

    def sum(self):
        def done(low):
            self.low, self.arriving = low, self.send_quarters([low] * (QUARTERS - 1))
        return sum_kernel, [self.low, *self.arriving], [self.shape()], done


class Small:
    def __init__(self, value):
        self.value = value
        self.ways = [PAIR_WAY, ("seq", 2), ("dp", 1)] + far_ways()
        self.arriving = cross(value, self.ways.pop(0))

    def next(self):
        def done(value):
            self.value = value
            if self.ways:
                self.arriving = cross(value, self.ways.pop(0))
        shape = (self.value.shape, self.value.dtype)
        return sum_kernel, [self.value, self.arriving], [shape], done


def advance(order, *sums):
    steps = [one.next() for one in sums]

    def kernel(*refs):
        refs = list(refs)
        ins, outs = refs[:count], refs[count:]
        for body, inputs, shapes, _ in steps:
            if body is not None:
                body(*ins[: len(inputs)], *outs[: len(shapes)])
                ins, outs = ins[len(inputs) :], outs[len(shapes) :]

    count = sum(len(inputs) for body, inputs, _, _ in steps if body is not None)
    shapes = [shape for body, _, outs, _ in steps if body is not None for shape in outs]

    def step(*values):
        values = list(values)
        worked = [value for value, own in zip(values, owned) if own]
        results = list(small_call(kernel, "advance", shapes, *worked)) if worked else []
        out, at = [], 0
        for body, inputs, own, _ in steps:
            if body is None:
                out.append(values[at : at + len(inputs)])
            else:
                out.append([results.pop(0) for _ in own])
            at += len(inputs)
        return out

    owned = [body is not None for body, inputs, _, _ in steps for _ in inputs]
    outs = order(step, *[value for _, inputs, _, _ in steps for value in inputs])
    for (_, _, _, done), out in zip(steps, outs):
        done(*out)


def lay_kernel(part, parts, *refs):
    gathered, (up, down, up_s, down_s, sems) = refs[:4], refs[-5:]
    route, line = Route(), line_index()
    slots = up_s.shape[0]
    size, down_rows = FCHUNK, FCHUNK // 32
    chunks = down_s.shape[1]
    columns = size // QUARTERS
    up_rows = up_s.shape[1] // 2
    copies = {}
    for rel in range(8):
        slot = rel % slots
        for copy in copies.pop(slot, ()):
            copy.wait()
        for q in range(QUARTERS):
            quarter = ORDER[q] ^ line
            piece = (((rel % 2) * QUARTERS + q) * parts + part) * (2 * up_rows)
            got = gathered[rel // 2].at[piece : piece + 2 * up_rows]
            for chunk in range(chunks):
                to = pl.ds(pl.multiple_of(chunk * size + quarter * columns, columns), columns)
                for half in range(2):
                    lanes = slice((2 * chunk + half) * columns, (2 * chunk + half + 1) * columns)
                    up_s[slot, half * up_rows : (half + 1) * up_rows, to] = (
                        got[:up_rows, lanes].astype(F32))
                at = up_rows + chunk * down_rows
                to = pl.ds(pl.multiple_of(quarter * down_rows, down_rows), down_rows)
                down_s[slot, chunk, to] = got[at : at + down_rows].astype(F32)
        eighth = route.eighth(rel)
        rows = pl.ds(pl.multiple_of(eighth * (2 * up_rows), 2 * up_rows), 2 * up_rows)
        copies[slot] = [
            pltpu.make_async_copy(
                up_s.at[slot], up.at[rows, pl.ds(part * chunks * size, chunks * size)],
                sems.at[slot, 0]),
            pltpu.make_async_copy(
                down_s.at[slot], down.at[pl.ds(part * chunks, chunks), eighth], sems.at[slot, 1]),
        ]
        for copy in copies[slot]:
            copy.start()
    for slot in copies:
        for copy in copies[slot]:
            copy.wait()


def lay_pieces(part, parts, gathered, width, hidden, before=()):
    chunks = hidden // FCHUNK // parts
    return pl.pallas_call(
        lambda *refs: lay_kernel(part, parts, *refs),
        out_shape=[
            jax.ShapeDtypeStruct((width, hidden), F32),
            jax.ShapeDtypeStruct((hidden // FCHUNK, 8, FCHUNK // 8, width), F32),
        ],
        in_specs=[VMEM_SPEC] * 4 + [ANY_SPEC] * len(before),
        out_specs=[ANY_SPEC] * 2,
        scratch_shapes=[
            pltpu.VMEM((4, width // 8, chunks * FCHUNK), F32),
            pltpu.VMEM((4, chunks, FCHUNK // 8, width), F32),
            pltpu.SemaphoreType.DMA((4, 2)),
        ],
        input_output_aliases={4 + i: i for i in range(len(before))},
        compiler_params=params(),
        cost_estimate=cost(0, 0, 14e6),
        name="lay_pieces",
    )(*gathered, *before)


def small_call(kernel, name, outs, *values):
    return pl.pallas_call(
        kernel,
        out_shape=[jax.ShapeDtypeStruct(shape, kind) for shape, kind in outs],
        in_specs=[VMEM_SPEC] * len(values),
        out_specs=[VMEM_SPEC] * len(outs),
        compiler_params=params(VMEM_LIMIT // 2),
        cost_estimate=cost(0, 0, 1e6),
        name=name,
    )(*values)


def pack_kernel(vec_in, vec_a, vec_b, vec_mid, down_bias, *rest):
    dubs, out = rest[:-1], rest[-1]
    width = out.shape[1]
    out[...] = jnp.zeros_like(out)
    out[0:2] = vec_in[0:2]
    for which in (0, 2):
        row, begin = 2 + which // 2, 0
        for vec in (vec_a, vec_b):
            size = vec.shape[1] // 3
            out[row : row + 1, begin : begin + size] = vec[0:1, which * size : (which + 1) * size]
            begin += size
    out[4:7] = vec_mid[0:3]
    out[7:8] = down_bias[0:1]
    row = 8
    for dub in dubs:
        for start in range(0, dub.shape[1], width):
            out[row : row + 1] = dub[0:1, start : start + width]
            row += 1


def lay_qkv_kernel(part, parts, *refs):
    gathered, refs = refs[:4], refs[4 + 2 * part :]
    out, dwo, stage, sems = refs
    route, line = Route(), line_index()
    slots, rows, size = stage.shape
    columns = size // QUARTERS
    width = dwo.shape[1]
    block = width // 3
    begin, count = (0, 2 * block) if part == 0 else (2 * block, block)
    copies = {}
    for rel in range(8):
        slot = rel % slots
        for copy in copies.pop(slot, ()):
            copy.wait()
        for q in range(QUARTERS):
            piece = (((rel % 2) * QUARTERS + q) * parts + part) * rows
            to = pl.ds(pl.multiple_of((ORDER[q] ^ line) * columns, columns), columns)
            stage[slot, :, to] = gathered[rel // 2][piece : piece + rows].astype(F32)
        at = pl.ds(pl.multiple_of(route.eighth(rel) * rows, rows), rows)
        moves = [
            (stage.at[slot, :, pl.ds(which * count, count)],
             out.at[at, pl.ds(which * width + begin, count)])
            for which in range(3)
        ]
        if part == 1:
            moves.append((stage.at[slot, :, pl.ds(3 * count, width)], dwo.at[at]))
        copies[slot] = [
            pltpu.make_async_copy(src, dst, sems.at[slot, i]) for i, (src, dst) in enumerate(moves)
        ]
        for copy in copies[slot]:
            copy.start()
    for slot in copies:
        for copy in copies[slot]:
            copy.wait()


def lay_qkv(part, gathered, width, before=()):
    return pl.pallas_call(
        lambda *refs: lay_qkv_kernel(part, 2, *refs),
        out_shape=[
            jax.ShapeDtypeStruct((width, 3 * width), F32),
            jax.ShapeDtypeStruct((width, width), F32),
        ],
        in_specs=[VMEM_SPEC] * 4 + [ANY_SPEC] * len(before),
        out_specs=[ANY_SPEC] * 2,
        scratch_shapes=[
            pltpu.VMEM((4, width // 8, 2 * width), F32),
            pltpu.SemaphoreType.DMA((4, 4)),
        ],
        input_output_aliases={4 + i: i for i in range(len(before))},
        compiler_params=params(),
        cost_estimate=cost(0, 0, 8e6),
        name="lay_qkv",
    )(*gathered, *before)


def norm_stats(values):
    center = values - jnp.mean(values, axis=-1, keepdims=True)
    rstd = lax.rsqrt(jnp.mean(center * center, axis=-1, keepdims=True) + EPS)
    return center * rstd, rstd


def norm_back(grad, hat, rstd, gain):
    scaled = grad * gain
    mean_scaled = jnp.mean(scaled, axis=-1, keepdims=True)
    mean_dot = jnp.mean(scaled * hat, axis=-1, keepdims=True)
    return rstd * (scaled - mean_scaled - hat * mean_dot)


def first_head(rows):
    return lax.broadcasted_iota(jnp.int32, (rows, PAIR), 1) < HEAD


def keep_head(values, low, head):
    zero = jnp.zeros_like(values)
    return jnp.where(low, values, zero) if head == 0 else jnp.where(low, zero, values)


def masked_scores(keys, queries, count, extent):
    scores = nt(keys, queries) * (SCALE * LOG2E)
    tail = scores[extent - BLK :]
    position = lax.broadcasted_iota(jnp.int32, tail.shape, 0) + (extent - BLK)
    tail = jnp.where(position < count, tail, NEG)
    if extent == BLK:
        return tail
    return jnp.concatenate([scores[: extent - BLK], tail], axis=0)


def attend_kernel(rows, groups, slot, len_ref, *refs):
    refs = list(refs)
    take = lambda n: [refs.pop(0) for _ in range(n)]
    pieces = take(groups)
    gain_ref, bias_ref, w_ref, shift_ref, wo_ref, bo_ref, g2_ref, b2_ref = take(8)
    if slot:
        take(7)
    x_ref, normed_ref, qkv_ref, ctx_ref, lse_ref, mid_ref, n2_ref = [ref.at[0] for ref in refs]
    count = my_counts(len_ref, rows, groups)[slot]
    whole, width = x_ref.shape
    span = whole // groups
    me = lax.axis_index("seq")
    for k in range(groups):
        x_ref[pl.ds(pl.multiple_of((me ^ k) * span, span), span)] = pieces[k][0]

    def body(extent):
        hat, _ = norm_stats(x_ref[:extent].astype(F32))
        normed = (hat * gain_ref[...] + bias_ref[...]).astype(BF16)
        normed_ref[:extent] = normed
        for part in range(3):
            cols = slice(part * width, (part + 1) * width)
            qkv_ref[:extent, cols] = (nn(normed, w_ref[:, cols]) + shift_ref[:, cols]).astype(BF16)
        low = first_head(extent)

        def pair(index, carry):
            start = pl.multiple_of(index * PAIR, PAIR)
            queries = qkv_ref[:extent, pl.ds(start, PAIR)]
            keys = qkv_ref[:extent, pl.ds(width + start, PAIR)]
            values = qkv_ref[:extent, pl.ds(2 * width + start, PAIR)]
            values_t = values.T
            outs = []
            for head in range(2):
                scores = masked_scores(keep_head(keys, low, head), queries, count, extent)
                top = jnp.max(scores, axis=0, keepdims=True)
                expo = jnp.exp2(scores - top)
                total = jnp.sum(expo, axis=0, keepdims=True)
                out = nn(values_t[head * HEAD : (head + 1) * HEAD], expo.astype(BF16))
                outs.append(out * (1.0 / total))
                lse_ref[index, head : head + 1, :extent] = top + jnp.log2(total)
            ctx_ref[:extent, pl.ds(start, PAIR)] = jnp.concatenate(outs, axis=0).T.astype(BF16)
            return carry

        lax.fori_loop(0, width // PAIR, pair, 0)
        middle = x_ref[:extent].astype(F32) + nn(ctx_ref[:extent], wo_ref[...]) + bo_ref[...]
        mid_ref[:extent] = middle
        hat, _ = norm_stats(middle)
        n2_ref[:extent] = (hat * g2_ref[...] + b2_ref[...]).astype(BF16)
        upto = (extent + TILE - 1) // TILE * TILE
        for ref in (normed_ref, ctx_ref, mid_ref, n2_ref):
            if upto > extent:
                ref[extent:upto] = jnp.zeros((upto - extent, width), ref.dtype)

    blocks = blocks_of(count)
    for n in range(1, whole // BLK + 1):
        pl.when(blocks == n)(lambda n=n: body(n * BLK))


def attend(slot, slots, lengths, pieces, gain, bias, weight, shift, wo, bo, g2, b2, before):
    groups = len(pieces)
    _, span, width = pieces[0].shape
    rows, whole = slots * groups, span * groups
    shapes = [
        ((slots, whole, width), BF16),
        ((slots, whole, width), BF16),
        ((slots, whole, 3 * width), BF16),
        ((slots, whole, width), BF16),
        ((slots, width // PAIR, 8, whole), F32),
        ((slots, whole, width), F32),
        ((slots, whole, width), BF16),
    ]
    one = lambda shape: pl.BlockSpec((1,) + shape[1:], lambda i: (slot,) + (0,) * (len(shape) - 1))
    return pl.pallas_call(
        lambda *refs: attend_kernel(rows, groups, slot, *refs),
        grid=(1,),
        out_shape=[jax.ShapeDtypeStruct(shape, kind) for shape, kind in shapes],
        in_specs=[SMEM_SPEC] + [VMEM_SPEC] * (groups + 8)
        + [ANY_SPEC] * len(before),
        out_specs=[one(shape) for shape, _ in shapes],
        input_output_aliases={1 + groups + 8 + i: i for i in range(len(before))},
        compiler_params=params(),
        cost_estimate=cost(5e9, 3e6, 12e6),
        name="attend",
    )(lengths, *pieces, gain, bias, weight, shift, wo, bo, g2, b2, *before)


def tile_state(len_ref, rows, groups, whole):
    counts = my_counts(len_ref, rows, groups)
    per_slot = whole // TILE

    def left(index):
        count = counts[0]
        for slot in range(1, len(counts)):
            count = jnp.where(index // per_slot == slot, counts[slot], count)
        return count - (index % per_slot) * TILE

    def valid(index):
        return lax.broadcasted_iota(jnp.int32, (TILE, 1), 0) < left(index)

    return left, valid


QUARTERS = 4
ORDER = (0, 2, 1, 3)


def write_pieces(dup_s, ddown_s, keep, send, line, chunk):
    route = Route()
    width, size = dup_s.shape
    up_rows, down_rows = width // 16, size // 32
    columns = size // QUARTERS
    for rel in range(8):
        dst = (keep, send)[rel // 4]
        eighth = route.eighth(rel)
        for q in range(QUARTERS):
            quarter = ORDER[q] ^ line
            piece = ((rel % 4) * QUARTERS + q) * (2 * up_rows)
            lanes = pl.ds(pl.multiple_of(quarter * columns, columns), columns)
            for half in range(2):
                begin = eighth * (2 * up_rows) + half * up_rows
                value = dup_s[pl.ds(pl.multiple_of(begin, up_rows), up_rows), lanes]
                to = pl.ds(pl.multiple_of((2 * chunk + half) * columns, columns), columns)
                dst[piece : piece + up_rows, to] = value.astype(BF16)
            begin = (eighth * QUARTERS + quarter) * down_rows
            value = ddown_s[pl.ds(pl.multiple_of(begin, down_rows), down_rows)]
            to = piece + up_rows + chunk * down_rows
            dst[pl.ds(pl.multiple_of(to, down_rows), down_rows)] = value.astype(BF16)


def feed_kernel(rows, groups, part, len_ref, *refs):
    refs = list(refs)
    take = lambda n: [refs.pop(0) for _ in range(n)]
    n2_ref = take(1)[0]
    sources = take(groups if part == 0 else 1)
    up_ref, ub_ref, down_ref = take(3)
    act_ref, hg_ref, keep_ref, send_ref, dub_ref = take(5)
    if part == 0:
        grad_ref, vec_ref = take(2)
    else:
        grad_ref = sources[0]
    dup_s, ddown_s = refs
    chunk = pl.program_id(0)
    tokens, width = n2_ref.shape
    whole = tokens // (rows // groups)
    span = whole // groups
    left, valid = tile_state(len_ref, rows, groups, whole)
    tiles = tokens // TILE
    me = lax.axis_index("seq")

    if part == 0:
        @pl.when(chunk == 0)
        def _():
            for k in range(groups):
                for slot in range(rows // groups):
                    at = pl.ds(pl.multiple_of(slot * whole + (me ^ k) * span, span), span)
                    grad_ref[at] = sources[k][slot]
            vec_ref[...] = jnp.zeros_like(vec_ref)

            def mask(index, carry):
                @pl.when(left(index) > 0)
                def _():
                    at = pl.ds(pl.multiple_of(index * TILE, TILE), TILE)
                    grad = jnp.where(valid(index), grad_ref[at], jnp.zeros((), BF16))
                    grad_ref[at] = grad
                    vec_ref[0:1] += jnp.sum(grad.astype(F32), axis=0, keepdims=True)
                return carry

            lax.fori_loop(0, tiles, mask, 0)

    def feed(index, first):
        at = pl.ds(pl.multiple_of(index * TILE, TILE), TILE)
        normed = n2_ref[at]
        grad = grad_ref[at]
        hidden = nn(normed, up_ref[...]) + ub_ref[...]
        phi = 0.5 + 0.5 * lax.erf(hidden * (1.0 / math.sqrt(2.0)))
        slope = phi + hidden * (jnp.exp(-0.5 * hidden * hidden) * (1.0 / math.sqrt(2.0 * math.pi)))
        active = (hidden * phi).astype(BF16)
        hidden_grad = (nt(grad, down_ref[...]) * slope).astype(BF16)
        act_ref[at] = active
        hg_ref[at] = hidden_grad
        ddown = tn(active, grad)
        dup = tn(normed, hidden_grad)
        dub = jnp.sum(hidden_grad.astype(F32), axis=0, keepdims=True)
        if first:
            ddown_s[...] = ddown
            dup_s[...] = dup
            dub_ref[...] = dub
        else:
            ddown_s[...] += ddown
            dup_s[...] += dup
            dub_ref[...] += dub

    feed(0, True)

    def more(index, carry):
        pl.when(left(index) > 0)(lambda: feed(index, False))
        return carry

    lax.fori_loop(1, tiles, more, 0)

    write_pieces(dup_s, ddown_s, keep_ref, send_ref, line_index(), chunk)


def feed_forward(part, parts, lengths, groups, n2, sources, up, ub, down):
    tokens, width = n2.shape
    rows = sources[0].shape[0] * groups if part == 0 else lengths.shape[0]
    hidden = up.shape[1] // parts
    count = hidden // FCHUNK
    ahead = part * count
    f32 = lambda *shape: jax.ShapeDtypeStruct(shape, F32)
    bf16 = lambda *shape: jax.ShapeDtypeStruct(shape, BF16)
    const = lambda *shape: pl.BlockSpec(shape, lambda f: (0,) * len(shape))
    half = (hidden * width) // width
    out_shape = [pltpu.HBM((tokens, hidden), BF16)] * 2 + [bf16(half, width)] * 2 + [f32(1, hidden)]
    out_specs = [pl.BlockSpec((tokens, FCHUNK), lambda f: (0, f))] * 2
    out_specs += [const(half, width)] * 2 + [pl.BlockSpec((1, FCHUNK), lambda f: (0, f))]
    if part == 0:
        out_shape += [bf16(tokens, width), f32(8, width)]
        out_specs += [const(tokens, width), const(8, width)]
    return pl.pallas_call(
        lambda *refs: feed_kernel(rows, groups, part, *refs),
        grid=(count,),
        out_shape=out_shape,
        in_specs=[SMEM_SPEC] + [VMEM_SPEC] * (1 + len(sources)) + [
            pl.BlockSpec((width, FCHUNK), lambda f: (0, ahead + f)),
            pl.BlockSpec((1, FCHUNK), lambda f: (0, ahead + f)),
            pl.BlockSpec((FCHUNK, width), lambda f: (ahead + f, 0)),
        ],
        out_specs=out_specs,
        scratch_shapes=[pltpu.VMEM((width, FCHUNK), F32), pltpu.VMEM((FCHUNK, width), F32)],
        compiler_params=params(),
        cost_estimate=cost(8 * tokens * width * hidden, 2 * tokens * hidden, 20e6),
        name="feed_forward",
    )(lengths, n2, *sources, in_hbm(up), ub, in_hbm(down))


def store_piece(refs, slot, block, value):
    me = lax.axis_index("seq")
    for k, ref in enumerate(refs):
        @pl.when((block ^ me) == k)
        def _(ref=ref):
            ref[slot] = value


def store_tile(refs, index, whole, value):
    per_slot = whole // TILE
    slot = index // per_slot
    for half in range(TILE // BLK):
        block = (index % per_slot) * (TILE // BLK) + half
        store_piece(refs, slot, block, value[half * BLK : (half + 1) * BLK])


def tile_call(kernel, name, tokens, in_parts, outs, estimate, scratch=()):
    specs = [SMEM_SPEC]
    for array, cut in in_parts[1:]:
        if cut:
            specs.append(pl.BlockSpec((TILE, array.shape[1]), lambda i: (i, 0)))
        else:
            specs.append(VMEM_SPEC)
    out_specs = []
    for shape, _, cut in outs:
        if cut:
            out_specs.append(pl.BlockSpec((TILE, shape[1]), lambda i: (i, 0)))
        else:
            out_specs.append(pl.BlockSpec(shape, lambda i, n=len(shape): (0,) * n))
    return pl.pallas_call(
        kernel,
        grid=(tokens // TILE,),
        out_shape=[jax.ShapeDtypeStruct(shape, kind) for shape, kind, _ in outs],
        in_specs=specs,
        out_specs=out_specs,
        scratch_shapes=list(scratch),
        compiler_params=params(),
        cost_estimate=estimate,
        name=name,
    )(*[array for array, _ in in_parts])


def feed_back_kernel(rows, groups, whole, parts, len_ref, *refs):
    hgs, refs = refs[:parts], refs[parts:]
    (up_ref, grad_ref, mid_ref, ctx_ref, wo_ref, g2_ref,
     mid_grad_ref, ctx_grad_ref, dwo_ref, vec_ref) = refs
    index = pl.program_id(0)
    left, _ = tile_state(len_ref, rows, groups, whole)

    @pl.when(index == 0)
    def _():
        dwo_ref[...] = jnp.zeros_like(dwo_ref)
        vec_ref[...] = jnp.zeros_like(vec_ref)

    @pl.when(left(index) > 0)
    def _():
        size = hgs[0].shape[1]
        back = nt(hgs[0][...], up_ref[:, :size])
        for part in range(1, parts):
            back += nt(hgs[part][...], up_ref[:, part * size : (part + 1) * size])
        hat, rstd = norm_stats(mid_ref[...])
        vec_ref[0:1] += jnp.sum(back * hat, axis=0, keepdims=True)
        vec_ref[1:2] += jnp.sum(back, axis=0, keepdims=True)
        mid_grad = norm_back(back, hat, rstd, g2_ref[...]) + grad_ref[...].astype(F32)
        branch = mid_grad.astype(BF16)
        mid_grad_ref[...] = mid_grad
        vec_ref[2:3] += jnp.sum(branch.astype(F32), axis=0, keepdims=True)
        dwo_ref[...] += tn(ctx_ref[...], branch)
        ctx_grad_ref[...] = nt(branch, wo_ref[...]).astype(BF16)


def feed_out_kernel(rows, groups, whole, parts, len_ref, *refs):
    acts, refs = refs[:parts], refs[parts:]
    (down_ref, mid_ref, bd_ref), outs = refs[:3], refs[3:]
    index = pl.program_id(0)
    left, valid = tile_state(len_ref, rows, groups, whole)

    @pl.when(left(index) > 0)
    def _():
        size = acts[0].shape[1]
        result = mid_ref[...] + bd_ref[...]
        for part in range(parts):
            result += nn(acts[part][...], down_ref[part * size : (part + 1) * size])
        store_tile(outs, index, whole, jnp.where(valid(index), result, 0.0).astype(BF16))

    @pl.when(left(index) <= 0)
    def _():
        store_tile(outs, index, whole, jnp.zeros((TILE, mid_ref.shape[1]), BF16))


def attend_back_kernel(rows, groups, part, len_ref, *refs):
    refs = list(refs)
    take = lambda n: [refs.pop(0) for _ in range(n)]
    blocks = 2 - part
    normed_ref = take(1)[0]
    qs, ks, vs, ctxs, grads = (take(blocks) for _ in range(5))
    lse_ref = take(1)[0]
    if part == 1:
        dwo_ref = take(1)[0]
    dqkv_ref, keep_ref, send_ref, vec_ref, dw_s = refs
    slots, whole, width = normed_ref.shape
    block = qs[0].shape[2]
    size = blocks * block
    counts = my_counts(len_ref, rows, groups)
    dw_s[:, : 3 * size] = jnp.zeros((width, 3 * size), F32)
    vec_ref[...] = jnp.zeros_like(vec_ref)

    def body(slot, count, extent):
        low = first_head(extent)

        def pair(b, index, carry):
            lanes = pl.ds(pl.multiple_of(index * PAIR, PAIR), PAIR)
            queries, keys, values, context, grad = (
                ref[b][slot, :extent, lanes] for ref in (qs, ks, vs, ctxs, grads))
            keys_t = keys.T
            products = (grad.astype(F32) * context.astype(F32)).T
            dqs, dks, dvs = [], [], []
            for head in range(2):
                mine = slice(head * HEAD, (head + 1) * HEAD)
                delta = jnp.sum(products[mine], axis=0, keepdims=True)
                lse = lse_ref[slot, b * (block // PAIR) + index, head : head + 1, :extent]
                scores = masked_scores(keep_head(keys, low, head), queries, count, extent)
                probs = jnp.exp2(scores - lse)
                probs_grad = nt(keep_head(values, low, head), grad)
                score_grad = (probs * (probs_grad - delta)).astype(BF16)
                dvs.append(nn(probs.astype(BF16), grad))
                dks.append(nn(score_grad, queries))
                dqs.append(nn(keys_t[mine], score_grad))
            put = lambda which, value: dqkv_ref.__setitem__(
                (slot, slice(0, extent),
                 pl.ds(pl.multiple_of(which * size + b * block + index * PAIR, PAIR), PAIR)),
                value.astype(BF16))
            put(0, jnp.concatenate(dqs, axis=0).T * SCALE)
            put(1, jnp.where(low, dks[0], dks[1]) * SCALE)
            put(2, jnp.where(low, dvs[0], dvs[1]))
            return carry

        for b in range(blocks):
            lax.fori_loop(0, block // PAIR, lambda index, carry, b=b: pair(b, index, carry), 0)
        got = dqkv_ref[slot, :extent]
        dw_s[:, : 3 * size] += tn(normed_ref[slot, :extent], got)
        vec_ref[0:1] += jnp.sum(got.astype(F32), axis=0, keepdims=True)
        upto = (extent + TILE - 1) // TILE * TILE
        if upto > extent:
            dqkv_ref[slot, extent:upto] = jnp.zeros((upto - extent, 3 * size), BF16)

    def per_slot(slot, carry):
        count = counts[0]
        for other in range(1, slots):
            count = jnp.where(slot == other, counts[other], count)
        for n in range(1, whole // BLK + 1):
            pl.when(blocks_of(count) == n)(lambda n=n: body(slot, count, n * BLK))
        return carry

    lax.fori_loop(0, slots, per_slot, 0)
    if part == 1:
        dw_s[:, 3 * size :] = dwo_ref[...]
    route, line = Route(), line_index()
    rows_each, columns = width // 8, dw_s.shape[1] // QUARTERS
    for rel in range(8):
        at = pl.ds(pl.multiple_of(route.eighth(rel) * rows_each, rows_each), rows_each)
        for q in range(QUARTERS):
            lanes = pl.ds(pl.multiple_of((ORDER[q] ^ line) * columns, columns), columns)
            to = ((rel % 4) * QUARTERS + q) * rows_each
            (keep_ref, send_ref)[rel // 4][to : to + rows_each] = dw_s[at, lanes].astype(BF16)


def attend_back(part, groups, lengths, normed, qkv, ctx, ctx_grad, lse, dwo):
    slots, whole, width = normed.shape
    block = width // 3
    mine = (0, 1) if part == 0 else (2,)
    size = len(mine) * block
    column = lambda index: pl.BlockSpec((slots, whole, block), lambda i: (0, 0, index))
    const = lambda *shape: pl.BlockSpec(shape, lambda i: (0,) * len(shape))
    pairs = size // PAIR
    bf16 = lambda *shape: jax.ShapeDtypeStruct(shape, BF16)
    half = (width // 2 * QUARTERS, 2 * width // QUARTERS)
    return pl.pallas_call(
        lambda *refs: attend_back_kernel(slots * groups, groups, part, *refs),
        grid=(1,),
        out_shape=[
            bf16(slots, whole, 3 * size), bf16(*half), bf16(*half),
            jax.ShapeDtypeStruct((8, 3 * size), F32),
        ],
        in_specs=[SMEM_SPEC, VMEM_SPEC] + [column(3 * which + b) for which in range(3) for b in mine]
        + [column(b) for b in mine] * 2
        + [pl.BlockSpec((slots, pairs, 8, whole), lambda i: (0, part * 2, 0, 0))]
        + [VMEM_SPEC] * part,
        out_specs=[const(slots, whole, 3 * size), const(*half), const(*half), const(8, 3 * size)],
        scratch_shapes=[pltpu.VMEM((width, 2 * width), F32)],
        compiler_params=params(),
        cost_estimate=cost(len(mine) * 6e9, 3e6, 12e6),
        name="attend_back",
    )(lengths, normed, *[qkv] * (3 * len(mine)), *[ctx] * len(mine), *[ctx_grad] * len(mine), lse,
      *[dwo] * part)


def input_back_kernel(rows, groups, whole, len_ref, *refs):
    (grad_a, grad_b, w_ref, x_ref, mid_grad_ref, gain_ref), refs = refs[:6], refs[6:]
    outs, vec_ref = refs[:groups], refs[groups]
    index = pl.program_id(0)
    left, _ = tile_state(len_ref, rows, groups, whole)
    width = x_ref.shape[1]

    @pl.when(index == 0)
    def _():
        vec_ref[...] = jnp.zeros_like(vec_ref)

    @pl.when(left(index) > 0)
    def _():
        back = jnp.zeros((TILE, width), F32)
        begin = 0
        for grads in (grad_a, grad_b):
            size = grads.shape[1] // 3
            for which in range(3):
                start = which * width + begin
                back += nt(grads[:, which * size : (which + 1) * size],
                           w_ref[:, start : start + size])
            begin += size
        hat, rstd = norm_stats(x_ref[...].astype(F32))
        vec_ref[0:1] += jnp.sum(back * hat, axis=0, keepdims=True)
        vec_ref[1:2] += jnp.sum(back, axis=0, keepdims=True)
        grad = norm_back(back, hat, rstd, gain_ref[...]) + mid_grad_ref[...]
        store_tile(outs, index, whole, grad.astype(BF16))

    @pl.when(left(index) <= 0)
    def _():
        store_tile(outs, index, whole, jnp.zeros((TILE, width), BF16))


def shards(
    molecules, lengths, norm1_gain, norm1_bias, qkv_weight, query_bias, value_bias, out_weight,
    out_bias, norm2_gain, norm2_bias, up_weight, up_bias, down_weight, down_bias, cotangent,
):
    rows, span, width = molecules.shape
    hidden = up_weight.shape[1]
    groups = lax.axis_size("seq")
    slots, whole = rows // groups, span * groups
    tokens = slots * whole
    line = lambda v: v.reshape(1, -1)
    shift = line(jnp.concatenate([query_bias, jnp.zeros_like(query_bias), value_bias]))
    g1, b1, g2, b2 = line(norm1_gain), line(norm1_bias), line(norm2_gain), line(norm2_bias)

    dealt = deal(lengths, molecules, groups, apart=True)
    pieces = [swap(dealt[slot * groups : (slot + 1) * groups]) for slot in range(slots)]
    cots = swap(deal(lengths, cotangent, groups))
    saved = ()
    for slot in range(slots):
        saved = attend(slot, slots, lengths, pieces[slot], g1, b1, qkv_weight, shift, out_weight,
                       line(out_bias), g2, b2, saved)
    x, normed, qkv, ctx, lse, mid, n2 = saved
    flat = lambda v: v.reshape(tokens, v.shape[-1])

    acts, hgs, dubs, order = [], [], [], Order()

    def feed(part, n2, sources):
        act, hg, keep, send, dub, *rest = feed_forward(
            part, PARTS, lengths, groups, n2, sources, up_weight, line(up_bias), down_weight)
        return act, hg, dub, keep, send, *rest

    def back(part, ctx_grad):
        return attend_back(part, groups, lengths, normed, qkv, ctx, ctx_grad, lse, dwo)

    def fed(act, hg, dub, keep, send, *rest):
        acts.append(act)
        hgs.append(hg)
        dubs.append(dub)
        return Pieces(keep, send), rest

    p0, (grad_out, down_bias_sum) = fed(*order(lambda v: feed(0, v, cots), flat(n2)))
    advance(order, p0)
    advance(order, p0)
    p1, _ = fed(*order(lambda v: feed(1, v, [grad_out]), flat(n2)))
    advance(order, p0, p1)
    mid_grad, ctx_grad, dwo, vec_mid = order(
        lambda hg0, hg1: tile_call(
            lambda *refs: feed_back_kernel(rows, groups, whole, PARTS, *refs), "feed_back", tokens,
            [(lengths, False), (hg0, True), (hg1, True), (up_weight, False), (grad_out, True),
             (flat(mid), True), (flat(ctx), True), (out_weight, False), (g2, False)],
            [((tokens, width), F32, True), ((tokens, width), BF16, True),
             ((width, width), F32, False), ((8, width), F32, False)],
            cost(2 * tokens * width * (hidden + 2 * width), 0, 25e6)),
        *hgs)
    ctx_grad = ctx_grad.reshape(slots, whole, width)
    advance(order, p1)
    dqkv_a, keep, send, vec_qkv_a = order(lambda v: back(0, v), ctx_grad)
    q0 = Pieces(keep, send)
    advance(order, p1, q0)
    dqkv_b, keep, send, vec_qkv_b = order(lambda v: back(1, v), ctx_grad)
    q1 = Pieces(keep, send)
    p = Merged([p0, p1])
    advance(order, p, q0, q1)
    out_pieces = order(
        lambda act0, act1: tile_call(
            lambda *refs: feed_out_kernel(rows, groups, whole, PARTS, *refs), "feed_out", tokens,
            [(lengths, False), (act0, True), (act1, True), (down_weight, False),
             (flat(mid), True), (line(down_bias), False)],
            [((slots, span, width), BF16, False)] * groups,
            cost(2 * tokens * width * hidden, 0, 16e6)),
        *acts)
    out_pieces = swap(out_pieces)
    *grad_pieces, vec_in = order(
        lambda grads: tile_call(
            lambda *refs: input_back_kernel(rows, groups, whole, *refs), "input_back", tokens,
            [(lengths, False), (flat(dqkv_a), True), (flat(grads), True), (qkv_weight, False),
             (flat(x), True), (mid_grad, True), (g1, False)],
            [((slots, span, width), BF16, False)] * groups + [((8, width), F32, False)],
            cost(6 * tokens * width * width, 0, 15e6)),
        dqkv_b)
    grad_pieces = swap(grad_pieces)
    advance(order, p, q0, q1)
    small = Small(order(
        lambda *parts: small_call(pack_kernel, "pack_small", [((16, width), F32)], *parts)[0],
        vec_in, vec_qkv_a, vec_qkv_b, vec_mid, down_bias_sum, *dubs))
    advance(order, p, q1)
    output = order(lambda *v: undeal(lengths, v, BF16), *out_pieces)
    molecules_grad = order(lambda *v: undeal(lengths, v, F32), *grad_pieces)
    q = Merged([q0, q1], straight=True)
    advance(order, p, small)
    while q.steps or p.steps:
        going = [one for one in (p, q) if one.steps]
        if small.ways:
            going.append(small)
        advance(order, *going)
        if len(q.steps) == 1:
            dup, ddown = order(lambda *v: lay_pieces(0, PARTS, v, width, hidden), *p.parts)
            dup, ddown = order(
                lambda *v: lay_pieces(1, PARTS, v, width, hidden, (dup, ddown)), *p.parts)
    dqkv, dwo = order(lambda *v: lay_qkv(0, v, width), *q.parts)
    dqkv, dwo = order(lambda *v: lay_qkv(1, v, width, (dqkv, dwo)), *q.parts)
    while small.ways:
        advance(order, small)
    small = order(lambda a, b: a + b, small.value, small.arriving)
    return (
        output, molecules_grad, small[0], small[1], dqkv, small[2], small[3], dwo, small[6],
        small[4], small[5], dup, small[8 : 8 + hidden // width].reshape(-1),
        ddown.reshape(hidden, width), small[7],
    )


def solution(mesh):
    tokens, whole = P("dp", "seq", None), P()
    in_specs = (tokens, P("dp")) + (whole,) * 13 + (tokens,)
    out_specs = (tokens, tokens) + (whole,) * 13
    return jax.shard_map(shards, mesh=mesh, in_specs=in_specs, out_specs=out_specs, check_vma=False)
```

```python
import math

import jax
import jax.numpy as jnp
from jax import lax
from jax.experimental import pallas as pl
from jax.experimental.pallas import tpu as pltpu
from jax.sharding import PartitionSpec as P

HEAD = 64
PAIR = 2 * HEAD
BLK = 128
TILE = 256
FCHUNK = 512
PARTS = 2
WEIGHT = 0.5
LOG2E = 1.4426950408889634
SCALE = 1.0 / math.sqrt(HEAD)
NEG = -1e30
EPS = 1e-12
F32 = jnp.float32
BF16 = jnp.bfloat16
VMEM_LIMIT = 20 * 1024 * 1024

SMEM_SPEC = pl.BlockSpec(memory_space=pltpu.SMEM)
VMEM_SPEC = pl.BlockSpec(memory_space=pltpu.VMEM)
ANY_SPEC = pl.BlockSpec(memory_space=pl.ANY)


def cost(flops, exps, moved):
    return pl.CostEstimate(
        flops=int(flops * WEIGHT), transcendentals=int(exps * WEIGHT), bytes_accessed=int(moved * WEIGHT))


def params(limit=VMEM_LIMIT):
    return pltpu.CompilerParams(vmem_limit_bytes=limit)


def in_hbm(array):
    return pltpu.with_memory_space_constraint(array, pltpu.HBM)


def nn(a, b):
    return lax.dot_general(a, b, (((1,), (0,)), ((), ())), preferred_element_type=F32)


def nt(a, b):
    return lax.dot_general(a, b, (((1,), (1,)), ((), ())), preferred_element_type=F32)


def tn(a, b):
    return lax.dot_general(a, b, (((0,), (0,)), ((), ())), preferred_element_type=F32)


def ranks_of(len_ref, rows):
    lens = [len_ref[r] for r in range(rows)]
    ranks = []
    for r in range(rows):
        rank = jnp.int32(0)
        for other in range(rows):
            if other < r:
                rank += (lens[other] >= lens[r]).astype(jnp.int32)
            elif other > r:
                rank += (lens[other] > lens[r]).astype(jnp.int32)
        ranks.append(rank)
    return lens, ranks


def rank_at(slot, group, groups):
    return slot * groups + (group if slot % 2 == 0 else groups - 1 - group)


def pick(values, ranks, wanted):
    found = jnp.int32(0)
    for value, rank in zip(values, ranks):
        found += jnp.where(rank == wanted, value, 0)
    return found


def my_counts(len_ref, rows, groups):
    me = lax.axis_index("seq")
    lens, ranks = ranks_of(len_ref, rows)
    return [
        (pick(lens, ranks, rank_at(slot, me, groups)) + 3) // 4
        for slot in range(rows // groups)
    ]


def blocks_of(count):
    return (count + BLK - 1) // BLK


def piece_rows(len_ref, rows, groups):
    me = lax.axis_index("seq")
    _, ranks = ranks_of(len_ref, rows)
    indices = [jnp.int32(r) for r in range(rows)]
    return {
        (slot, k): pick(indices, ranks, rank_at(slot, me ^ k, groups))
        for slot in range(rows // groups)
        for k in range(groups)
    }


def deal_kernel(rows, groups, apart, len_ref, src, *dsts):
    for (slot, k), row in piece_rows(len_ref, rows, groups).items():
        if apart:
            dsts[slot * groups + k][0] = src[row]
        else:
            dsts[k][slot] = src[row]


def deal(lengths, values, groups, apart=False):
    rows, span, width = values.shape
    slots = rows // groups
    count, deep = (slots * groups, 1) if apart else (groups, slots)
    return pl.pallas_call(
        lambda *refs: deal_kernel(rows, groups, apart, *refs),
        out_shape=[jax.ShapeDtypeStruct((deep, span, width), values.dtype)] * count,
        in_specs=[SMEM_SPEC, VMEM_SPEC],
        out_specs=[VMEM_SPEC] * count,
        compiler_params=params(),
        cost_estimate=cost(0, 0, 3e6),
        name="deal_rows",
    )(lengths, values)


def undeal_kernel(rows, groups, len_ref, *rest):
    srcs, dst = rest[:groups], rest[groups]
    for (slot, k), row in piece_rows(len_ref, rows, groups).items():
        dst[row] = srcs[k][slot].astype(dst.dtype)


def undeal(lengths, pieces, kind):
    slots, span, width = pieces[0].shape
    groups = len(pieces)
    rows = groups * slots
    return pl.pallas_call(
        lambda *refs: undeal_kernel(rows, groups, *refs),
        out_shape=jax.ShapeDtypeStruct((rows, span, width), kind),
        in_specs=[SMEM_SPEC] + [VMEM_SPEC] * groups,
        out_specs=VMEM_SPEC,
        compiler_params=params(),
        cost_estimate=cost(0, 0, 4e6),
        name="undeal_rows",
    )(lengths, *pieces)


def swap(pieces):
    groups = len(pieces)
    return [pieces[0]] + [
        lax.ppermute(pieces[k], "seq", [(i, i ^ k) for i in range(groups)])
        for k in range(1, groups)
    ]


class Route:
    def __init__(self):
        seq, dp = lax.axis_index("seq"), lax.axis_index("dp")
        pair, y, x = seq & 1, (seq >> 1) & 1, dp & 1
        low, high = x * 2 + y, y * 2 + x
        self.mine = pair * 4 + jnp.where(pair == 0, low, high)
        self.pairs = (1 - pair) * 4 + jnp.where(pair == 0, high, low)

    def eighth(self, rel):
        return rel ^ self.mine if rel < 4 else (rel - 4) ^ self.pairs


def turn(x_first):
    groups, size = lax.axis_size("seq"), lax.axis_size("dp")
    partners = []
    for dp in range(size):
        for seq in range(groups):
            if (seq % 2 == 0) == x_first:
                partners.append((dp ^ 1) * groups + seq)
            else:
                partners.append(dp * groups + (seq ^ 2))
    return list(enumerate(partners))


FIRST, SECOND = "first", "second"


def cross(values, way):
    if way in (FIRST, SECOND):
        return lax.ppermute(values, ("dp", "seq"), turn(way == FIRST))
    axis, mask = way
    size = lax.axis_size(axis)
    return lax.ppermute(values, axis, [(i, i ^ mask) for i in range(size)])


PAIR_WAY = ("seq", 1)


def far_ways():
    size, mask, ways = lax.axis_size("dp"), 2, []
    while mask < size:
        ways.append(("dp", mask))
        mask *= 2
    return ways


class Order:
    def __init__(self):
        self.last = None

    def __call__(self, step, *values):
        if self.last is not None:
            values, _ = lax.optimization_barrier((values, self.last))
        out = step(*values)
        self.last = jax.tree.leaves(out)
        return out


def line_size():
    return lax.axis_size("dp") // 2


def line_index():
    return (lax.axis_index("dp") // 2) % QUARTERS


def halve_kernel(keep, recv, low, high):
    rows = low.shape[0]
    for out, at in ((high, slice(rows, 2 * rows)), (low, slice(0, rows))):
        out[...] = (keep[at].astype(F32) + recv[at].astype(F32)).astype(out.dtype)


def sum_kernel(*refs):
    total = refs[0][...].astype(F32)
    for ref in refs[1:-1]:
        total += ref[...].astype(F32)
    refs[-1][...] = total.astype(refs[-1].dtype)


def stack_kernel(*refs):
    begin = 0
    for ref in refs[:-1]:
        refs[-1][begin : begin + ref.shape[0]] = ref[...]
        begin += ref.shape[0]


def merge_kernel(parts, *refs):
    ins, outs = refs[: 2 * parts], refs[2 * parts :]
    rows = ins[0].shape[0] // QUARTERS
    each = QUARTERS // len(outs)
    for q in (2, 3, 1, 0):
        for part in range(parts):
            keep, recv = ins[2 * part : 2 * part + 2]
            at = slice(q * rows, (q + 1) * rows)
            begin = ((q % each) * parts + part) * rows
            outs[q // each][begin : begin + rows] = (
                keep[at].astype(F32) + recv[at].astype(F32)).astype(keep.dtype)


LINE_WAYS = (("dp", 2), ("dp", 4))


def extra_ways():
    return [way for way in far_ways() if way not in LINE_WAYS]


class Steps:
    def next(self):
        return self.steps.pop(0)()

    def shape(self, parts=1, of=1):
        rows, width = self.low.shape
        return ((rows * parts // of, width), self.low.dtype)

    def begin(self):
        def done(send):
            self.arriving = [cross(send, PAIR_WAY)]
        return None, [self.send], None, done

    def halve(self, way):
        def done(low, high):
            self.low, self.arriving = low, [cross(high, way)]
        return halve_kernel, [self.low, *self.arriving], [self.shape(1, 2)] * 2, done

    def double(self, way):
        def done(low):
            self.low, self.arriving = low, [cross(low, way)]
        return sum_kernel, [self.low, *self.arriving], [self.shape()], done

    def gather(self, way):
        def done(low):
            self.low, self.arriving = low, [cross(low, way)]
        return stack_kernel, [self.low, *self.arriving], [self.shape(1 + len(self.arriving))], done

    def gather_pair(self):
        def done(*near):
            self.parts = list(near) + [cross(part, PAIR_WAY) for part in near]
        return None, [self.low, *self.arriving], None, done

    def along_line(self):
        near, far = LINE_WAYS
        ways = extra_ways() + [far]
        return [lambda: self.halve(far)] + [lambda way=way: self.double(way) for way in ways] + [
            lambda way=way: self.gather(way) for way in (near, SECOND, FIRST)]


class Pieces(Steps):
    def __init__(self, keep, send):
        self.low, self.send = keep, send
        self.steps = [self.begin, lambda: self.halve(FIRST), lambda: self.halve(SECOND)]


class Merged(Steps):
    def __init__(self, pieces, straight=False):
        self.pieces = pieces
        if straight and lax.axis_size("dp") == 2 * QUARTERS:
            self.steps = [self.quarter, self.sum]
            self.steps += [lambda way=way: self.gather(way) for way in (SECOND, FIRST)]
        else:
            self.steps = [self.merge] + self.along_line()
        self.steps.append(self.gather_pair)

    def merging(self, outs, done):
        parts = len(self.pieces)
        inputs = [v for one in self.pieces for v in (one.low, *one.arriving)]
        self.low = self.pieces[0].low
        shapes = [self.shape(parts, outs)] * outs
        return (lambda *refs: merge_kernel(parts, *refs)), inputs, shapes, done

    def merge(self):
        def done(low, high):
            self.low, self.arriving = low, [cross(high, LINE_WAYS[0])]
        return self.merging(2, done)

    def send_quarters(self, values):
        return [cross(value, ("dp", 2 * rel)) for value, rel in zip(values, ORDER[1:])]

    def quarter(self):
        def done(*quarters):
            self.low = quarters[0]
            self.arriving = self.send_quarters(quarters[1:])
        return self.merging(QUARTERS, done)

    def sum(self):
        def done(low):
            self.low, self.arriving = low, self.send_quarters([low] * (QUARTERS - 1))
        return sum_kernel, [self.low, *self.arriving], [self.shape()], done


class Small:
    def __init__(self, value):
        self.value = value
        self.ways = [PAIR_WAY, ("seq", 2), ("dp", 1)] + far_ways()
        self.arriving = cross(value, self.ways.pop(0))

    def next(self):
        def done(value):
            self.value = value
            if self.ways:
                self.arriving = cross(value, self.ways.pop(0))
        shape = (self.value.shape, self.value.dtype)
        return sum_kernel, [self.value, self.arriving], [shape], done


def advance(order, *sums):
    steps = [one.next() for one in sums]

    def kernel(*refs):
        refs = list(refs)
        ins, outs = refs[:count], refs[count:]
        for body, inputs, shapes, _ in steps:
            if body is not None:
                body(*ins[: len(inputs)], *outs[: len(shapes)])
                ins, outs = ins[len(inputs) :], outs[len(shapes) :]

    count = sum(len(inputs) for body, inputs, _, _ in steps if body is not None)
    shapes = [shape for body, _, outs, _ in steps if body is not None for shape in outs]

    def step(*values):
        values = list(values)
        worked = [value for value, own in zip(values, owned) if own]
        results = list(small_call(kernel, "advance", shapes, *worked)) if worked else []
        out, at = [], 0
        for body, inputs, own, _ in steps:
            if body is None:
                out.append(values[at : at + len(inputs)])
            else:
                out.append([results.pop(0) for _ in own])
            at += len(inputs)
        return out

    owned = [body is not None for body, inputs, _, _ in steps for _ in inputs]
    outs = order(step, *[value for _, inputs, _, _ in steps for value in inputs])
    for (_, _, _, done), out in zip(steps, outs):
        done(*out)


def lay_kernel(part, parts, *refs):
    gathered, (up, down, up_s, down_s, sems) = refs[:4], refs[-5:]
    route, line = Route(), line_index()
    slots = up_s.shape[0]
    size, down_rows = FCHUNK, FCHUNK // 32
    chunks = down_s.shape[1]
    columns = size // QUARTERS
    up_rows = up_s.shape[1] // 2
    copies = {}
    for rel in range(8):
        slot = rel % slots
        for copy in copies.pop(slot, ()):
            copy.wait()
        for q in range(QUARTERS):
            quarter = ORDER[q] ^ line
            piece = (((rel % 2) * QUARTERS + q) * parts + part) * (2 * up_rows)
            got = gathered[rel // 2].at[piece : piece + 2 * up_rows]
            for chunk in range(chunks):
                to = pl.ds(pl.multiple_of(chunk * size + quarter * columns, columns), columns)
                for half in range(2):
                    lanes = slice((2 * chunk + half) * columns, (2 * chunk + half + 1) * columns)
                    up_s[slot, half * up_rows : (half + 1) * up_rows, to] = (
                        got[:up_rows, lanes].astype(F32))
                at = up_rows + chunk * down_rows
                to = pl.ds(pl.multiple_of(quarter * down_rows, down_rows), down_rows)
                down_s[slot, chunk, to] = got[at : at + down_rows].astype(F32)
        eighth = route.eighth(rel)
        rows = pl.ds(pl.multiple_of(eighth * (2 * up_rows), 2 * up_rows), 2 * up_rows)
        copies[slot] = [
            pltpu.make_async_copy(
                up_s.at[slot], up.at[rows, pl.ds(part * chunks * size, chunks * size)],
                sems.at[slot, 0]),
            pltpu.make_async_copy(
                down_s.at[slot], down.at[pl.ds(part * chunks, chunks), eighth], sems.at[slot, 1]),
        ]
        for copy in copies[slot]:
            copy.start()
    for slot in copies:
        for copy in copies[slot]:
            copy.wait()


def lay_pieces(part, parts, gathered, width, hidden, before=()):
    chunks = hidden // FCHUNK // parts
    return pl.pallas_call(
        lambda *refs: lay_kernel(part, parts, *refs),
        out_shape=[
            jax.ShapeDtypeStruct((width, hidden), F32),
            jax.ShapeDtypeStruct((hidden // FCHUNK, 8, FCHUNK // 8, width), F32),
        ],
        in_specs=[VMEM_SPEC] * 4 + [ANY_SPEC] * len(before),
        out_specs=[ANY_SPEC] * 2,
        scratch_shapes=[
            pltpu.VMEM((4, width // 8, chunks * FCHUNK), F32),
            pltpu.VMEM((4, chunks, FCHUNK // 8, width), F32),
            pltpu.SemaphoreType.DMA((4, 2)),
        ],
        input_output_aliases={4 + i: i for i in range(len(before))},
        compiler_params=params(),
        cost_estimate=cost(0, 0, 14e6),
        name="lay_pieces",
    )(*gathered, *before)


def small_call(kernel, name, outs, *values):
    return pl.pallas_call(
        kernel,
        out_shape=[jax.ShapeDtypeStruct(shape, kind) for shape, kind in outs],
        in_specs=[VMEM_SPEC] * len(values),
        out_specs=[VMEM_SPEC] * len(outs),
        compiler_params=params(VMEM_LIMIT // 2),
        cost_estimate=cost(0, 0, 1e6),
        name=name,
    )(*values)


def pack_kernel(vec_in, vec_a, vec_b, vec_mid, down_bias, *rest):
    dubs, out = rest[:-1], rest[-1]
    width = out.shape[1]
    out[...] = jnp.zeros_like(out)
    out[0:2] = vec_in[0:2]
    for which in (0, 2):
        row, begin = 2 + which // 2, 0
        for vec in (vec_a, vec_b):
            size = vec.shape[1] // 3
            out[row : row + 1, begin : begin + size] = vec[0:1, which * size : (which + 1) * size]
            begin += size
    out[4:7] = vec_mid[0:3]
    out[7:8] = down_bias[0:1]
    row = 8
    for dub in dubs:
        for start in range(0, dub.shape[1], width):
            out[row : row + 1] = dub[0:1, start : start + width]
            row += 1


def lay_qkv_kernel(part, parts, *refs):
    gathered, refs = refs[:4], refs[4 + 2 * part :]
    out, dwo, stage, sems = refs
    route, line = Route(), line_index()
    slots, rows, size = stage.shape
    columns = size // QUARTERS
    width = dwo.shape[1]
    block = width // 3
    begin, count = (0, 2 * block) if part == 0 else (2 * block, block)
    copies = {}
    for rel in range(8):
        slot = rel % slots
        for copy in copies.pop(slot, ()):
            copy.wait()
        for q in range(QUARTERS):
            piece = (((rel % 2) * QUARTERS + q) * parts + part) * rows
            to = pl.ds(pl.multiple_of((ORDER[q] ^ line) * columns, columns), columns)
            stage[slot, :, to] = gathered[rel // 2][piece : piece + rows].astype(F32)
        at = pl.ds(pl.multiple_of(route.eighth(rel) * rows, rows), rows)
        moves = [
            (stage.at[slot, :, pl.ds(which * count, count)],
             out.at[at, pl.ds(which * width + begin, count)])
            for which in range(3)
        ]
        if part == 1:
            moves.append((stage.at[slot, :, pl.ds(3 * count, width)], dwo.at[at]))
        copies[slot] = [
            pltpu.make_async_copy(src, dst, sems.at[slot, i]) for i, (src, dst) in enumerate(moves)
        ]
        for copy in copies[slot]:
            copy.start()
    for slot in copies:
        for copy in copies[slot]:
            copy.wait()


def lay_qkv(part, gathered, width, before=()):
    return pl.pallas_call(
        lambda *refs: lay_qkv_kernel(part, 2, *refs),
        out_shape=[
            jax.ShapeDtypeStruct((width, 3 * width), F32),
            jax.ShapeDtypeStruct((width, width), F32),
        ],
        in_specs=[VMEM_SPEC] * 4 + [ANY_SPEC] * len(before),
        out_specs=[ANY_SPEC] * 2,
        scratch_shapes=[
            pltpu.VMEM((4, width // 8, 2 * width), F32),
            pltpu.SemaphoreType.DMA((4, 4)),
        ],
        input_output_aliases={4 + i: i for i in range(len(before))},
        compiler_params=params(),
        cost_estimate=cost(0, 0, 8e6),
        name="lay_qkv",
    )(*gathered, *before)


def norm_stats(values):
    center = values - jnp.mean(values, axis=-1, keepdims=True)
    rstd = lax.rsqrt(jnp.mean(center * center, axis=-1, keepdims=True) + EPS)
    return center * rstd, rstd


def norm_back(grad, hat, rstd, gain):
    scaled = grad * gain
    mean_scaled = jnp.mean(scaled, axis=-1, keepdims=True)
    mean_dot = jnp.mean(scaled * hat, axis=-1, keepdims=True)
    return rstd * (scaled - mean_scaled - hat * mean_dot)


def first_head(rows):
    return lax.broadcasted_iota(jnp.int32, (rows, PAIR), 1) < HEAD


def keep_head(values, low, head):
    zero = jnp.zeros_like(values)
    return jnp.where(low, values, zero) if head == 0 else jnp.where(low, zero, values)


def masked_scores(keys, queries, count, extent):
    scores = nt(keys, queries) * (SCALE * LOG2E)
    tail = scores[extent - BLK :]
    position = lax.broadcasted_iota(jnp.int32, tail.shape, 0) + (extent - BLK)
    tail = jnp.where(position < count, tail, NEG)
    if extent == BLK:
        return tail
    return jnp.concatenate([scores[: extent - BLK], tail], axis=0)


def attend_kernel(rows, groups, slot, len_ref, *refs):
    refs = list(refs)
    take = lambda n: [refs.pop(0) for _ in range(n)]
    pieces = take(groups)
    gain_ref, bias_ref, w_ref, shift_ref, wo_ref, bo_ref, g2_ref, b2_ref = take(8)
    if slot:
        take(7)
    x_ref, normed_ref, qkv_ref, ctx_ref, lse_ref, mid_ref, n2_ref = [ref.at[0] for ref in refs]
    count = my_counts(len_ref, rows, groups)[slot]
    whole, width = x_ref.shape
    span = whole // groups
    me = lax.axis_index("seq")
    for k in range(groups):
        x_ref[pl.ds(pl.multiple_of((me ^ k) * span, span), span)] = pieces[k][0]

    def body(extent):
        hat, _ = norm_stats(x_ref[:extent].astype(F32))
        normed = (hat * gain_ref[...] + bias_ref[...]).astype(BF16)
        normed_ref[:extent] = normed
        for part in range(3):
            cols = slice(part * width, (part + 1) * width)
            qkv_ref[:extent, cols] = (nn(normed, w_ref[:, cols]) + shift_ref[:, cols]).astype(BF16)
        low = first_head(extent)

        def pair(index, carry):
            start = pl.multiple_of(index * PAIR, PAIR)
            queries = qkv_ref[:extent, pl.ds(start, PAIR)]
            keys = qkv_ref[:extent, pl.ds(width + start, PAIR)]
            values = qkv_ref[:extent, pl.ds(2 * width + start, PAIR)]
            values_t = values.T
            outs = []
            for head in range(2):
                scores = masked_scores(keep_head(keys, low, head), queries, count, extent)
                top = jnp.max(scores, axis=0, keepdims=True)
                expo = jnp.exp2(scores - top)
                total = jnp.sum(expo, axis=0, keepdims=True)
                out = nn(values_t[head * HEAD : (head + 1) * HEAD], expo.astype(BF16))
                outs.append(out * (1.0 / total))
                lse_ref[index, head : head + 1, :extent] = top + jnp.log2(total)
            ctx_ref[:extent, pl.ds(start, PAIR)] = jnp.concatenate(outs, axis=0).T.astype(BF16)
            return carry

        lax.fori_loop(0, width // PAIR, pair, 0)
        middle = x_ref[:extent].astype(F32) + nn(ctx_ref[:extent], wo_ref[...]) + bo_ref[...]
        mid_ref[:extent] = middle
        hat, _ = norm_stats(middle)
        n2_ref[:extent] = (hat * g2_ref[...] + b2_ref[...]).astype(BF16)
        upto = (extent + TILE - 1) // TILE * TILE
        for ref in (normed_ref, ctx_ref, mid_ref, n2_ref):
            if upto > extent:
                ref[extent:upto] = jnp.zeros((upto - extent, width), ref.dtype)

    blocks = blocks_of(count)
    for n in range(1, whole // BLK + 1):
        pl.when(blocks == n)(lambda n=n: body(n * BLK))


def attend(slot, slots, lengths, pieces, gain, bias, weight, shift, wo, bo, g2, b2, before):
    groups = len(pieces)
    _, span, width = pieces[0].shape
    rows, whole = slots * groups, span * groups
    shapes = [
        ((slots, whole, width), BF16),
        ((slots, whole, width), BF16),
        ((slots, whole, 3 * width), BF16),
        ((slots, whole, width), BF16),
        ((slots, width // PAIR, 8, whole), F32),
        ((slots, whole, width), F32),
        ((slots, whole, width), BF16),
    ]
    one = lambda shape: pl.BlockSpec((1,) + shape[1:], lambda i: (slot,) + (0,) * (len(shape) - 1))
    return pl.pallas_call(
        lambda *refs: attend_kernel(rows, groups, slot, *refs),
        grid=(1,),
        out_shape=[jax.ShapeDtypeStruct(shape, kind) for shape, kind in shapes],
        in_specs=[SMEM_SPEC] + [VMEM_SPEC] * (groups + 8)
        + [ANY_SPEC] * len(before),
        out_specs=[one(shape) for shape, _ in shapes],
        input_output_aliases={1 + groups + 8 + i: i for i in range(len(before))},
        compiler_params=params(),
        cost_estimate=cost(5e9, 3e6, 12e6),
        name="attend",
    )(lengths, *pieces, gain, bias, weight, shift, wo, bo, g2, b2, *before)


def tile_state(len_ref, rows, groups, whole):
    counts = my_counts(len_ref, rows, groups)
    per_slot = whole // TILE

    def left(index):
        count = counts[0]
        for slot in range(1, len(counts)):
            count = jnp.where(index // per_slot == slot, counts[slot], count)
        return count - (index % per_slot) * TILE

    def valid(index):
        return lax.broadcasted_iota(jnp.int32, (TILE, 1), 0) < left(index)

    return left, valid


QUARTERS = 4
ORDER = (0, 2, 1, 3)


def write_pieces(dup_s, ddown_s, keep, send, line, chunk):
    route = Route()
    width, size = dup_s.shape
    up_rows, down_rows = width // 16, size // 32
    columns = size // QUARTERS
    for rel in range(8):
        dst = (keep, send)[rel // 4]
        eighth = route.eighth(rel)
        for q in range(QUARTERS):
            quarter = ORDER[q] ^ line
            piece = ((rel % 4) * QUARTERS + q) * (2 * up_rows)
            lanes = pl.ds(pl.multiple_of(quarter * columns, columns), columns)
            for half in range(2):
                begin = eighth * (2 * up_rows) + half * up_rows
                value = dup_s[pl.ds(pl.multiple_of(begin, up_rows), up_rows), lanes]
                to = pl.ds(pl.multiple_of((2 * chunk + half) * columns, columns), columns)
                dst[piece : piece + up_rows, to] = value.astype(BF16)
            begin = (eighth * QUARTERS + quarter) * down_rows
            value = ddown_s[pl.ds(pl.multiple_of(begin, down_rows), down_rows)]
            to = piece + up_rows + chunk * down_rows
            dst[pl.ds(pl.multiple_of(to, down_rows), down_rows)] = value.astype(BF16)


def feed_kernel(rows, groups, part, len_ref, *refs):
    refs = list(refs)
    take = lambda n: [refs.pop(0) for _ in range(n)]
    n2_ref = take(1)[0]
    sources = take(groups if part == 0 else 1)
    up_ref, ub_ref, down_ref = take(3)
    act_ref, hg_ref, keep_ref, send_ref, dub_ref = take(5)
    if part == 0:
        grad_ref, vec_ref = take(2)
    else:
        grad_ref = sources[0]
    dup_s, ddown_s = refs
    chunk = pl.program_id(0)
    tokens, width = n2_ref.shape
    whole = tokens // (rows // groups)
    span = whole // groups
    left, valid = tile_state(len_ref, rows, groups, whole)
    tiles = tokens // TILE
    me = lax.axis_index("seq")

    if part == 0:
        @pl.when(chunk == 0)
        def _():
            for k in range(groups):
                for slot in range(rows // groups):
                    at = pl.ds(pl.multiple_of(slot * whole + (me ^ k) * span, span), span)
                    grad_ref[at] = sources[k][slot]
            vec_ref[...] = jnp.zeros_like(vec_ref)

            def mask(index, carry):
                @pl.when(left(index) > 0)
                def _():
                    at = pl.ds(pl.multiple_of(index * TILE, TILE), TILE)
                    grad = jnp.where(valid(index), grad_ref[at], jnp.zeros((), BF16))
                    grad_ref[at] = grad
                    vec_ref[0:1] += jnp.sum(grad.astype(F32), axis=0, keepdims=True)
                return carry

            lax.fori_loop(0, tiles, mask, 0)

    def feed(index, first):
        at = pl.ds(pl.multiple_of(index * TILE, TILE), TILE)
        normed = n2_ref[at]
        grad = grad_ref[at]
        hidden = nn(normed, up_ref[...]) + ub_ref[...]
        phi = 0.5 + 0.5 * lax.erf(hidden * (1.0 / math.sqrt(2.0)))
        slope = phi + hidden * (jnp.exp(-0.5 * hidden * hidden) * (1.0 / math.sqrt(2.0 * math.pi)))
        active = (hidden * phi).astype(BF16)
        hidden_grad = (nt(grad, down_ref[...]) * slope).astype(BF16)
        act_ref[at] = active
        hg_ref[at] = hidden_grad
        ddown = tn(active, grad)
        dup = tn(normed, hidden_grad)
        dub = jnp.sum(hidden_grad.astype(F32), axis=0, keepdims=True)
        if first:
            ddown_s[...] = ddown
            dup_s[...] = dup
            dub_ref[...] = dub
        else:
            ddown_s[...] += ddown
            dup_s[...] += dup
            dub_ref[...] += dub

    feed(0, True)

    def more(index, carry):
        pl.when(left(index) > 0)(lambda: feed(index, False))
        return carry

    lax.fori_loop(1, tiles, more, 0)

    write_pieces(dup_s, ddown_s, keep_ref, send_ref, line_index(), chunk)


def feed_forward(part, parts, lengths, groups, n2, sources, up, ub, down):
    tokens, width = n2.shape
    rows = sources[0].shape[0] * groups if part == 0 else lengths.shape[0]
    hidden = up.shape[1] // parts
    count = hidden // FCHUNK
    ahead = part * count
    f32 = lambda *shape: jax.ShapeDtypeStruct(shape, F32)
    bf16 = lambda *shape: jax.ShapeDtypeStruct(shape, BF16)
    const = lambda *shape: pl.BlockSpec(shape, lambda f: (0,) * len(shape))
    half = (hidden * width) // width
    out_shape = [pltpu.HBM((tokens, hidden), BF16)] * 2 + [bf16(half, width)] * 2 + [f32(1, hidden)]
    out_specs = [pl.BlockSpec((tokens, FCHUNK), lambda f: (0, f))] * 2
    out_specs += [const(half, width)] * 2 + [pl.BlockSpec((1, FCHUNK), lambda f: (0, f))]
    if part == 0:
        out_shape += [bf16(tokens, width), f32(8, width)]
        out_specs += [const(tokens, width), const(8, width)]
    return pl.pallas_call(
        lambda *refs: feed_kernel(rows, groups, part, *refs),
        grid=(count,),
        out_shape=out_shape,
        in_specs=[SMEM_SPEC] + [VMEM_SPEC] * (1 + len(sources)) + [
            pl.BlockSpec((width, FCHUNK), lambda f: (0, ahead + f)),
            pl.BlockSpec((1, FCHUNK), lambda f: (0, ahead + f)),
            pl.BlockSpec((FCHUNK, width), lambda f: (ahead + f, 0)),
        ],
        out_specs=out_specs,
        scratch_shapes=[pltpu.VMEM((width, FCHUNK), F32), pltpu.VMEM((FCHUNK, width), F32)],
        compiler_params=params(),
        cost_estimate=cost(8 * tokens * width * hidden, 2 * tokens * hidden, 20e6),
        name="feed_forward",
    )(lengths, n2, *sources, in_hbm(up), ub, in_hbm(down))


def store_piece(refs, slot, block, value):
    me = lax.axis_index("seq")
    for k, ref in enumerate(refs):
        @pl.when((block ^ me) == k)
        def _(ref=ref):
            ref[slot] = value


def store_tile(refs, index, whole, value):
    per_slot = whole // TILE
    slot = index // per_slot
    for half in range(TILE // BLK):
        block = (index % per_slot) * (TILE // BLK) + half
        store_piece(refs, slot, block, value[half * BLK : (half + 1) * BLK])


def tile_call(kernel, name, tokens, in_parts, outs, estimate, scratch=()):
    specs = [SMEM_SPEC]
    for array, cut in in_parts[1:]:
        if cut:
            specs.append(pl.BlockSpec((TILE, array.shape[1]), lambda i: (i, 0)))
        else:
            specs.append(VMEM_SPEC)
    out_specs = []
    for shape, _, cut in outs:
        if cut:
            out_specs.append(pl.BlockSpec((TILE, shape[1]), lambda i: (i, 0)))
        else:
            out_specs.append(pl.BlockSpec(shape, lambda i, n=len(shape): (0,) * n))
    return pl.pallas_call(
        kernel,
        grid=(tokens // TILE,),
        out_shape=[jax.ShapeDtypeStruct(shape, kind) for shape, kind, _ in outs],
        in_specs=specs,
        out_specs=out_specs,
        scratch_shapes=list(scratch),
        compiler_params=params(),
        cost_estimate=estimate,
        name=name,
    )(*[array for array, _ in in_parts])


def feed_back_kernel(rows, groups, whole, parts, len_ref, *refs):
    hgs, refs = refs[:parts], refs[parts:]
    (up_ref, grad_ref, mid_ref, ctx_ref, wo_ref, g2_ref,
     mid_grad_ref, ctx_grad_ref, dwo_ref, vec_ref) = refs
    index = pl.program_id(0)
    left, _ = tile_state(len_ref, rows, groups, whole)

    @pl.when(index == 0)
    def _():
        dwo_ref[...] = jnp.zeros_like(dwo_ref)
        vec_ref[...] = jnp.zeros_like(vec_ref)

    @pl.when(left(index) > 0)
    def _():
        size = hgs[0].shape[1]
        back = nt(hgs[0][...], up_ref[:, :size])
        for part in range(1, parts):
            back += nt(hgs[part][...], up_ref[:, part * size : (part + 1) * size])
        hat, rstd = norm_stats(mid_ref[...])
        vec_ref[0:1] += jnp.sum(back * hat, axis=0, keepdims=True)
        vec_ref[1:2] += jnp.sum(back, axis=0, keepdims=True)
        mid_grad = norm_back(back, hat, rstd, g2_ref[...]) + grad_ref[...].astype(F32)
        branch = mid_grad.astype(BF16)
        mid_grad_ref[...] = mid_grad
        vec_ref[2:3] += jnp.sum(branch.astype(F32), axis=0, keepdims=True)
        dwo_ref[...] += tn(ctx_ref[...], branch)
        ctx_grad_ref[...] = nt(branch, wo_ref[...]).astype(BF16)


def feed_out_kernel(rows, groups, whole, parts, len_ref, *refs):
    acts, refs = refs[:parts], refs[parts:]
    (down_ref, mid_ref, bd_ref), outs = refs[:3], refs[3:]
    index = pl.program_id(0)
    left, valid = tile_state(len_ref, rows, groups, whole)

    @pl.when(left(index) > 0)
    def _():
        size = acts[0].shape[1]
        result = mid_ref[...] + bd_ref[...]
        for part in range(parts):
            result += nn(acts[part][...], down_ref[part * size : (part + 1) * size])
        store_tile(outs, index, whole, jnp.where(valid(index), result, 0.0).astype(BF16))

    @pl.when(left(index) <= 0)
    def _():
        store_tile(outs, index, whole, jnp.zeros((TILE, mid_ref.shape[1]), BF16))


def attend_back_kernel(rows, groups, part, len_ref, *refs):
    refs = list(refs)
    take = lambda n: [refs.pop(0) for _ in range(n)]
    blocks = 2 - part
    normed_ref = take(1)[0]
    qs, ks, vs, ctxs, grads = (take(blocks) for _ in range(5))
    lse_ref = take(1)[0]
    if part == 1:
        dwo_ref = take(1)[0]
    dqkv_ref, keep_ref, send_ref, vec_ref, dw_s = refs
    slots, whole, width = normed_ref.shape
    block = qs[0].shape[2]
    size = blocks * block
    counts = my_counts(len_ref, rows, groups)
    dw_s[:, : 3 * size] = jnp.zeros((width, 3 * size), F32)
    vec_ref[...] = jnp.zeros_like(vec_ref)

    def body(slot, count, extent):
        low = first_head(extent)

        def pair(b, index, carry):
            lanes = pl.ds(pl.multiple_of(index * PAIR, PAIR), PAIR)
            queries, keys, values, context, grad = (
                ref[b][slot, :extent, lanes] for ref in (qs, ks, vs, ctxs, grads))
            keys_t = keys.T
            products = (grad.astype(F32) * context.astype(F32)).T
            dqs, dks, dvs = [], [], []
            for head in range(2):
                mine = slice(head * HEAD, (head + 1) * HEAD)
                delta = jnp.sum(products[mine], axis=0, keepdims=True)
                lse = lse_ref[slot, b * (block // PAIR) + index, head : head + 1, :extent]
                scores = masked_scores(keep_head(keys, low, head), queries, count, extent)
                probs = jnp.exp2(scores - lse)
                probs_grad = nt(keep_head(values, low, head), grad)
                score_grad = (probs * (probs_grad - delta)).astype(BF16)
                dvs.append(nn(probs.astype(BF16), grad))
                dks.append(nn(score_grad, queries))
                dqs.append(nn(keys_t[mine], score_grad))
            put = lambda which, value: dqkv_ref.__setitem__(
                (slot, slice(0, extent),
                 pl.ds(pl.multiple_of(which * size + b * block + index * PAIR, PAIR), PAIR)),
                value.astype(BF16))
            put(0, jnp.concatenate(dqs, axis=0).T * SCALE)
            put(1, jnp.where(low, dks[0], dks[1]) * SCALE)
            put(2, jnp.where(low, dvs[0], dvs[1]))
            return carry

        for b in range(blocks):
            lax.fori_loop(0, block // PAIR, lambda index, carry, b=b: pair(b, index, carry), 0)
        got = dqkv_ref[slot, :extent]
        dw_s[:, : 3 * size] += tn(normed_ref[slot, :extent], got)
        vec_ref[0:1] += jnp.sum(got.astype(F32), axis=0, keepdims=True)
        upto = (extent + TILE - 1) // TILE * TILE
        if upto > extent:
            dqkv_ref[slot, extent:upto] = jnp.zeros((upto - extent, 3 * size), BF16)

    def per_slot(slot, carry):
        count = counts[0]
        for other in range(1, slots):
            count = jnp.where(slot == other, counts[other], count)
        for n in range(1, whole // BLK + 1):
            pl.when(blocks_of(count) == n)(lambda n=n: body(slot, count, n * BLK))
        return carry

    lax.fori_loop(0, slots, per_slot, 0)
    if part == 1:
        dw_s[:, 3 * size :] = dwo_ref[...]
    route, line = Route(), line_index()
    rows_each, columns = width // 8, dw_s.shape[1] // QUARTERS
    for rel in range(8):
        at = pl.ds(pl.multiple_of(route.eighth(rel) * rows_each, rows_each), rows_each)
        for q in range(QUARTERS):
            lanes = pl.ds(pl.multiple_of((ORDER[q] ^ line) * columns, columns), columns)
            to = ((rel % 4) * QUARTERS + q) * rows_each
            (keep_ref, send_ref)[rel // 4][to : to + rows_each] = dw_s[at, lanes].astype(BF16)


def attend_back(part, groups, lengths, normed, qkv, ctx, ctx_grad, lse, dwo):
    slots, whole, width = normed.shape
    block = width // 3
    mine = (0, 1) if part == 0 else (2,)
    size = len(mine) * block
    column = lambda index: pl.BlockSpec((slots, whole, block), lambda i: (0, 0, index))
    const = lambda *shape: pl.BlockSpec(shape, lambda i: (0,) * len(shape))
    pairs = size // PAIR
    bf16 = lambda *shape: jax.ShapeDtypeStruct(shape, BF16)
    half = (width // 2 * QUARTERS, 2 * width // QUARTERS)
    return pl.pallas_call(
        lambda *refs: attend_back_kernel(slots * groups, groups, part, *refs),
        grid=(1,),
        out_shape=[
            bf16(slots, whole, 3 * size), bf16(*half), bf16(*half),
            jax.ShapeDtypeStruct((8, 3 * size), F32),
        ],
        in_specs=[SMEM_SPEC, VMEM_SPEC] + [column(3 * which + b) for which in range(3) for b in mine]
        + [column(b) for b in mine] * 2
        + [pl.BlockSpec((slots, pairs, 8, whole), lambda i: (0, part * 2, 0, 0))]
        + [VMEM_SPEC] * part,
        out_specs=[const(slots, whole, 3 * size), const(*half), const(*half), const(8, 3 * size)],
        scratch_shapes=[pltpu.VMEM((width, 2 * width), F32)],
        compiler_params=params(),
        cost_estimate=cost(len(mine) * 6e9, 3e6, 12e6),
        name="attend_back",
    )(lengths, normed, *[qkv] * (3 * len(mine)), *[ctx] * len(mine), *[ctx_grad] * len(mine), lse,
      *[dwo] * part)


def input_back_kernel(rows, groups, whole, len_ref, *refs):
    (grad_a, grad_b, w_ref, x_ref, mid_grad_ref, gain_ref), refs = refs[:6], refs[6:]
    outs, vec_ref = refs[:groups], refs[groups]
    index = pl.program_id(0)
    left, _ = tile_state(len_ref, rows, groups, whole)
    width = x_ref.shape[1]

    @pl.when(index == 0)
    def _():
        vec_ref[...] = jnp.zeros_like(vec_ref)

    @pl.when(left(index) > 0)
    def _():
        back = jnp.zeros((TILE, width), F32)
        begin = 0
        for grads in (grad_a, grad_b):
            size = grads.shape[1] // 3
            for which in range(3):
                start = which * width + begin
                back += nt(grads[:, which * size : (which + 1) * size],
                           w_ref[:, start : start + size])
            begin += size
        hat, rstd = norm_stats(x_ref[...].astype(F32))
        vec_ref[0:1] += jnp.sum(back * hat, axis=0, keepdims=True)
        vec_ref[1:2] += jnp.sum(back, axis=0, keepdims=True)
        grad = norm_back(back, hat, rstd, gain_ref[...]) + mid_grad_ref[...]
        store_tile(outs, index, whole, grad.astype(BF16))

    @pl.when(left(index) <= 0)
    def _():
        store_tile(outs, index, whole, jnp.zeros((TILE, width), BF16))


def shards(
    molecules, lengths, norm1_gain, norm1_bias, qkv_weight, query_bias, value_bias, out_weight,
    out_bias, norm2_gain, norm2_bias, up_weight, up_bias, down_weight, down_bias, cotangent,
):
    rows, span, width = molecules.shape
    hidden = up_weight.shape[1]
    groups = lax.axis_size("seq")
    slots, whole = rows // groups, span * groups
    tokens = slots * whole
    line = lambda v: v.reshape(1, -1)
    shift = line(jnp.concatenate([query_bias, jnp.zeros_like(query_bias), value_bias]))
    g1, b1, g2, b2 = line(norm1_gain), line(norm1_bias), line(norm2_gain), line(norm2_bias)

    dealt = deal(lengths, molecules, groups, apart=True)
    pieces = [swap(dealt[slot * groups : (slot + 1) * groups]) for slot in range(slots)]
    cots = swap(deal(lengths, cotangent, groups))
    saved = ()
    for slot in range(slots):
        saved = attend(slot, slots, lengths, pieces[slot], g1, b1, qkv_weight, shift, out_weight,
                       line(out_bias), g2, b2, saved)
    x, normed, qkv, ctx, lse, mid, n2 = saved
    flat = lambda v: v.reshape(tokens, v.shape[-1])

    acts, hgs, dubs, order = [], [], [], Order()

    def feed(part, n2, sources):
        act, hg, keep, send, dub, *rest = feed_forward(
            part, PARTS, lengths, groups, n2, sources, up_weight, line(up_bias), down_weight)
        return act, hg, dub, keep, send, *rest

    def back(part, ctx_grad):
        return attend_back(part, groups, lengths, normed, qkv, ctx, ctx_grad, lse, dwo)

    def fed(act, hg, dub, keep, send, *rest):
        acts.append(act)
        hgs.append(hg)
        dubs.append(dub)
        return Pieces(keep, send), rest

    p0, (grad_out, down_bias_sum) = fed(*order(lambda v: feed(0, v, cots), flat(n2)))
    advance(order, p0)
    advance(order, p0)
    p1, _ = fed(*order(lambda v: feed(1, v, [grad_out]), flat(n2)))
    advance(order, p0, p1)
    mid_grad, ctx_grad, dwo, vec_mid = order(
        lambda hg0, hg1: tile_call(
            lambda *refs: feed_back_kernel(rows, groups, whole, PARTS, *refs), "feed_back", tokens,
            [(lengths, False), (hg0, True), (hg1, True), (up_weight, False), (grad_out, True),
             (flat(mid), True), (flat(ctx), True), (out_weight, False), (g2, False)],
            [((tokens, width), F32, True), ((tokens, width), BF16, True),
             ((width, width), F32, False), ((8, width), F32, False)],
            cost(2 * tokens * width * (hidden + 2 * width), 0, 25e6)),
        *hgs)
    ctx_grad = ctx_grad.reshape(slots, whole, width)
    advance(order, p1)
    dqkv_a, keep, send, vec_qkv_a = order(lambda v: back(0, v), ctx_grad)
    q0 = Pieces(keep, send)
    advance(order, p1, q0)
    dqkv_b, keep, send, vec_qkv_b = order(lambda v: back(1, v), ctx_grad)
    q1 = Pieces(keep, send)
    p = Merged([p0, p1])
    advance(order, p, q0, q1)
    out_pieces = order(
        lambda act0, act1: tile_call(
            lambda *refs: feed_out_kernel(rows, groups, whole, PARTS, *refs), "feed_out", tokens,
            [(lengths, False), (act0, True), (act1, True), (down_weight, False),
             (flat(mid), True), (line(down_bias), False)],
            [((slots, span, width), BF16, False)] * groups,
            cost(2 * tokens * width * hidden, 0, 16e6)),
        *acts)
    out_pieces = swap(out_pieces)
    *grad_pieces, vec_in = order(
        lambda grads: tile_call(
            lambda *refs: input_back_kernel(rows, groups, whole, *refs), "input_back", tokens,
            [(lengths, False), (flat(dqkv_a), True), (flat(grads), True), (qkv_weight, False),
             (flat(x), True), (mid_grad, True), (g1, False)],
            [((slots, span, width), BF16, False)] * groups + [((8, width), F32, False)],
            cost(6 * tokens * width * width, 0, 15e6)),
        dqkv_b)
    grad_pieces = swap(grad_pieces)
    advance(order, p, q0, q1)
    small = Small(order(
        lambda *parts: small_call(pack_kernel, "pack_small", [((16, width), F32)], *parts)[0],
        vec_in, vec_qkv_a, vec_qkv_b, vec_mid, down_bias_sum, *dubs))
    advance(order, p, q1)
    output = order(lambda *v: undeal(lengths, v, BF16), *out_pieces)
    molecules_grad = order(lambda *v: undeal(lengths, v, F32), *grad_pieces)
    q = Merged([q0, q1], straight=True)
    advance(order, p, q, small)
    while q.steps or p.steps:
        going = [one for one in (p, q) if one.steps]
        if small.ways:
            going.append(small)
        advance(order, *going)
        if len(q.steps) == 1:
            dup, ddown = order(lambda *v: lay_pieces(0, PARTS, v, width, hidden), *p.parts)
            dup, ddown = order(
                lambda *v: lay_pieces(1, PARTS, v, width, hidden, (dup, ddown)), *p.parts)
    dqkv, dwo = order(lambda *v: lay_qkv(0, v, width), *q.parts)
    dqkv, dwo = order(lambda *v: lay_qkv(1, v, width, (dqkv, dwo)), *q.parts)
    while small.ways:
        advance(order, small)
    small = order(lambda a, b: a + b, small.value, small.arriving)
    return (
        output, molecules_grad, small[0], small[1], dqkv, small[2], small[3], dwo, small[6],
        small[4], small[5], dup, small[8 : 8 + hidden // width].reshape(-1),
        ddown.reshape(hidden, width), small[7],
    )


def solution(mesh):
    tokens, whole = P("dp", "seq", None), P()
    in_specs = (tokens, P("dp")) + (whole,) * 13 + (tokens,)
    out_specs = (tokens, tokens) + (whole,) * 13
    return jax.shard_map(shards, mesh=mesh, in_specs=in_specs, out_specs=out_specs, check_vma=False)
```
